32 devices in a mesh: rep: 4 (over z), exp: 8 (over y, x, core).
Axes of the slice: x: 2, y: 2, z: 4, core: 2. Of those that a mesh axis runs over, the one named last changes fastest.
Arguments:
- tokens: bfloat16 [16384, 1024], P(('rep', 'exp')), may hold values from -6 to 6
- routes: int32 [16384, 1], P(('rep', 'exp')), may hold values from 0 to 7; in each aligned block of 512 rows (0 to 511, 512 to 1023, ...) at most 64 rows name the same one
- lengths: int32 [8], replicated, may hold values from 1024 to 2048
- centroids: float32 [8, 1024], P('exp'), may hold values from -0.125 to 0.125
- norm_gains: float32 [8, 2, 1024], P('exp'), may hold values from 0.1 to 1.9
- norm_biases: float32 [8, 2, 1024], P('exp'), may hold values from -4 to 4
- w_in: bfloat16 [8, 2, 1024, 4096], P('exp', None, None, 'rep'), may hold values from -0.1875 to 0.1875
- in_biases: float32 [8, 2, 4096], P('exp'), may hold values from -4 to 4
- w_out: bfloat16 [8, 2, 4096, 1024], P('exp', None, 'rep'), may hold values from -0.09375 to 0.09375
- out_biases: float32 [8, 2, 1024], P('exp'), may hold values from -4 to 4
- cotangent: bfloat16 [16384, 1024], P(('rep', 'exp')), may hold values from -6 to 6
Outputs:
- mixed: bfloat16 [16384, 1024], P(('rep', 'exp'))
- tokens_grad: bfloat16 [16384, 1024], P(('rep', 'exp'))
- centroid_grad: float32 [8, 1024], P('exp')
- gain_grad: float32 [8, 2, 1024], P('exp')
- norm_bias_grad: float32 [8, 2, 1024], P('exp')
- w_in_grad: float32 [8, 2, 1024, 4096], P('exp', None, None, 'rep')
- in_bias_grad: float32 [8, 2, 4096], P('exp')
- w_out_grad: float32 [8, 2, 4096, 1024], P('exp', None, 'rep')
- out_bias_grad: float32 [8, 2, 1024], P('exp')
The draws below stay inside these ranges and needn't reach their ends.
Inputs may be any that keep to these rules, and one draw needn't show every extreme that they name: `routes`: within the token slots of one device, each expert is named by exactly 64 slots.
All inputs are finite; a program needn't handle non-finite values.
Results may differ from the reference program's by a relative error of at most 0.0068.
Values may be sent and summed in bfloat16 or wider, within the bound.
A program may use at most 256 MiB of HBM per device.

```python
import math
import jax
import jax.numpy as jnp
import numpy as np
from jax import lax

D = 1024
FF = 4096
TOK_DEV = 512
SLOT = 2048
EXPERTS = 8
CAP = 64
TOKENS = 16384
SEQS = 8
ROWS = 2048


def touch_ends(drawn, key, least, top_value):
    shape = drawn.shape
    spot = [jax.random.randint(jax.random.fold_in(key, axis), (), 0, shape[axis]) for axis in range(len(shape))]
    drawn = drawn.at[tuple(spot)].set(least)
    longest = shape.index(max(shape))
    spot[longest] = (spot[longest] + 1) % shape[longest]
    return drawn.at[tuple(spot)].set(top_value)


def levels(own_key, extent, shards, smallest, top_value):
    factor_of = 1.0
    for dim, shards_of in shards:
        draws = jax.random.uniform(jax.random.fold_in(jax.random.fold_in(own_key, 6), dim), (shards_of,), jnp.float32, smallest / len(shards), top_value / len(shards))
        factor_of = factor_of * jnp.repeat(jnp.exp(draws), extent[dim] // shards_of).reshape((-1,) + (1,) * (len(extent) - 1 - dim))
    return factor_of


def routed_block(own_key, own, number, rows, count, top, bound, lean):
    ranking = jax.random.permutation(own_key, count)
    heavy_load, usual = portions_of(count, rows * top, bound, lean, True), portions_of(count, rows * top, bound, lean, False)
    places = jnp.arange(count)

    def named(sizes, rotation):
        used = int((sizes > 0).sum())
        fixed = max(1, used // 4)
        shifted = fixed + (places - fixed + rotation * (used - fixed)) % max(1, count - fixed)
        return jnp.zeros((count,), jnp.int32).at[ranking[jnp.where(places < fixed, places, shifted)]].set(jnp.asarray(sizes, jnp.int32))

    sizes = jnp.where(number % 4 == 0, named(heavy_load, number // 4), named(usual, number - number // 4 - 1))
    mixed = jax.random.permutation(jax.random.fold_in(own, 3), count)
    giver, receiver = mixed[0:count // 2 * 2:2], mixed[1:count // 2 * 2:2]
    slack = jnp.minimum(sizes[giver] - 1, bound - sizes[receiver]) // 2
    slack = jnp.where((giver == ranking[0]) | (receiver == ranking[0]) | (sizes[receiver] == 0), 0, jnp.maximum(slack, 0))
    shifted = jax.random.randint(jax.random.fold_in(own, 4), (count // 2,), 0, 1 << 20) % (slack + 1)
    sizes = sizes.at[giver].add(-shifted).at[receiver].add(shifted)
    members = jnp.searchsorted(jnp.cumsum(sizes), jnp.arange(rows * top), side="right").astype(jnp.int32)
    listing = members.reshape(top, rows).T
    listing = listing[jax.random.permutation(jax.random.fold_in(own, 1), rows)]
    rotation = jax.random.randint(jax.random.fold_in(own, 2), (rows, 1), 0, top)
    return jnp.take_along_axis(listing, (jnp.arange(top)[None, :] + rotation) % top, axis=1)


def portions_of(amount, total, reach, lean, full):
    loads = [(1 << 20) // math.isqrt(rank ** lean) + 1 for rank in range(1, amount + 1)]
    largest = reach if full else min(reach, max(-(-total // amount), total * loads[0] // sum(loads)))
    least = 1 if total - largest >= amount - 1 else 0
    given, surplus = [largest] + [least] * (amount - 1), total - largest - least * (amount - 1)
    while surplus > 0:
        movable = [i for i in range(1, amount) if given[i] < largest] or [i for i in range(1, amount) if given[i] < reach]
        whole, left = sum([loads[i] for i in movable]), surplus
        for i in movable:
            extra = min(reach - given[i], max(1, left * loads[i] // whole), surplus)
            given[i] = given[i] + extra
            surplus = surplus - extra
    return np.array(given)


def normal_values(own_key, dims, scale, limit, shards=(), held_as=jnp.bfloat16):
    level = levels(own_key, dims, shards, -0.22, 0.18) if shards else 1.0
    entries = jax.random.normal(own_key, dims, jnp.float32) * scale * level
    return jnp.minimum(jnp.maximum(entries, -limit), limit).astype(held_as)


def setup_inputs(seed: int = 0) -> dict:
    streams_of = jax.random.split(jax.random.key(seed), 12)
    tokens = normal_values(streams_of[0], (TOKENS, D), 1.0, 6.0, ((0, 32),))
    routes_keys = jax.random.split(jax.random.fold_in(streams_of[1], 1), TOKENS // TOK_DEV)
    routes_turns = jax.random.permutation(jax.random.fold_in(streams_of[1], 3), TOKENS // TOK_DEV)
    routes = jax.vmap(lambda own, number: routed_block(jax.random.fold_in(streams_of[1], 2), own, number, TOK_DEV, EXPERTS, 1, CAP, 0))(routes_keys, routes_turns).reshape((TOKENS, 1))
    lengths = touch_ends(jax.random.randint(streams_of[2], (SEQS,), SLOT // 2, SLOT + 1), jax.random.fold_in(streams_of[2], 1), SLOT // 2, SLOT).astype(jnp.int32)
    centroids = normal_values(streams_of[3], (EXPERTS, D), (2 * D) ** -0.5, 0.125, ((0, 8),), jnp.float32)
    norm_gains = jnp.clip(1.0 + 0.18 * jax.random.normal(streams_of[4], (EXPERTS, 2, D), jnp.float32), 0.1, 1.9)
    norm_biases = normal_values(streams_of[5], (EXPERTS, 2, D), 0.3, 4.0, ((0, 8),), jnp.float32)
    w_in = normal_values(streams_of[6], (EXPERTS, 2, D, FF), D ** -0.5, 0.1875, ((0, 8), (3, 4)))
    in_biases = normal_values(streams_of[7], (EXPERTS, 2, FF), 0.3, 4.0, ((0, 8),), jnp.float32)
    w_out = normal_values(streams_of[8], (EXPERTS, 2, FF, D), FF ** -0.5, 0.09375, ((0, 8), (2, 4)))
    out_biases = normal_values(streams_of[9], (EXPERTS, 2, D), 0.3, 4.0, ((0, 8),), jnp.float32)
    cotangent = normal_values(streams_of[10], (TOKENS, D), 1.0, 6.0, ((0, 32),))
    return {"tokens": tokens, "routes": routes, "lengths": lengths, "centroids": centroids, "norm_gains": norm_gains, "norm_biases": norm_biases, "w_in": w_in, "in_biases": in_biases, "w_out": w_out, "out_biases": out_biases, "cotangent": cotangent}


@jax.custom_vjp
def low(v):
    return lax.optimization_barrier(v.astype(jnp.bfloat16)).astype(jnp.float32)

@jax.custom_vjp
def low_back(v):
    return v

def low_keep(v):
    return (low(v), None)

def low_pass(kept, grad):
    return (grad,)

def back_keep(v):
    return (v, None)

def back_low(kept, grad):
    return (low(grad),)
low.defvjp(low_keep, low_pass)
low_back.defvjp(back_keep, back_low)
eps = 1e-05

def layer_norm(values, gain, bias):
    center = values - lax.optimization_barrier(jnp.mean(values, -1, keepdims=True))
    spread = lax.optimization_barrier(jnp.mean(center * center, -1, keepdims=True))
    return center * lax.rsqrt(spread + eps) * gain + bias

def sublayer(values, gain, bias, first, first_bias, second, second_bias):
    normed = layer_norm(values, gain[:, None, :], bias[:, None, :])
    inner = low_back(jnp.einsum('emd,edf->emf', low(normed), first, precision=lax.Precision.HIGHEST))
    active = jax.nn.gelu(inner + first_bias[:, None, :])
    outer = low_back(jnp.einsum('emf,efd->emd', low(active), second, precision=lax.Precision.HIGHEST))
    return values + outer + second_bias[:, None, :]

def reference(tokens, routes, lengths, centroids, norm_gains, norm_biases, w_in, in_biases, w_out, out_biases, cotangent):
    positions = jnp.arange(TOKENS, dtype=jnp.int32)
    live = (positions % SLOT < lengths[positions // SLOT]).astype(jnp.float32)
    order = jnp.argsort(routes[:, 0], stable=True).astype(jnp.int32)

    def forward(inputs, cent, gains, nbias, first, fbias, second, sbias):
        expert_in = low_back(inputs[order]).reshape(EXPERTS, ROWS, D)
        mid = sublayer(expert_in, gains[:, 0], nbias[:, 0], first[:, 0], fbias[:, 0], second[:, 0], sbias[:, 0])
        top = sublayer(mid, gains[:, 1], nbias[:, 1], first[:, 1], fbias[:, 1], second[:, 1], sbias[:, 1])
        gate = jax.nn.sigmoid(lax.optimization_barrier(jnp.sum(expert_in * cent[:, None, :], -1)))
        result = low_back(low(gate[..., None] * top)).reshape(TOKENS, D)
        placed = jnp.zeros((TOKENS, D), jnp.float32).at[order].set(result)
        return inputs + live[:, None] * placed
    primals = (tokens.astype(jnp.float32), centroids, norm_gains, norm_biases, w_in.astype(jnp.float32), in_biases, w_out.astype(jnp.float32), out_biases)
    mixed, pull = jax.vjp(forward, *primals)
    grads = pull(cotangent.astype(jnp.float32))
    return (mixed.astype(jnp.bfloat16), grads[0].astype(jnp.bfloat16), grads[1], grads[2], grads[3], grads[4], grads[5], grads[6], grads[7])
```

```python
import jax
import jax.numpy as jnp
from jax import lax
from jax.sharding import PartitionSpec as P

SLOT = 2048


eps = 1e-05


def layer_norm(values, gain, bias):
    center = values - jnp.mean(values, -1, keepdims=True)
    spread = jnp.mean(center * center, -1, keepdims=True)
    return center * lax.rsqrt(spread + eps) * gain + bias


def contract_rows(left, right):
    return lax.dot_general(
        left, right, (((0,), (0,)), ((), ())), preferred_element_type=jnp.float32
    )


def contract_cols(left, right):
    return lax.dot_general(
        left, right, (((1,), (1,)), ((), ())), preferred_element_type=jnp.float32
    )


def gather_rows(values):
    return lax.all_gather(values, "rep", axis=0, tiled=True)


def scatter_rows(values):
    return lax.psum_scatter(values.astype(jnp.bfloat16), "rep", scatter_dimension=0, tiled=True).astype(
        jnp.float32
    )


def shards(
    tokens,
    routes,
    lengths,
    centroids,
    norm_gains,
    norm_biases,
    w_in,
    in_biases,
    w_out,
    out_biases,
    cotangent,
):
    n_exp = lax.axis_size("exp")
    tok_rows = tokens.shape[0]
    cap = tok_rows // n_exp
    device = lax.axis_index(("rep", "exp"))
    positions = device * tok_rows + lax.iota(jnp.int32, tok_rows)
    seq_ids = positions // SLOT
    seq_table = lax.iota(jnp.int32, lengths.shape[0])
    seq_len = jnp.sum(jnp.where(seq_ids[:, None] == seq_table[None, :], lengths[None, :], 0), 1)
    live = (positions % SLOT < seq_len).astype(jnp.float32)[:, None]
    route = routes[:, 0]
    hits = (route[:, None] == lax.iota(jnp.int32, n_exp)[None, :]).astype(jnp.int32)
    before = jnp.cumsum(hits, 0) - hits
    target = route * cap + jnp.sum(before * hits, 1)
    place = (lax.iota(jnp.int32, tok_rows)[:, None] == target[None, :]).astype(jnp.bfloat16)
    grad_out = (live * cotangent.astype(jnp.float32)).astype(jnp.bfloat16)

    def send(rows):
        ordered = jnp.dot(place, rows, preferred_element_type=jnp.float32).astype(jnp.bfloat16)
        return lax.all_to_all(ordered, "exp", split_axis=0, concat_axis=0, tiled=True)

    def give_back(rows):
        back = lax.all_to_all(rows, "exp", split_axis=0, concat_axis=0, tiled=True)
        return contract_rows(place, back)

    expert_in = send(tokens).astype(jnp.float32)
    grad_recv = send(grad_out).astype(jnp.float32)
    centroid = centroids[0]
    gate = jax.nn.sigmoid(jnp.sum(expert_in * centroid, -1))[:, None]
    grad_upper = gate * grad_recv
    ff = w_in.shape[3]
    my_bias = lax.dynamic_slice_in_dim(in_biases[0], lax.axis_index("rep") * ff, ff, 1)

    def sub_forward(values, k):
        normed = gather_rows(layer_norm(values, norm_gains[0, k], norm_biases[0, k]).astype(jnp.bfloat16))
        inner = jnp.dot(normed, w_in[0, k], preferred_element_type=jnp.float32) + my_bias[k]
        act = jax.nn.gelu(inner).astype(jnp.bfloat16)
        outer = scatter_rows(jnp.dot(act, w_out[0, k], preferred_element_type=jnp.float32))
        return (values + outer + out_biases[0, k], (values, normed, inner, act))

    middle, kept_first = sub_forward(expert_in, 0)
    upper, kept_second = sub_forward(middle, 1)
    result = (gate * upper).astype(jnp.bfloat16)
    mixed = (tokens.astype(jnp.float32) + live * give_back(result)).astype(jnp.bfloat16)
    grad_logit = jnp.sum(grad_recv * upper, -1, keepdims=True) * gate * (1.0 - gate)
    grad_centroid = jnp.sum(grad_logit * expert_in, 0)

    def sub_backward(grad_top, kept, k):
        values, normed, inner, act = kept
        grad_outer = gather_rows(grad_top.astype(jnp.bfloat16))
        grad_second = contract_rows(act, grad_outer)
        grad_sbias = jnp.sum(grad_top, 0)
        grad_act = contract_cols(grad_outer, w_out[0, k])
        grad_inner = jax.vjp(jax.nn.gelu, inner)[1](grad_act)[0]
        grad_fbias = jnp.sum(grad_inner, 0)
        grad_inner_low = grad_inner.astype(jnp.bfloat16)
        grad_first = contract_rows(normed, grad_inner_low)
        grad_normed = scatter_rows(contract_cols(grad_inner_low, w_in[0, k]))
        norm_pull = jax.vjp(layer_norm, values, norm_gains[0, k], norm_biases[0, k])[1]
        grad_values, grad_gain, grad_nbias = norm_pull(grad_normed)
        return (
            grad_top + grad_values,
            (grad_first, grad_second),
            (grad_gain, grad_nbias, grad_fbias, grad_sbias),
        )

    grad_middle, large_second, small_second = sub_backward(grad_upper, kept_second, 1)
    grad_input, large_first, small_first = sub_backward(grad_middle, kept_first, 0)
    w_in_grad = jnp.stack([large_first[0], large_second[0]], 0)[None]
    w_out_grad = jnp.stack([large_first[1], large_second[1]], 0)[None]
    grad_local = (grad_input + grad_logit * centroid).astype(jnp.bfloat16)
    tokens_grad = (cotangent.astype(jnp.float32) + give_back(grad_local)).astype(jnp.bfloat16)

    def stacked(i):
        return jnp.stack([small_first[i], small_second[i]], 0)[None]

    in_bias_grad = lax.all_gather(stacked(2), "rep", axis=2, tiled=True)
    centroid_grad, gain_grad, norm_bias_grad, out_bias_grad = lax.psum(
        (grad_centroid[None], stacked(0), stacked(1), stacked(3)), "rep"
    )
    return (
        mixed,
        tokens_grad,
        centroid_grad,
        gain_grad,
        norm_bias_grad,
        w_in_grad,
        in_bias_grad,
        w_out_grad,
        out_bias_grad,
    )


def solution(mesh):
    placed = (
        P(("rep", "exp"), None),
        P(("rep", "exp"), None),
        P(),
        P("exp", None),
        P("exp", None, None),
        P("exp", None, None),
        P("exp", None, None, "rep"),
        P("exp", None, None),
        P("exp", None, "rep", None),
        P("exp", None, None),
        P(("rep", "exp"), None),
    )
    return jax.shard_map(
        shards,
        mesh=mesh,
        in_specs=placed,
        out_specs=(
            P(("rep", "exp"), None),
            P(("rep", "exp"), None),
            P("exp", None),
            P("exp", None, None),
            P("exp", None, None),
            P("exp", None, None, "rep"),
            P("exp", None, None),
            P("exp", None, "rep", None),
            P("exp", None, None),
        ),
        check_vma=False,
    )
```

```python
import functools

import jax
import jax.numpy as jnp
from jax import lax
from jax.experimental import pallas as pl
from jax.experimental.pallas import tpu as pltpu
from jax.sharding import PartitionSpec as P

SLOT = 2048


eps = 1e-05
VMEM_BYTES = 60 * 1024 * 1024


def contract_rows(left, right):
    return lax.dot_general(
        left, right, (((0,), (0,)), ((), ())), preferred_element_type=jnp.float32
    )


def contract_cols(left, right):
    return lax.dot_general(
        left, right, (((1,), (1,)), ((), ())), preferred_element_type=jnp.float32
    )


MESH = pl.DeviceIdType.MESH
CHUNKS = 4
POOL = 4
ROOT = 0.7978845608028654
CUBE = 0.044715


def layer_stats(values):
    center = values - jnp.mean(values, -1, keepdims=True)
    spread = jnp.mean(center * center, -1, keepdims=True)
    scale = lax.rsqrt(spread + eps)
    return center * scale, scale


def gelu_and_slope(inner):
    square = inner * inner
    bent = jnp.tanh(inner * (ROOT + (ROOT * CUBE) * square))
    half = 0.5 * (1.0 + bent)
    slope = half + (0.5 * inner) * (1.0 - bent * bent) * (ROOT + (3.0 * ROOT * CUBE) * square)
    return inner * half, slope


def fold(rows):
    return jnp.sum(rows.reshape(rows.shape[0] // 8, 8, rows.shape[1]), 0)


def kernel(
    n,
    x_ref,
    dy_ref,
    gain_ref,
    nbias_ref,
    cent_ref,
    bin_ref,
    bout_ref,
    wi_hbm,
    wo_hbm,
    y_ref,
    dv_ref,
    gwi_hbm,
    gwo_hbm,
    sums_ref,
    bins_ref,
    gath,
    wi,
    wo,
    gwi,
    gwo,
    part,
    act,
    dq,
    slope,
    total,
    state,
    dlog,
    recv,
    stage,
    accs,
    bacc,
    mine,
    peers,
    send_sem,
    recv_sem,
    load_sem,
    store_sem,
    peer_send,
    peer_recv,
):
    r = lax.axis_index("rep")
    rows, width = x_ref.shape
    hidden = bin_ref.shape[1]
    chunk = rows // CHUNKS
    half = chunk // 2
    ops = 4 * CHUNKS
    rounds = ops + 1
    block = min(32, chunk)
    tile = min(512, hidden)
    wtile = hidden // 4
    last = n - 1

    def op_type(i):
        return jnp.where(i < CHUNKS, 0, jnp.where(i >= 3 * CHUNKS, 3, 1 + lax.rem(i + CHUNKS, 2)))

    def op_chunk(i):
        return jnp.where(
            i < CHUNKS, i, jnp.where(i >= 3 * CHUNKS, i - 3 * CHUNKS, (i - CHUNKS) // 2)
        )

    def op_slot(i):
        return jnp.where(i < CHUNKS, i, CHUNKS + lax.rem(i, POOL))

    def half_rows(h):
        return pl.ds(h * half, half)

    ahead = (jnp.minimum(r + 1, last), jnp.maximum(r - 1, 0))
    pos = (r, last - r)

    def item_sent(d, s):
        return lax.rem(r - s + n, n) if d == 0 else lax.rem(r + s, n)

    def sends(d, k, s):
        return (pos[d] < last) & jnp.where(s <= pos[d], k < ops, k >= 1)

    def receives(d, k, s):
        return (pos[d] > 0) & jnp.where(s <= pos[d] - 1, k < ops, k >= 1)

    def copy(d, k, s, h, src, dst):
        return pltpu.make_async_remote_copy(
            src_ref=src,
            dst_ref=dst,
            send_sem=send_sem.at[d, lax.rem(s, 2), h],
            recv_sem=recv_sem.at[d, lax.rem(k, 2), s, h],
            device_id={"rep": ahead[d]},
            device_id_type=MESH,
        )

    def landing(d, k, s, h):
        return recv.at[d, lax.rem(k, 2), s, h]

    def wait_sent(d, k, s, h):
        @pl.when(sends(d, k, s))
        def _():
            copy(d, k, s, h, stage.at[d, lax.rem(s, 2), h], landing(d, k, s, h)).wait_send()

    def wait_received(d, k, s, h):
        @pl.when(receives(d, k, s))
        def _():
            copy(d, k, s, h, stage.at[d, lax.rem(s, 2), h], landing(d, k, s, h)).wait_recv()

    def finish_sum(k, h):
        rs = half_rows(h)
        total[rs, :] = part[r, rs, :]
        for d in range(2):

            @pl.when(pos[d] > 0)
            def _():
                total[rs, :] += landing(d, k, n - 1, h)[...].astype(jnp.float32)

    def send(d, k, s, h):
        gathers = s <= pos[d]
        p = item_sent(d, s)
        rs = half_rows(h)

        @pl.when(sends(d, k, s) & gathers)
        def _():
            here = gath.at[op_slot(k), p, rs]
            copy(d, k, s, h, here, here).start()

        @pl.when(sends(d, k, s) & jnp.logical_not(gathers))
        def _():
            out = stage.at[d, lax.rem(s, 2), h]

            @pl.when(pos[d] == 0)
            def _():
                out[...] = part[p, rs, :].astype(jnp.bfloat16)

            @pl.when(pos[d] > 0)
            def _():
                came = landing(d, k, s - 1, h)[...].astype(jnp.float32)
                out[...] = (part[p, rs, :] + came).astype(jnp.bfloat16)

            copy(d, k, s, h, out, landing(d, k, s, h)).start()

    def over_blocks(body):
        def step(b, carry):
            body(pl.multiple_of(b * block, block))
            return carry

        lax.fori_loop(0, chunk // block, step, 0)

    def gate_of(x):
        return jax.nn.sigmoid(jnp.sum(x * cent_ref[...], -1, keepdims=True))

    def prepare(i):
        kind, c, slot = op_type(i), op_chunk(i), op_slot(i)

        def own(offset, value):
            gath[slot, r, pl.ds(offset, block), :] = value.astype(jnp.bfloat16)

        def source(offset):
            return pl.ds(pl.multiple_of(c * chunk + offset, block), block)

        @pl.when(kind == 0)
        def _():
            over_blocks(
                lambda o: own(
                    o,
                    layer_stats(x_ref[source(o), :].astype(jnp.float32))[0] * gain_ref[0:1, :]
                    + nbias_ref[0:1, :],
                )
            )

        @pl.when(kind == 1)
        def _():
            over_blocks(
                lambda o: own(
                    o, layer_stats(state[source(o), :])[0] * gain_ref[1:2, :] + nbias_ref[1:2, :]
                )
            )

        @pl.when(kind == 2)
        def _():
            over_blocks(
                lambda o: own(
                    o,
                    gate_of(x_ref[source(o), :].astype(jnp.float32))
                    * dy_ref[source(o), :].astype(jnp.float32),
                )
            )

        @pl.when(kind == 3)
        def _():
            over_blocks(lambda o: own(o, state[source(o), :]))

    def norm_back(values, grad, k):
        unit, scale = layer_stats(values)
        accs[1 + k] += fold(grad * unit)
        accs[3 + k] += fold(grad)
        through = grad * gain_ref[k : k + 1, :]
        return scale * (
            through
            - jnp.mean(through, -1, keepdims=True)
            - unit * jnp.mean(through * unit, -1, keepdims=True)
        )

    def finish(i):
        kind, c = op_type(i), op_chunk(i)

        def source(offset):
            return pl.ds(pl.multiple_of(c * chunk + offset, block), block)

        @pl.when(kind == 0)
        def _():
            def body(o):
                state[source(o), :] = (
                    x_ref[source(o), :].astype(jnp.float32)
                    + total[pl.ds(o, block), :]
                    + bout_ref[0:1, :]
                )

            over_blocks(body)

        @pl.when(kind == 1)
        def _():
            def body(o):
                x = x_ref[source(o), :].astype(jnp.float32)
                dy = dy_ref[source(o), :].astype(jnp.float32)
                upper = state[source(o), :] + total[pl.ds(o, block), :] + bout_ref[1:2, :]
                gate = gate_of(x)
                y_ref[source(o), :] = (gate * upper).astype(jnp.bfloat16)
                logit = jnp.sum(dy * upper, -1, keepdims=True) * gate * (1.0 - gate)
                dlog[source(o), :] = jnp.broadcast_to(logit, (block, dlog.shape[1]))
                accs[0] += fold(logit * x)

            over_blocks(body)

        @pl.when(kind == 2)
        def _():
            def body(o):
                x = x_ref[source(o), :].astype(jnp.float32)
                top = gate_of(x) * dy_ref[source(o), :].astype(jnp.float32)
                middle = top + norm_back(state[source(o), :], total[pl.ds(o, block), :], 1)
                state[source(o), :] = middle
                accs[5] += fold(middle)
                accs[6] += fold(top)

            over_blocks(body)

        @pl.when(kind == 3)
        def _():
            def body(o):
                x = x_ref[source(o), :].astype(jnp.float32)
                dv_ref[source(o), :] = (
                    state[source(o), :]
                    + norm_back(x, total[pl.ds(o, block), :], 0)
                    + dlog[source(o), 0:1] * cent_ref[...]
                ).astype(jnp.bfloat16)

            over_blocks(body)

    def over_tiles(count, size, body):
        def step(j, carry):
            body(pl.ds(pl.multiple_of(j * size, size), size))
            return carry

        lax.fori_loop(0, count, step, 0)

    def item_first(i, par, p):
        kind = op_type(i)
        k = jnp.where((kind == 1) | (kind == 2), 1, 0)
        slot = jnp.where(
            kind == 2, op_slot(i - 1), jnp.where(kind == 3, op_chunk(i), op_slot(i))
        )

        def body(cs):
            inner = (
                jnp.dot(gath[slot, p], wi[k, :, cs], preferred_element_type=jnp.float32)
                + bin_ref[pl.ds(k, 1), cs]
            )
            low, pull = gelu_and_slope(inner)
            act[par, p, :, cs] = low.astype(jnp.bfloat16)
            slope[:, cs] = pull

        over_tiles(hidden // tile, tile, body)

    def item_second(i, par, p):
        kind = op_type(i)
        k = jnp.where((kind == 1) | (kind == 2), 1, 0)

        @pl.when(kind < 2)
        def _():
            def body(cs):
                part[p, :, cs] = jnp.dot(
                    act[par, p], wo[k, :, cs], preferred_element_type=jnp.float32
                )

            over_tiles(width // tile, tile, body)

        @pl.when(kind >= 2)
        def _():
            slot = op_slot(i)

            def pull(cs):
                grad = contract_cols(gath[slot, p], wo[k, cs, :]) * slope[:, cs]
                bacc[k, :, cs] += fold(grad)
                dq[par, p, :, cs] = grad.astype(jnp.bfloat16)

            over_tiles(hidden // tile, tile, pull)

            def push(cs):
                part[p, :, cs] = contract_cols(dq[par, p], wi[k, cs, :])

            over_tiles(width // tile, tile, push)

    def weight_grads(i, par, j):
        kind = op_type(i)
        k = jnp.where(kind == 2, 1, 0)
        slot = jnp.where(kind == 2, op_slot(i - 1), op_chunk(i))
        cs = pl.ds(pl.multiple_of(j * wtile, wtile), wtile)
        depth = n * chunk
        normed = gath[slot, :, :, cs].reshape(depth, wtile)
        gwi[k, cs, :] += contract_rows(normed, dq[par].reshape(depth, hidden))
        active = act[par, :, :, cs].reshape(depth, wtile)
        gwo[k, cs, :] += contract_rows(active, gath[op_slot(i)].reshape(depth, width))

    def item_at(s):
        near = jnp.minimum(r, last - r)
        base = jnp.where(near == 0, last - s, jnp.where(s < 2, last - s, s - 2))
        return jnp.where(r < 2, base, last - base)

    def load(w):
        src, dst = ((wi_hbm, wi), (wo_hbm, wo))[w]
        return pltpu.make_async_copy(src, dst, load_sem.at[w])

    def store(w, k):
        src, dst = ((gwi, gwi_hbm), (gwo, gwo_hbm))[w]
        return pltpu.make_async_copy(src.at[k], dst.at[k], store_sem.at[w, k])

    barrier = pltpu.get_barrier_semaphore()
    for q in range(1, n):
        pl.semaphore_signal(
            barrier, inc=1, device_id={"rep": lax.rem(r + q, n)}, device_id_type=MESH
        )
    load(0).start()
    load(1).start()
    prepare(0)
    pl.semaphore_wait(barrier, n - 1)

    def step(t, carry):
        k, s = t // n, lax.rem(t, n)
        k_before, s_before = (t - 1) // n, lax.rem(t + n - 1, n)
        i = k - 1
        par = lax.rem(k, 2)
        p = item_at(s)

        def exchange(h):
            for d in range(2):

                @pl.when(t >= 1)
                def _():
                    wait_received(d, k_before, s_before, h)

                @pl.when(t >= 2)
                def _():
                    wait_sent(d, (t - 2) // n, lax.rem(t + n - 2, n), h)

            @pl.when((s == 0) & (k >= 2))
            def _():
                finish_sum(k - 1, h)

            for d in range(2):
                send(d, k, s, h)

        def grads(j):
            old = k - 2

            @pl.when((s < 2) & (old >= CHUNKS) & (op_type(old) >= 2))
            def _():
                weight_grads(old, lax.rem(k + 1, 2), j)

        exchange(0)

        @pl.when(t == 0)
        def _():
            def clear(b, carry):
                zero_rows = pl.ds(pl.multiple_of(b * 64, 64), 64)
                for w in range(2):
                    gwi[w, zero_rows, :] = jnp.zeros((64, hidden), jnp.float32)
                    gwo[w, zero_rows, :] = jnp.zeros((64, width), jnp.float32)
                return carry

            lax.fori_loop(0, width // 64, clear, 0)
            accs[...] = jnp.zeros_like(accs)
            bacc[...] = jnp.zeros_like(bacc)

        @pl.when(t == n)
        def _():
            load(0).wait()
            load(1).wait()

        @pl.when(k >= 1)
        def _():
            item_first(i, par, p)

        grads(2 * s)
        exchange(1)

        @pl.when(k >= 1)
        def _():
            item_second(i, par, p)

        grads(2 * s + 1)

        @pl.when((s == 2) & (k >= 2))
        def _():
            finish(k - 2)

        @pl.when((s == 3) & (k < ops - 1))
        def _():
            prepare(k + 1)

        @pl.when(t == n * (3 * CHUNKS + 1) + 2)
        def _():
            store(0, 1).start()
            store(1, 1).start()

        return carry

    steps = rounds * n
    lax.fori_loop(0, steps, step, 0)

    def last_grads(j, carry):
        weight_grads(ops - 1, (rounds - 1) % 2, j)
        return carry

    lax.fori_loop(0, 4, last_grads, 0)
    store(0, 0).start()
    store(1, 0).start()
    for h in range(2):
        for d in range(2):
            wait_received(d, rounds - 1, n - 1, h)
        finish_sum(rounds - 1, h)
    finish(ops - 1)
    for h in range(2):
        for d in range(2):
            for back in (2, 1):
                wait_sent(d, (steps - back) // n, (steps - back) % n, h)

    for a in range(7):
        mine[a : a + 1, :width] = jnp.sum(accs[a], 0, keepdims=True)
    mine[7:8, :] = jnp.zeros((1, mine.shape[1]), jnp.float32)
    for k in range(2):
        mine[8 + k : 9 + k, :hidden] = jnp.sum(bacc[k], 0, keepdims=True)
    mine[10:16, :] = jnp.zeros((6, mine.shape[1]), jnp.float32)

    def tell(q):
        return pltpu.make_async_remote_copy(
            src_ref=mine,
            dst_ref=peers.at[q - 1],
            send_sem=peer_send.at[q - 1],
            recv_sem=peer_recv.at[q - 1],
            device_id={"rep": lax.rem(r + q, n)},
            device_id_type=MESH,
        )

    for q in range(1, n):
        tell(q).start()
    sums = mine[0:8, :width]
    bins_ref[r] = mine[8:16, :hidden]
    for q in range(1, n):
        tell(q).wait_recv()
        sums += peers[q - 1, 0:8, :width]
        bins_ref[lax.rem(r - q + n, n)] = peers[q - 1, 8:16, :hidden]
    sums_ref[...] = sums
    for q in range(1, n):
        tell(q).wait_send()
    for w in range(2):
        for k in range(2):
            store(w, k).wait()


def run_layer(x, dy, gains, nbias, cent, my_bias, bout, wi, wo):
    n = lax.axis_size("rep")
    rows, width = x.shape
    hidden = wi.shape[2]
    chunk = rows // CHUNKS
    half = chunk // 2
    wide = max(width, hidden)
    low, full = jnp.bfloat16, jnp.float32
    vmem = pl.BlockSpec(memory_space=pltpu.VMEM)
    anywhere = pl.BlockSpec(memory_space=pl.ANY)
    flops = 2 * 16 * n * rows * width * hidden
    return pl.pallas_call(
        functools.partial(kernel, n),
        out_shape=(
            jax.ShapeDtypeStruct((rows, width), low),
            jax.ShapeDtypeStruct((rows, width), low),
            jax.ShapeDtypeStruct((2, width, hidden), full),
            jax.ShapeDtypeStruct((2, hidden, width), full),
            jax.ShapeDtypeStruct((8, width), full),
            jax.ShapeDtypeStruct((n, 8, hidden), full),
        ),
        in_specs=[vmem] * 7 + [anywhere] * 2,
        out_specs=(vmem, vmem, anywhere, anywhere, vmem, vmem),
        scratch_shapes=[
            pltpu.VMEM((CHUNKS + POOL, n, chunk, width), low),
            pltpu.VMEM((2, width, hidden), low),
            pltpu.VMEM((2, hidden, width), low),
            pltpu.VMEM((2, width, hidden), full),
            pltpu.VMEM((2, hidden, width), full),
            pltpu.VMEM((n, chunk, width), full),
            pltpu.VMEM((2, n, chunk, hidden), low),
            pltpu.VMEM((2, n, chunk, hidden), low),
            pltpu.VMEM((chunk, hidden), full),
            pltpu.VMEM((chunk, width), full),
            pltpu.VMEM((rows, width), full),
            pltpu.VMEM((rows, 128), full),
            pltpu.VMEM((2, 2, n, 2, half, width), low),
            pltpu.VMEM((2, 2, 2, half, width), low),
            pltpu.VMEM((7, 8, width), full),
            pltpu.VMEM((2, 8, hidden), full),
            pltpu.VMEM((16, wide), full),
            pltpu.VMEM((n - 1, 16, wide), full),
            pltpu.SemaphoreType.DMA((2, 2, 2)),
            pltpu.SemaphoreType.DMA((2, 2, n, 2)),
            pltpu.SemaphoreType.DMA((2,)),
            pltpu.SemaphoreType.DMA((2, 2)),
            pltpu.SemaphoreType.DMA((n - 1,)),
            pltpu.SemaphoreType.DMA((n - 1,)),
        ],
        compiler_params=pltpu.CompilerParams(
            collective_id=0, has_side_effects=True, vmem_limit_bytes=VMEM_BYTES
        ),
        cost_estimate=pl.CostEstimate(
            flops=flops, bytes_accessed=40 * rows * width, transcendentals=8 * rows * hidden * n
        ),
    )(x, dy, gains, nbias, cent, my_bias, bout, wi, wo)


def shards(
    tokens,
    routes,
    lengths,
    centroids,
    norm_gains,
    norm_biases,
    w_in,
    in_biases,
    w_out,
    out_biases,
    cotangent,
):
    n_exp = lax.axis_size("exp")
    tok_rows = tokens.shape[0]
    cap = tok_rows // n_exp
    device = lax.axis_index(("rep", "exp"))
    positions = device * tok_rows + lax.iota(jnp.int32, tok_rows)
    seq_ids = positions // SLOT
    seq_table = lax.iota(jnp.int32, lengths.shape[0])
    seq_len = jnp.sum(jnp.where(seq_ids[:, None] == seq_table[None, :], lengths[None, :], 0), 1)
    live = (positions % SLOT < seq_len).astype(jnp.float32)[:, None]
    route = routes[:, 0]
    hits = (route[:, None] == lax.iota(jnp.int32, n_exp)[None, :]).astype(jnp.int32)
    before = jnp.cumsum(hits, 0) - hits
    target = route * cap + jnp.sum(before * hits, 1)
    place = (lax.iota(jnp.int32, tok_rows)[:, None] == target[None, :]).astype(jnp.bfloat16)
    grad_out = (live * cotangent.astype(jnp.float32)).astype(jnp.bfloat16)

    def send(rows):
        ordered = jnp.dot(place, rows, preferred_element_type=jnp.float32).astype(jnp.bfloat16)
        return lax.all_to_all(ordered, "exp", split_axis=0, concat_axis=0, tiled=True)

    def give_back(rows):
        back = lax.all_to_all(rows, "exp", split_axis=0, concat_axis=0, tiled=True)
        return contract_rows(place, back)

    ff = w_in.shape[3]
    my_bias = lax.dynamic_slice_in_dim(in_biases[0], lax.axis_index("rep") * ff, ff, 1)
    result, grad_local, w_in_grad, w_out_grad, sums, bins = run_layer(
        send(tokens),
        send(grad_out),
        norm_gains[0],
        norm_biases[0],
        centroids,
        my_bias,
        out_biases[0],
        w_in[0],
        w_out[0],
    )
    mixed = (tokens.astype(jnp.float32) + live * give_back(result)).astype(jnp.bfloat16)
    tokens_grad = (cotangent.astype(jnp.float32) + give_back(grad_local)).astype(jnp.bfloat16)
    in_bias_grad = jnp.transpose(bins[:, 0:2], (1, 0, 2)).reshape(1, 2, -1)
    return (
        mixed,
        tokens_grad,
        sums[0:1],
        sums[1:3][None],
        sums[3:5][None],
        w_in_grad[None],
        in_bias_grad,
        w_out_grad[None],
        sums[5:7][None],
    )


def solution(mesh):
    placed = (
        P(("rep", "exp"), None),
        P(("rep", "exp"), None),
        P(),
        P("exp", None),
        P("exp", None, None),
        P("exp", None, None),
        P("exp", None, None, "rep"),
        P("exp", None, None),
        P("exp", None, "rep", None),
        P("exp", None, None),
        P(("rep", "exp"), None),
    )
    return jax.shard_map(
        shards,
        mesh=mesh,
        in_specs=placed,
        out_specs=(
            P(("rep", "exp"), None),
            P(("rep", "exp"), None),
            P("exp", None),
            P("exp", None, None),
            P("exp", None, None),
            P("exp", None, None, "rep"),
            P("exp", None, None),
            P("exp", None, "rep", None),
            P("exp", None, None),
        ),
        check_vma=False,
    )
```

```python
import functools

import jax
import jax.numpy as jnp
from jax import lax
from jax.experimental import pallas as pl
from jax.experimental.pallas import tpu as pltpu
from jax.sharding import PartitionSpec as P

eps = 1e-05
VMEM_BYTES = 60 * 1024 * 1024


def contract_rows(left, right):
    return lax.dot_general(
        left, right, (((0,), (0,)), ((), ())), preferred_element_type=jnp.float32
    )


def contract_cols(left, right):
    return lax.dot_general(
        left, right, (((1,), (1,)), ((), ())), preferred_element_type=jnp.float32
    )


MESH = pl.DeviceIdType.MESH
CHUNKS = 4
POOL = 4
ROOT = 0.7978845608028654
CUBE = 0.044715


def layer_stats(values):
    center = values - jnp.mean(values, -1, keepdims=True)
    spread = jnp.mean(center * center, -1, keepdims=True)
    scale = lax.rsqrt(spread + eps)
    return center * scale, scale


def gelu_and_slope(inner):
    square = inner * inner
    bent = jnp.tanh(inner * (ROOT + (ROOT * CUBE) * square))
    half = 0.5 * (1.0 + bent)
    slope = half + (0.5 * inner) * (1.0 - bent * bent) * (ROOT + (3.0 * ROOT * CUBE) * square)
    return inner * half, slope


def fold(rows):
    return jnp.sum(rows.reshape(rows.shape[0] // 8, 8, rows.shape[1]), 0)


def order_of(blocks):
    if blocks == 1:
        return [0]
    others = [b for b in range(2, blocks, 2)] + [b for b in range(blocks - 1, 2, -2)]
    return [0] + others + [1]


def flip(index, bits):
    out, place = index, 1
    while place <= bits:
        if bits & place:
            out = out + place * (1 - 2 * lax.rem(index // place, 2))
        place *= 2
    return out


def slot_rows(routes, blocks, cap):
    rows = routes.shape[1]
    along = routes.astype(jnp.float32)
    table = lax.broadcasted_iota(jnp.int32, (max(blocks, 8), rows), 0).astype(jnp.float32)
    hits = (table == along).astype(jnp.float32)
    first = lax.broadcasted_iota(jnp.int32, (rows, rows), 0)
    second = lax.broadcasted_iota(jnp.int32, (rows, rows), 1)
    earlier = (first < second).astype(jnp.bfloat16)
    before = jnp.dot(hits.astype(jnp.bfloat16), earlier, preferred_element_type=jnp.float32)
    target = along * cap + jnp.sum(before * hits, 0, keepdims=True)
    return (first.astype(jnp.float32) == target).astype(jnp.bfloat16)


def live_rows(lengths_ref, device, devices, rows):
    slot = rows * devices // lengths_ref.shape[0]
    start = device * rows
    count = lengths_ref[start // slot] - lax.rem(start, slot)
    return (lax.broadcasted_iota(jnp.int32, (rows, 1), 0) < count).astype(jnp.float32)


def kernel(n, blocks, inside, *refs):
    refs = list(refs)
    take = lambda count: [refs.pop(0) for _ in range(count)]
    if inside:
        tok_ref, cot_ref, routes_ref, lengths_ref = take(4)
    else:
        x_ref, dy_ref = take(2)
    gain_ref, nbias_ref, cent_ref, bias_ref, bout_ref, wi_hbm, wo_hbm = take(7)
    home_y, home_dv, gwi_hbm, gwo_hbm, cent_out, gain_out, nbias_out, bin_out, bout_out = take(9)
    gath, wi, wo, gwi, gwo, part, act, dq, slope, total, state, dlog, recv, stage = take(14)
    accs, bacc, mine, peers = take(4)
    send_sem, recv_sem, load_sem, store_sem, peer_send, peer_recv = take(6)
    if inside:
        x_ref, dy_ref, y_ref, dv_ref, place, out_x, out_dy = take(7)
        out_send, out_recv, home_send, home_recv, home_own = take(5)
    else:
        y_ref, dv_ref = home_y, home_dv
    r = lax.axis_index("rep")
    e = lax.axis_index("exp")
    rows, width = x_ref.shape
    hidden = wi_hbm.shape[2]
    cap = rows // blocks
    order = order_of(blocks)
    per_chunk = blocks // CHUNKS
    chunk = rows // CHUNKS
    half = chunk // 2
    ops = 4 * CHUNKS
    rounds = ops + 1
    block = min(32, half)
    tile = min(512, hidden)
    wtile = hidden // 4
    last = n - 1

    def op_type(i):
        return jnp.where(i < CHUNKS, 0, jnp.where(i >= 3 * CHUNKS, 3, 1 + lax.rem(i + CHUNKS, 2)))

    def op_chunk(i):
        return jnp.where(
            i < CHUNKS, i, jnp.where(i >= 3 * CHUNKS, i - 3 * CHUNKS, (i - CHUNKS) // 2)
        )

    def op_slot(i):
        return jnp.where(i < CHUNKS, i, CHUNKS + lax.rem(i, POOL))

    def half_rows(h):
        return pl.ds(h * half, half)

    ahead = (jnp.minimum(r + 1, last), jnp.maximum(r - 1, 0))
    pos = (r, last - r)

    def item_sent(d, s):
        return lax.rem(r - s + n, n) if d == 0 else lax.rem(r + s, n)

    def sends(d, k, s):
        return (pos[d] < last) & jnp.where(s <= pos[d], k < ops, k >= 1)

    def receives(d, k, s):
        return (pos[d] > 0) & jnp.where(s <= pos[d] - 1, k < ops, k >= 1)

    def copy(d, k, s, h, src, dst):
        return pltpu.make_async_remote_copy(
            src_ref=src,
            dst_ref=dst,
            send_sem=send_sem.at[d, lax.rem(s, 2), h],
            recv_sem=recv_sem.at[d, lax.rem(k, 2), s, h],
            device_id={"rep": ahead[d]},
            device_id_type=MESH,
        )

    def landing(d, k, s, h):
        return recv.at[d, lax.rem(k, 2), s, h]

    def wait_sent(d, k, s, h):
        @pl.when(sends(d, k, s))
        def _():
            copy(d, k, s, h, stage.at[d, lax.rem(s, 2), h], landing(d, k, s, h)).wait_send()

    def wait_received(d, k, s, h):
        @pl.when(receives(d, k, s))
        def _():
            copy(d, k, s, h, stage.at[d, lax.rem(s, 2), h], landing(d, k, s, h)).wait_recv()

    def finish_sum(k, h):
        rs = half_rows(h)
        total[rs, :] = part[r, rs, :]
        for d in range(2):

            @pl.when(pos[d] > 0)
            def _():
                total[rs, :] += landing(d, k, n - 1, h)[...].astype(jnp.float32)

    def send(d, k, s, h):
        gathers = s <= pos[d]
        p = item_sent(d, s)
        rs = half_rows(h)

        @pl.when(sends(d, k, s) & gathers)
        def _():
            here = gath.at[op_slot(k), p, rs]
            copy(d, k, s, h, here, here).start()

        @pl.when(sends(d, k, s) & jnp.logical_not(gathers))
        def _():
            out = stage.at[d, lax.rem(s, 2), h]

            @pl.when(pos[d] == 0)
            def _():
                out[...] = part[p, rs, :].astype(jnp.bfloat16)

            @pl.when(pos[d] > 0)
            def _():
                came = landing(d, k, s - 1, h)[...].astype(jnp.float32)
                out[...] = (part[p, rs, :] + came).astype(jnp.bfloat16)

            copy(d, k, s, h, out, landing(d, k, s, h)).start()

    def over_blocks(h, body):
        def step(b, carry):
            body(pl.multiple_of(h * half + b * block, block))
            return carry

        lax.fori_loop(0, half // block, step, 0)

    def cap_rows(q):
        return pl.ds(pl.multiple_of(q * cap, cap), cap)

    def outward(w, q):
        src, dst = ((out_x, x_ref), (out_dy, dy_ref))[w]
        return pltpu.make_async_remote_copy(
            src_ref=src.at[cap_rows(q)],
            dst_ref=dst.at[cap_rows(q)],
            send_sem=out_send.at[w, q],
            recv_sem=out_recv.at[w, q],
            device_id={"exp": flip(e, order[q])},
            device_id_type=MESH,
        )

    def homeward(w, q):
        src, dst = ((y_ref, home_y), (dv_ref, home_dv))[w]
        if q == 0:
            return pltpu.make_async_copy(
                src.at[cap_rows(q)], dst.at[cap_rows(e)], home_own.at[w]
            )
        return pltpu.make_async_remote_copy(
            src_ref=src.at[cap_rows(q)],
            dst_ref=dst.at[cap_rows(e)],
            send_sem=home_send.at[w, q],
            recv_sem=home_recv.at[w, q],
            device_id={"exp": flip(e, order[q])},
            device_id_type=MESH,
        )

    def dispatch(w):
        for q in range(blocks):
            expert = flip(e, order[q])
            picked = place[cap_rows(expert), :]
            source = tok_ref if w == 0 else cot_ref
            values = source[...]
            if w == 1:
                device = r * blocks + e
                values = (
                    live_rows(lengths_ref, device, n * blocks, rows) * values.astype(jnp.float32)
                ).astype(jnp.bfloat16)
            ordered = jnp.dot(picked, values, preferred_element_type=jnp.float32)
            target = ((x_ref, dy_ref) if q == 0 else (out_x, out_dy))[w]
            target[cap_rows(q), :] = ordered.astype(jnp.bfloat16)
            if q > 0:
                if w == 0 and q == 1:
                    pl.semaphore_wait(barrier, n - 1 + blocks - 1)
                outward(w, q).start()

    def each_block(c, h, body):
        for chunk_at in range(CHUNKS):

            @pl.when(c == chunk_at)
            def _():
                for q in range(
                    chunk_at * per_chunk + h * (per_chunk // 2),
                    chunk_at * per_chunk + (h + 1) * (per_chunk // 2),
                ):
                    body(q)

    def arrived(w, c, h):
        if inside:
            each_block(c, h, lambda q: outward(w, q).wait_recv() if q > 0 else None)

    def go_home(w, c, h):
        if inside:
            each_block(c, h, lambda q: homeward(w, q).start())

    def gate_of(x):
        return jax.nn.sigmoid(jnp.sum(x * cent_ref[...], -1, keepdims=True))

    def prepare(i, h):
        kind, c, slot = op_type(i), op_chunk(i), op_slot(i)

        def own(offset, value):
            gath[slot, r, pl.ds(offset, block), :] = value.astype(jnp.bfloat16)

        def source(offset):
            return pl.ds(pl.multiple_of(c * chunk + offset, block), block)

        @pl.when(kind == 0)
        def _():
            arrived(0, c, h)
            over_blocks(
                h,
                lambda o: own(
                    o,
                    layer_stats(x_ref[source(o), :].astype(jnp.float32))[0] * gain_ref[0:1, :]
                    + nbias_ref[0:1, :],
                )
            )

        @pl.when(kind == 1)
        def _():
            over_blocks(
                h,
                lambda o: own(
                    o, layer_stats(state[source(o), :])[0] * gain_ref[1:2, :] + nbias_ref[1:2, :]
                )
            )

        @pl.when(kind == 2)
        def _():
            arrived(1, c, h)
            over_blocks(
                h,
                lambda o: own(
                    o,
                    gate_of(x_ref[source(o), :].astype(jnp.float32))
                    * dy_ref[source(o), :].astype(jnp.float32),
                )
            )

        @pl.when(kind == 3)
        def _():
            over_blocks(h, lambda o: own(o, state[source(o), :]))

    def norm_back(values, grad, k):
        unit, scale = layer_stats(values)
        accs[1 + k] += fold(grad * unit)
        accs[3 + k] += fold(grad)
        through = grad * gain_ref[k : k + 1, :]
        return scale * (
            through
            - jnp.mean(through, -1, keepdims=True)
            - unit * jnp.mean(through * unit, -1, keepdims=True)
        )

    def finish(i, h):
        kind, c = op_type(i), op_chunk(i)

        def source(offset):
            return pl.ds(pl.multiple_of(c * chunk + offset, block), block)

        @pl.when(kind == 0)
        def _():
            def body(o):
                state[source(o), :] = (
                    x_ref[source(o), :].astype(jnp.float32)
                    + total[pl.ds(o, block), :]
                    + bout_ref[0:1, :]
                )

            over_blocks(h, body)

        @pl.when(kind == 1)
        def _():
            def body(o):
                x = x_ref[source(o), :].astype(jnp.float32)
                dy = dy_ref[source(o), :].astype(jnp.float32)
                upper = state[source(o), :] + total[pl.ds(o, block), :] + bout_ref[1:2, :]
                gate = gate_of(x)
                y_ref[source(o), :] = (gate * upper).astype(jnp.bfloat16)
                logit = jnp.sum(dy * upper, -1, keepdims=True) * gate * (1.0 - gate)
                dlog[source(o), :] = jnp.broadcast_to(logit, (block, dlog.shape[1]))
                accs[0] += fold(logit * x)

            over_blocks(h, body)
            go_home(0, c, h)

        @pl.when(kind == 2)
        def _():
            def body(o):
                x = x_ref[source(o), :].astype(jnp.float32)
                top = gate_of(x) * dy_ref[source(o), :].astype(jnp.float32)
                middle = top + norm_back(state[source(o), :], total[pl.ds(o, block), :], 1)
                state[source(o), :] = middle
                accs[5] += fold(middle)
                accs[6] += fold(top)

            over_blocks(h, body)

        @pl.when(kind == 3)
        def _():
            def body(o):
                x = x_ref[source(o), :].astype(jnp.float32)
                dv_ref[source(o), :] = (
                    state[source(o), :]
                    + norm_back(x, total[pl.ds(o, block), :], 0)
                    + dlog[source(o), 0:1] * cent_ref[...]
                ).astype(jnp.bfloat16)

            over_blocks(h, body)
            go_home(1, c, h)

    def over_tiles(count, size, body):
        def step(j, carry):
            body(pl.ds(pl.multiple_of(j * size, size), size))
            return carry

        lax.fori_loop(0, count, step, 0)

    def item_first(i, par, p):
        kind = op_type(i)
        k = jnp.where((kind == 1) | (kind == 2), 1, 0)
        slot = jnp.where(
            kind == 2, op_slot(i - 1), jnp.where(kind == 3, op_chunk(i), op_slot(i))
        )

        def body(cs):
            inner = (
                jnp.dot(gath[slot, p], wi[k, :, cs], preferred_element_type=jnp.float32)
                + bias_ref[pl.ds(k, 1), pl.ds(pl.multiple_of(r * hidden + cs.start, tile), tile)]
            )
            low, pull = gelu_and_slope(inner)
            act[par, p, :, cs] = low.astype(jnp.bfloat16)
            slope[:, cs] = pull

        over_tiles(hidden // tile, tile, body)

    def item_second(i, par, p):
        kind = op_type(i)
        k = jnp.where((kind == 1) | (kind == 2), 1, 0)

        @pl.when(kind < 2)
        def _():
            def body(cs):
                part[p, :, cs] = jnp.dot(
                    act[par, p], wo[k, :, cs], preferred_element_type=jnp.float32
                )

            over_tiles(width // tile, tile, body)

        @pl.when(kind >= 2)
        def _():
            slot = op_slot(i)

            def pull(cs):
                grad = contract_cols(gath[slot, p], wo[k, cs, :]) * slope[:, cs]
                bacc[k, :, cs] += fold(grad)
                dq[par, p, :, cs] = grad.astype(jnp.bfloat16)

            over_tiles(hidden // tile, tile, pull)

            def push(cs):
                part[p, :, cs] = contract_cols(dq[par, p], wi[k, cs, :])

            over_tiles(width // tile, tile, push)

    def weight_grads(i, par, j):
        kind = op_type(i)
        k = jnp.where(kind == 2, 1, 0)
        slot = jnp.where(kind == 2, op_slot(i - 1), op_chunk(i))
        cs = pl.ds(pl.multiple_of(j * wtile, wtile), wtile)
        depth = n * chunk
        normed = gath[slot, :, :, cs].reshape(depth, wtile)
        gwi[k, cs, :] += contract_rows(normed, dq[par].reshape(depth, hidden))
        active = act[par, :, :, cs].reshape(depth, wtile)
        gwo[k, cs, :] += contract_rows(active, gath[op_slot(i)].reshape(depth, width))

    def item_at(s):
        near = jnp.minimum(r, last - r)
        base = jnp.where(near == 0, last - s, jnp.where(s < 2, last - s, s - 2))
        return jnp.where(r < 2, base, last - base)

    def load(w):
        src, dst = ((wi_hbm, wi), (wo_hbm, wo))[w]
        return pltpu.make_async_copy(src, dst, load_sem.at[w])

    def store(w, k):
        src, dst = ((gwi, gwi_hbm), (gwo, gwo_hbm))[w]
        return pltpu.make_async_copy(src.at[k], dst.at[k], store_sem.at[w, k])

    barrier = pltpu.get_barrier_semaphore()
    for q in range(1, n):
        pl.semaphore_signal(
            barrier, inc=1, device_id={"rep": lax.rem(r + q, n)}, device_id_type=MESH
        )
    load(0).start()
    load(1).start()
    if inside:
        for b in range(1, blocks):
            pl.semaphore_signal(
                barrier, inc=1, device_id={"exp": flip(e, b)}, device_id_type=MESH
            )
        place[...] = slot_rows(routes_ref[...], blocks, cap)
        dispatch(0)
    else:
        pl.semaphore_wait(barrier, n - 1)
    prepare(0, 0)

    def step(t, carry):
        k, s = t // n, lax.rem(t, n)
        k_before, s_before = (t - 1) // n, lax.rem(t + n - 1, n)
        i = k - 1
        par = lax.rem(k, 2)
        p = item_at(s)

        def exchange(h):
            for d in range(2):

                @pl.when(t >= 1)
                def _():
                    wait_received(d, k_before, s_before, h)

                @pl.when(t >= 2)
                def _():
                    wait_sent(d, (t - 2) // n, lax.rem(t + n - 2, n), h)

            @pl.when((s == 0) & (k >= 2))
            def _():
                finish_sum(k - 1, h)

            for d in range(2):
                send(d, k, s, h)

        def grads(j):
            old = k - 2

            @pl.when((s < 2) & (old >= CHUNKS) & (op_type(old) >= 2))
            def _():
                weight_grads(old, lax.rem(k + 1, 2), j)

        exchange(0)

        @pl.when(t == 0)
        def _():
            prepare(0, 1)

        @pl.when(t == 1)
        def _():
            def clear(b, carry):
                zero_rows = pl.ds(pl.multiple_of(b * 64, 64), 64)
                for w in range(2):
                    gwi[w, zero_rows, :] = jnp.zeros((64, hidden), jnp.float32)
                    gwo[w, zero_rows, :] = jnp.zeros((64, width), jnp.float32)
                return carry

            lax.fori_loop(0, width // 64, clear, 0)
            accs[...] = jnp.zeros_like(accs)
            bacc[...] = jnp.zeros_like(bacc)

        if inside:

            @pl.when(t == 2)
            def _():
                dispatch(1)

        @pl.when(t == n)
        def _():
            load(0).wait()
            load(1).wait()

        @pl.when(k >= 1)
        def _():
            item_first(i, par, p)

        grads(2 * s)
        exchange(1)

        @pl.when(k >= 1)
        def _():
            item_second(i, par, p)

        grads(2 * s + 1)

        @pl.when((s == 2) & (k >= 2))
        def _():
            for h in range(2):
                finish(k - 2, h)

        @pl.when((s == 3) & (k < ops - 1))
        def _():
            for h in range(2):
                prepare(k + 1, h)

        @pl.when(t == n * (3 * CHUNKS + 1) + 2)
        def _():
            store(0, 1).start()
            store(1, 1).start()

        return carry

    steps = rounds * n
    lax.fori_loop(0, steps, step, 0)

    def last_grads(j, carry):
        weight_grads(ops - 1, (rounds - 1) % 2, j)
        return carry

    lax.fori_loop(0, 4, last_grads, 0)
    store(0, 0).start()
    store(1, 0).start()
    for h in range(2):
        for d in range(2):
            wait_received(d, rounds - 1, n - 1, h)
        finish_sum(rounds - 1, h)
        finish(ops - 1, h)
    for h in range(2):
        for d in range(2):
            for back in (2, 1):
                wait_sent(d, (steps - back) // n, (steps - back) % n, h)

    for a in range(7):
        mine[a : a + 1, :width] = jnp.sum(accs[a], 0, keepdims=True)
    mine[7:8, :] = jnp.zeros((1, mine.shape[1]), jnp.float32)
    for k in range(2):
        mine[8 + k : 9 + k, :hidden] = jnp.sum(bacc[k], 0, keepdims=True)
    mine[10:16, :] = jnp.zeros((6, mine.shape[1]), jnp.float32)

    def tell(q):
        return pltpu.make_async_remote_copy(
            src_ref=mine,
            dst_ref=peers.at[q - 1],
            send_sem=peer_send.at[q - 1],
            recv_sem=peer_recv.at[q - 1],
            device_id={"rep": lax.rem(r + q, n)},
            device_id_type=MESH,
        )

    for q in range(1, n):
        tell(q).start()

    def place_bins(q, bins):
        bin_out[:, pl.ds(pl.multiple_of(q * hidden, hidden), hidden)] = bins

    sums = mine[0:8, :width]
    place_bins(r, mine[8:10, :hidden])
    for q in range(1, n):
        tell(q).wait_recv()
        sums += peers[q - 1, 0:8, :width]
        place_bins(lax.rem(r - q + n, n), peers[q - 1, 8:10, :hidden])
    cent_out[...] = sums[0:1]
    gain_out[...] = sums[1:3]
    nbias_out[...] = sums[3:5]
    bout_out[...] = sums[5:7]
    for q in range(1, n):
        tell(q).wait_send()
    if inside:
        for w in range(2):
            homeward(w, 0).wait()
            for q in range(1, blocks):
                outward(w, q).wait_send()
                homeward(w, q).wait_send()
                homeward(w, q).wait_recv()
    for w in range(2):
        for k in range(2):
            store(w, k).wait()


def run_layer(inside, rows_in, gains, nbias, cent, biases, bout, wi, wo):
    n, blocks = lax.axis_size("rep"), lax.axis_size("exp")
    rows, width = rows_in[0].shape
    hidden = wi.shape[2]
    chunk = rows // CHUNKS
    half = chunk // 2
    wide = max(width, hidden)
    low, full = jnp.bfloat16, jnp.float32
    vmem = pl.BlockSpec(memory_space=pltpu.VMEM)
    anywhere = pl.BlockSpec(memory_space=pl.ANY)
    home = anywhere if inside else vmem
    row_specs = [vmem] * 2
    extra = []
    if inside:
        row_specs = [vmem] * 3 + [pl.BlockSpec(memory_space=pltpu.SMEM)]
        extra = (
            [pltpu.VMEM((rows, width), low)] * 4
            + [pltpu.VMEM((rows, rows), low)]
            + [pltpu.VMEM((rows, width), low)] * 2
            + [pltpu.SemaphoreType.DMA((2, blocks))] * 4
            + [pltpu.SemaphoreType.DMA((2,))]
        )
    flops = 2 * 16 * n * rows * width * hidden
    return pl.pallas_call(
        functools.partial(kernel, n, blocks, inside),
        out_shape=(
            jax.ShapeDtypeStruct((rows, width), low),
            jax.ShapeDtypeStruct((rows, width), low),
            jax.ShapeDtypeStruct((2, width, hidden), full),
            jax.ShapeDtypeStruct((2, hidden, width), full),
            jax.ShapeDtypeStruct((1, width), full),
            jax.ShapeDtypeStruct((2, width), full),
            jax.ShapeDtypeStruct((2, width), full),
            jax.ShapeDtypeStruct((2, n * hidden), full),
            jax.ShapeDtypeStruct((2, width), full),
        ),
        in_specs=row_specs + [vmem] * 5 + [anywhere] * 2,
        out_specs=(home, home, anywhere, anywhere, vmem, vmem, vmem, vmem, vmem),
        scratch_shapes=[
            pltpu.VMEM((CHUNKS + POOL, n, chunk, width), low),
            pltpu.VMEM((2, width, hidden), low),
            pltpu.VMEM((2, hidden, width), low),
            pltpu.VMEM((2, width, hidden), full),
            pltpu.VMEM((2, hidden, width), full),
            pltpu.VMEM((n, chunk, width), full),
            pltpu.VMEM((2, n, chunk, hidden), low),
            pltpu.VMEM((2, n, chunk, hidden), low),
            pltpu.VMEM((chunk, hidden), full),
            pltpu.VMEM((chunk, width), full),
            pltpu.VMEM((rows, width), full),
            pltpu.VMEM((rows, 128), full),
            pltpu.VMEM((2, 2, n, 2, half, width), low),
            pltpu.VMEM((2, 2, 2, half, width), low),
            pltpu.VMEM((7, 8, width), full),
            pltpu.VMEM((2, 8, hidden), full),
            pltpu.VMEM((16, wide), full),
            pltpu.VMEM((n - 1, 16, wide), full),
            pltpu.SemaphoreType.DMA((2, 2, 2)),
            pltpu.SemaphoreType.DMA((2, 2, n, 2)),
            pltpu.SemaphoreType.DMA((2,)),
            pltpu.SemaphoreType.DMA((2, 2)),
            pltpu.SemaphoreType.DMA((n - 1,)),
            pltpu.SemaphoreType.DMA((n - 1,)),
        ]
        + extra,
        compiler_params=pltpu.CompilerParams(
            collective_id=0, has_side_effects=True, vmem_limit_bytes=VMEM_BYTES
        ),
        cost_estimate=pl.CostEstimate(
            flops=flops, bytes_accessed=40 * rows * width, transcendentals=8 * rows * hidden * n
        ),
    )(*rows_in, gains, nbias, cent, biases, bout, wi, wo)


def close_kernel(device_count, cap, *refs):
    tok_hbm, cot_hbm, routes_ref, lengths_ref, y_hbm, dv_hbm, gwi_in, gwo_in = refs[:8]
    small_in, refs = refs[8:13], refs[13:]
    mixed_ref, grad_ref, gwi_out, gwo_out = refs[:4]
    small_out, refs = refs[4:9], refs[9:]
    tok, cot, y, dv, hold_wi, hold_wo, load_sem, in_sem, out_sem = refs
    rows = tok.shape[0]
    pieces = in_sem.shape[1]
    moves = []
    for w, (src, hold, dst) in enumerate(
        ((gwi_in, hold_wi, gwi_out), (gwo_in, hold_wo, gwo_out))
    ):
        depth = src.shape[1] * 2 // pieces
        for j in range(pieces):
            at = (j * 2 // pieces, pl.ds(j % (pieces // 2) * depth, depth))
            moves.append(
                (
                    pltpu.make_async_copy(src.at[at], hold.at[at], in_sem.at[w, j]),
                    pltpu.make_async_copy(hold.at[at], dst.at[at], out_sem.at[w, j]),
                )
            )
    loads = [
        pltpu.make_async_copy(src, dst, load_sem.at[j])
        for j, (src, dst) in enumerate(((y_hbm, y), (dv_hbm, dv), (tok_hbm, tok), (cot_hbm, cot)))
    ]
    for copy in loads:
        copy.start()
    for fetch, _ in moves:
        fetch.start()
    for src, dst in zip(small_in, small_out):
        dst[...] = src[...]
    place = slot_rows(routes_ref[...], rows // cap, cap)
    device = lax.axis_index("rep") * lax.axis_size("exp") + lax.axis_index("exp")
    live = live_rows(lengths_ref, device, device_count, rows)
    for copy in loads:
        copy.wait()
    for fetch, give in moves[:pieces]:
        fetch.wait()
        give.start()
    mixed_ref[...] = (tok[...].astype(jnp.float32) + live * contract_rows(place, y[...])).astype(
        jnp.bfloat16
    )
    for fetch, give in moves[pieces:]:
        fetch.wait()
        give.start()
    grad_ref[...] = (cot[...].astype(jnp.float32) + contract_rows(place, dv[...])).astype(
        jnp.bfloat16
    )
    for _, give in moves:
        give.wait()


def close(tokens, cotangent, routes, lengths, home_y, home_dv, gwi, gwo, *small):
    n, blocks = lax.axis_size("rep"), lax.axis_size("exp")
    rows, width = tokens.shape
    vmem = pl.BlockSpec(memory_space=pltpu.VMEM)
    anywhere = pl.BlockSpec(memory_space=pl.ANY)
    rows_shape = jax.ShapeDtypeStruct(tokens.shape, tokens.dtype)
    like = lambda a: jax.ShapeDtypeStruct(a.shape, a.dtype)
    return pl.pallas_call(
        functools.partial(close_kernel, n * blocks, rows // blocks),
        out_shape=(rows_shape, rows_shape, like(gwi), like(gwo), *map(like, small)),
        in_specs=[anywhere, anywhere, vmem, pl.BlockSpec(memory_space=pltpu.SMEM)]
        + [anywhere] * 4
        + [vmem] * 5,
        out_specs=[vmem, vmem, anywhere, anywhere] + [vmem] * 5,
        scratch_shapes=[pltpu.VMEM((rows, width), tokens.dtype)] * 4
        + [pltpu.VMEM(gwi.shape, gwi.dtype), pltpu.VMEM(gwo.shape, gwo.dtype)]
        + [pltpu.SemaphoreType.DMA((4,))]
        + [pltpu.SemaphoreType.DMA((2, 8))] * 2,
        compiler_params=pltpu.CompilerParams(vmem_limit_bytes=VMEM_BYTES),
    )(tokens, cotangent, routes, lengths, home_y, home_dv, gwi, gwo, *small)


def shards(
    tokens,
    routes,
    lengths,
    centroids,
    norm_gains,
    norm_biases,
    w_in,
    in_biases,
    w_out,
    out_biases,
    cotangent,
):
    n_exp = lax.axis_size("exp")
    tok_rows = tokens.shape[0]
    cap = tok_rows // n_exp
    params = (
        norm_gains[0],
        norm_biases[0],
        centroids,
        in_biases[0],
        out_biases[0],
        w_in[0],
        w_out[0],
    )
    if cap % 16 == 0 and n_exp % (2 * CHUNKS) == 0:
        row_routes = routes.reshape(1, tok_rows)
        results = run_layer(True, (tokens, cotangent, row_routes, lengths), *params)
        results = close(tokens, cotangent, row_routes, lengths, *results)
    else:
        device = lax.axis_index(("rep", "exp"))
        slot = tok_rows * n_exp * lax.axis_size("rep") // lengths.shape[0]
        positions = device * tok_rows + lax.iota(jnp.int32, tok_rows)
        seq_ids = positions // slot
        seq_table = lax.iota(jnp.int32, lengths.shape[0])
        seq_len = jnp.sum(
            jnp.where(seq_ids[:, None] == seq_table[None, :], lengths[None, :], 0), 1
        )
        live = (positions % slot < seq_len).astype(jnp.float32)[:, None]
        route = routes[:, 0]
        hits = (route[:, None] == lax.iota(jnp.int32, n_exp)[None, :]).astype(jnp.int32)
        before = jnp.cumsum(hits, 0) - hits
        target = route * cap + jnp.sum(before * hits, 1)
        place = (lax.iota(jnp.int32, tok_rows)[:, None] == target[None, :]).astype(jnp.bfloat16)
        grad_out = (live * cotangent.astype(jnp.float32)).astype(jnp.bfloat16)

        def send(rows):
            ordered = jnp.dot(place, rows, preferred_element_type=jnp.float32).astype(jnp.bfloat16)
            return lax.all_to_all(ordered, "exp", split_axis=0, concat_axis=0, tiled=True)

        def give_back(rows):
            back = lax.all_to_all(rows, "exp", split_axis=0, concat_axis=0, tiled=True)
            return contract_rows(place, back)

        result, grad_local, *rest = run_layer(False, (send(tokens), send(grad_out)), *params)
        mixed = (tokens.astype(jnp.float32) + live * give_back(result)).astype(jnp.bfloat16)
        tokens_grad = (cotangent.astype(jnp.float32) + give_back(grad_local)).astype(jnp.bfloat16)
        results = (mixed, tokens_grad, *rest)
    mixed, tokens_grad, gwi, gwo, cent_grad, gain_grad, nbias_grad, bin_grad, bout_grad = results
    return (
        mixed,
        tokens_grad,
        cent_grad,
        gain_grad[None],
        nbias_grad[None],
        gwi[None],
        bin_grad[None],
        gwo[None],
        bout_grad[None],
    )


def solution(mesh):
    placed = (
        P(("rep", "exp"), None),
        P(("rep", "exp"), None),
        P(),
        P("exp", None),
        P("exp", None, None),
        P("exp", None, None),
        P("exp", None, None, "rep"),
        P("exp", None, None),
        P("exp", None, "rep", None),
        P("exp", None, None),
        P(("rep", "exp"), None),
    )
    return jax.shard_map(
        shards,
        mesh=mesh,
        in_specs=placed,
        out_specs=(
            P(("rep", "exp"), None),
            P(("rep", "exp"), None),
            P("exp", None),
            P("exp", None, None),
            P("exp", None, None),
            P("exp", None, None, "rep"),
            P("exp", None, None),
            P("exp", None, "rep", None),
            P("exp", None, None),
        ),
        check_vma=False,
    )
```

```python
import functools

import jax
import jax.numpy as jnp
from jax import lax
from jax.experimental import pallas as pl
from jax.experimental.pallas import tpu as pltpu
from jax.sharding import PartitionSpec as P

eps = 1e-05
VMEM_BYTES = 42 * 1024 * 1024


def contract_rows(left, right):
    return lax.dot_general(
        left, right, (((0,), (0,)), ((), ())), preferred_element_type=jnp.float32
    )


def contract_cols(left, right):
    return lax.dot_general(
        left, right, (((1,), (1,)), ((), ())), preferred_element_type=jnp.float32
    )


MESH = pl.DeviceIdType.MESH
CHUNKS = 4
POOL = 4
ROOT = 0.7978845608028654
CUBE = 0.044715


def layer_stats(values):
    center = values - jnp.mean(values, -1, keepdims=True)
    spread = jnp.mean(center * center, -1, keepdims=True)
    scale = lax.rsqrt(spread + eps)
    return center * scale, scale


def gelu_and_slope(inner):
    square = inner * inner
    bent = jnp.tanh(inner * (ROOT + (ROOT * CUBE) * square))
    half = 0.5 * (1.0 + bent)
    slope = half + (0.5 * inner) * (1.0 - bent * bent) * (ROOT + (3.0 * ROOT * CUBE) * square)
    return inner * half, slope


def fold(rows):
    return jnp.sum(rows.reshape(rows.shape[0] // 8, 8, rows.shape[1]), 0)


def order_of(blocks):
    if blocks == 1:
        return [0]
    others = [b for b in range(2, blocks, 2)] + [b for b in range(blocks - 1, 2, -2)]
    return [0] + others + [1]


def flip(index, bits):
    out, place = index, 1
    while place <= bits:
        if bits & place:
            out = out + place * (1 - 2 * lax.rem(index // place, 2))
        place *= 2
    return out


def slot_rows(routes, blocks, cap):
    rows = routes.shape[1]
    along = routes.astype(jnp.float32)
    table = lax.broadcasted_iota(jnp.int32, (max(blocks, 8), rows), 0).astype(jnp.float32)
    hits = (table == along).astype(jnp.float32)
    first = lax.broadcasted_iota(jnp.int32, (rows, rows), 0)
    second = lax.broadcasted_iota(jnp.int32, (rows, rows), 1)
    earlier = (first < second).astype(jnp.bfloat16)
    before = jnp.dot(hits.astype(jnp.bfloat16), earlier, preferred_element_type=jnp.float32)
    target = along * cap + jnp.sum(before * hits, 0, keepdims=True)
    return (first.astype(jnp.float32) == target).astype(jnp.bfloat16)


def live_rows(lengths_ref, device, devices, rows):
    slot = rows * devices // lengths_ref.shape[0]
    start = device * rows
    count = lengths_ref[start // slot] - lax.rem(start, slot)
    return (lax.broadcasted_iota(jnp.int32, (rows, 1), 0) < count).astype(jnp.float32)


def kernel(n, blocks, inside, *refs):
    refs = list(refs)
    take = lambda count: [refs.pop(0) for _ in range(count)]
    if inside:
        tok_ref, cot_hbm, routes_ref, lengths_ref = take(4)
    else:
        x_ref, dy_ref = take(2)
    gain_ref, nbias_ref, cent_ref, bias_ref, bout_ref, wi_hbm, wo_hbm = take(7)
    home_y, home_dv, gwi, gwo, cent_out, gain_out, nbias_out, bin_out, bout_out = take(9)
    gath, wi, wo, part, act, dq, slope, total, state, dlog, recv, stage = take(12)
    accs, bacc, mine, peers, mine_late, peers_late = take(6)
    send_sem, recv_sem, load_sem, peer_send, peer_recv = take(5)
    if inside:
        x_ref, dy_ref, y_ref, dv_ref, place, cot_ref = take(6)
        out_x, out_dy = y_ref, dv_ref
        out_send, out_recv, home_send, home_recv, home_own, cot_sem = take(6)
    else:
        y_ref, dv_ref = home_y, home_dv
    r = lax.axis_index("rep")
    e = lax.axis_index("exp")
    rows, width = x_ref.shape
    hidden = wi_hbm.shape[2]
    cap = rows // blocks
    order = order_of(blocks)
    per_chunk = blocks // CHUNKS
    chunk = rows // CHUNKS
    half = chunk // 2
    ops = 4 * CHUNKS
    rounds = ops + 1
    block = min(32, half)
    tile = min(512, hidden)
    wtile = hidden // 4
    last = n - 1

    def op_type(i):
        return jnp.where(i < CHUNKS, 0, jnp.where(i >= 3 * CHUNKS, 3, 1 + lax.rem(i + CHUNKS, 2)))

    def op_chunk(i):
        return jnp.where(
            i < CHUNKS, i, jnp.where(i >= 3 * CHUNKS, i - 3 * CHUNKS, (i - CHUNKS) // 2)
        )

    def op_slot(i):
        return jnp.where(i < CHUNKS, i, CHUNKS + lax.rem(i, POOL))

    def half_rows(h):
        return pl.ds(h * half, half)

    ahead = (jnp.minimum(r + 1, last), jnp.maximum(r - 1, 0))
    pos = (r, last - r)

    def item_sent(d, s):
        return lax.rem(r - s + n, n) if d == 0 else lax.rem(r + s, n)

    def sends(d, k, s):
        return (pos[d] < last) & jnp.where(s <= pos[d], k < ops, k >= 1)

    def receives(d, k, s):
        return (pos[d] > 0) & jnp.where(s <= pos[d] - 1, k < ops, k >= 1)

    def copy(d, k, s, h, src, dst):
        return pltpu.make_async_remote_copy(
            src_ref=src,
            dst_ref=dst,
            send_sem=send_sem.at[d, lax.rem(s, 2), h],
            recv_sem=recv_sem.at[d, lax.rem(k, 2), s, h],
            device_id={"rep": ahead[d]},
            device_id_type=MESH,
        )

    def landing(d, k, s, h):
        return recv.at[d, lax.rem(k, 2), s, h]

    def wait_sent(d, k, s, h):
        @pl.when(sends(d, k, s))
        def _():
            copy(d, k, s, h, stage.at[d, lax.rem(s, 2), h], landing(d, k, s, h)).wait_send()

    def wait_received(d, k, s, h):
        @pl.when(receives(d, k, s))
        def _():
            copy(d, k, s, h, stage.at[d, lax.rem(s, 2), h], landing(d, k, s, h)).wait_recv()

    def finish_sum(k, h):
        rs = half_rows(h)
        total[rs, :] = part[r, rs, :]
        for d in range(2):

            @pl.when(pos[d] > 0)
            def _():
                total[rs, :] += landing(d, k, n - 1, h)[...].astype(jnp.float32)

    def send(d, k, s, h):
        gathers = s <= pos[d]
        p = item_sent(d, s)
        rs = half_rows(h)

        @pl.when(sends(d, k, s) & gathers)
        def _():
            here = gath.at[op_slot(k), p, rs]
            copy(d, k, s, h, here, here).start()

        @pl.when(sends(d, k, s) & jnp.logical_not(gathers))
        def _():
            out = stage.at[d, lax.rem(s, 2), h]

            @pl.when(pos[d] == 0)
            def _():
                out[...] = part[p, rs, :].astype(jnp.bfloat16)

            @pl.when(pos[d] > 0)
            def _():
                came = landing(d, k, s - 1, h)[...].astype(jnp.float32)
                out[...] = (part[p, rs, :] + came).astype(jnp.bfloat16)

            copy(d, k, s, h, out, landing(d, k, s, h)).start()

    def over_blocks(h, body):
        def step(b, carry):
            body(pl.multiple_of(h * half + b * block, block))
            return carry

        lax.fori_loop(0, half // block, step, 0)

    def cap_rows(q):
        return pl.ds(pl.multiple_of(q * cap, cap), cap)

    def outward(w, q):
        src, dst = ((out_x, x_ref), (out_dy, dy_ref))[w]
        return pltpu.make_async_remote_copy(
            src_ref=src.at[cap_rows(q)],
            dst_ref=dst.at[cap_rows(q)],
            send_sem=out_send.at[w, q],
            recv_sem=out_recv.at[w, q],
            device_id={"exp": flip(e, order[q])},
            device_id_type=MESH,
        )

    def homeward(w, q):
        src, dst = ((y_ref, home_y), (dv_ref, home_dv))[w]
        if q == 0:
            return pltpu.make_async_copy(
                src.at[cap_rows(q)], dst.at[cap_rows(e)], home_own.at[w]
            )
        return pltpu.make_async_remote_copy(
            src_ref=src.at[cap_rows(q)],
            dst_ref=dst.at[cap_rows(e)],
            send_sem=home_send.at[w, q],
            recv_sem=home_recv.at[w, q],
            device_id={"exp": flip(e, order[q])},
            device_id_type=MESH,
        )

    def dispatch(w, first, stop):
        values = (tok_ref, cot_ref)[w][...]
        if w == 1:
            device = r * blocks + e
            live = live_rows(lengths_ref, device, n * blocks, rows)
            values = (live * values.astype(jnp.float32)).astype(jnp.bfloat16)
        for q in range(first, stop):
            picked = place[cap_rows(flip(e, order[q])), :]
            ordered = jnp.dot(picked, values, preferred_element_type=jnp.float32)
            target = ((x_ref, dy_ref) if q == 0 else (out_x, out_dy))[w]
            target[cap_rows(q), :] = ordered.astype(jnp.bfloat16)
            if q > 0:
                if w == 0 and q == 1:
                    pl.semaphore_wait(barrier, n - 1 + blocks - 1)
                outward(w, q).start()

    def each_block(c, h, body):
        for chunk_at in range(CHUNKS):

            @pl.when(c == chunk_at)
            def _():
                for q in range(
                    chunk_at * per_chunk + h * (per_chunk // 2),
                    chunk_at * per_chunk + (h + 1) * (per_chunk // 2),
                ):
                    body(q)

    def arrived(w, c, h):
        if inside:
            each_block(c, h, lambda q: outward(w, q).wait_recv() if q > 0 else None)

    def go_home(w, c, h):
        if inside:
            each_block(c, h, lambda q: homeward(w, q).start())

    def gate_of(x):
        return jax.nn.sigmoid(jnp.sum(x * cent_ref[...], -1, keepdims=True))

    def prepare(i, h):
        kind, c, slot = op_type(i), op_chunk(i), op_slot(i)

        def own(offset, value):
            gath[slot, r, pl.ds(offset, block), :] = value.astype(jnp.bfloat16)

        def source(offset):
            return pl.ds(pl.multiple_of(c * chunk + offset, block), block)

        @pl.when(kind == 0)
        def _():
            arrived(0, c, h)
            over_blocks(
                h,
                lambda o: own(
                    o,
                    layer_stats(x_ref[source(o), :].astype(jnp.float32))[0] * gain_ref[0:1, :]
                    + nbias_ref[0:1, :],
                )
            )

        @pl.when(kind == 1)
        def _():
            over_blocks(
                h,
                lambda o: own(
                    o, layer_stats(state[source(o), :])[0] * gain_ref[1:2, :] + nbias_ref[1:2, :]
                )
            )

        @pl.when(kind == 2)
        def _():
            arrived(1, c, h)
            over_blocks(
                h,
                lambda o: own(
                    o,
                    gate_of(x_ref[source(o), :].astype(jnp.float32))
                    * dy_ref[source(o), :].astype(jnp.float32),
                )
            )

        @pl.when(kind == 3)
        def _():
            over_blocks(h, lambda o: own(o, state[source(o), :]))

    def norm_back(values, grad, k):
        unit, scale = layer_stats(values)
        accs[1 + k] += fold(grad * unit)
        accs[3 + k] += fold(grad)
        through = grad * gain_ref[k : k + 1, :]
        return scale * (
            through
            - jnp.mean(through, -1, keepdims=True)
            - unit * jnp.mean(through * unit, -1, keepdims=True)
        )

    def finish(i, h):
        kind, c = op_type(i), op_chunk(i)

        def source(offset):
            return pl.ds(pl.multiple_of(c * chunk + offset, block), block)

        @pl.when(kind == 0)
        def _():
            def body(o):
                state[source(o), :] = (
                    x_ref[source(o), :].astype(jnp.float32)
                    + total[pl.ds(o, block), :]
                    + bout_ref[0:1, :]
                )

            over_blocks(h, body)

        @pl.when(kind == 1)
        def _():
            def body(o):
                x = x_ref[source(o), :].astype(jnp.float32)
                dy = dy_ref[source(o), :].astype(jnp.float32)
                upper = state[source(o), :] + total[pl.ds(o, block), :] + bout_ref[1:2, :]
                gate = gate_of(x)
                y_ref[source(o), :] = (gate * upper).astype(jnp.bfloat16)
                logit = jnp.sum(dy * upper, -1, keepdims=True) * gate * (1.0 - gate)
                dlog[source(o), :] = jnp.broadcast_to(logit, (block, dlog.shape[1]))
                accs[0] += fold(logit * x)

            over_blocks(h, body)
            go_home(0, c, h)

        @pl.when(kind == 2)
        def _():
            def body(o):
                x = x_ref[source(o), :].astype(jnp.float32)
                top = gate_of(x) * dy_ref[source(o), :].astype(jnp.float32)
                middle = top + norm_back(state[source(o), :], total[pl.ds(o, block), :], 1)
                state[source(o), :] = middle
                accs[5] += fold(middle)
                accs[6] += fold(top)

            over_blocks(h, body)

        @pl.when(kind == 3)
        def _():
            def body(o):
                x = x_ref[source(o), :].astype(jnp.float32)
                dv_ref[source(o), :] = (
                    state[source(o), :]
                    + norm_back(x, total[pl.ds(o, block), :], 0)
                    + dlog[source(o), 0:1] * cent_ref[...]
                ).astype(jnp.bfloat16)

            over_blocks(h, body)
            go_home(1, c, h)

    def over_tiles(count, size, body):
        def step(j, carry):
            body(pl.ds(pl.multiple_of(j * size, size), size))
            return carry

        lax.fori_loop(0, count, step, 0)

    def item_first(i, par, p):
        kind = op_type(i)
        k = jnp.where((kind == 1) | (kind == 2), 1, 0)
        slot = jnp.where(
            kind == 2, op_slot(i - 1), jnp.where(kind == 3, op_chunk(i), op_slot(i))
        )

        def body(cs):
            inner = (
                jnp.dot(gath[slot, p], wi[k, :, cs], preferred_element_type=jnp.float32)
                + bias_ref[pl.ds(k, 1), pl.ds(pl.multiple_of(r * hidden + cs.start, tile), tile)]
            )
            low, pull = gelu_and_slope(inner)
            act[par, p, :, cs] = low.astype(jnp.bfloat16)
            slope[:, cs] = pull

        over_tiles(hidden // tile, tile, body)

    def item_second(i, par, p):
        kind = op_type(i)
        k = jnp.where((kind == 1) | (kind == 2), 1, 0)

        @pl.when(kind < 2)
        def _():
            def body(cs):
                part[p, :, cs] = jnp.dot(
                    act[par, p], wo[k, :, cs], preferred_element_type=jnp.float32
                )

            over_tiles(width // tile, tile, body)

        @pl.when(kind >= 2)
        def _():
            slot = op_slot(i)

            def pull(cs):
                grad = contract_cols(gath[slot, p], wo[k, cs, :]) * slope[:, cs]
                bacc[k, :, cs] += fold(grad)
                dq[par, p, :, cs] = grad.astype(jnp.bfloat16)

            over_tiles(hidden // tile, tile, pull)

            def push(cs):
                part[p, :, cs] = contract_cols(dq[par, p], wi[k, cs, :])

            over_tiles(width // tile, tile, push)

    def weight_grads(i, par, j):
        kind = op_type(i)
        k = jnp.where(kind == 2, 1, 0)
        slot = jnp.where(kind == 2, op_slot(i - 1), op_chunk(i))
        cs = pl.ds(pl.multiple_of(j * wtile, wtile), wtile)
        depth = n * chunk
        normed = gath[slot, :, :, cs].reshape(depth, wtile)
        gwi[k, cs, :] += contract_rows(normed, dq[par].reshape(depth, hidden))
        active = act[par, :, :, cs].reshape(depth, wtile)
        gwo[k, cs, :] += contract_rows(active, gath[op_slot(i)].reshape(depth, width))

    def item_at(s):
        near = jnp.minimum(r, last - r)
        base = jnp.where(near == 0, last - s, jnp.where(s < 2, last - s, s - 2))
        return jnp.where(r < 2, base, last - base)

    def cot_load():
        return pltpu.make_async_copy(cot_hbm, cot_ref, cot_sem)

    EARLY, LATE = (0, 2, 4, 5, 6), (1, 3)

    def tell(late, q):
        src, dst = ((mine, peers), (mine_late, peers_late))[late]
        return pltpu.make_async_remote_copy(
            src_ref=src,
            dst_ref=dst.at[q - 1],
            send_sem=peer_send.at[late, q - 1],
            recv_sem=peer_recv.at[late, q - 1],
            device_id={"rep": lax.rem(r + q, n)},
            device_id_type=MESH,
        )

    def tell_early():
        for a, row in enumerate(EARLY):
            mine[a : a + 1, :width] = jnp.sum(accs[row], 0, keepdims=True)
        mine[5:6, :hidden] = jnp.sum(bacc[1], 0, keepdims=True)
        mine[6:8, :] = jnp.zeros((2, mine.shape[1]), jnp.float32)
        for q in range(1, n):
            tell(0, q).start()

    def tell_late():
        at = 0
        for values in (accs[LATE[0]], accs[LATE[1]], bacc[0]):
            flat = jnp.sum(values, 0, keepdims=True)
            for j in range(flat.shape[1] // 128):
                mine_late[at : at + 1, :] = flat[:, j * 128 : (j + 1) * 128]
                at += 1
        for q in range(1, n):
            tell(1, q).start()

    def unpack(packed, at, size):
        return jnp.concatenate([packed[at + j : at + j + 1] for j in range(size // 128)], 1)

    def load(w):
        src, dst = ((wi_hbm, wi), (wo_hbm, wo))[w]
        return pltpu.make_async_copy(src, dst, load_sem.at[w])

    barrier = pltpu.get_barrier_semaphore()
    for q in range(1, n):
        pl.semaphore_signal(
            barrier, inc=1, device_id={"rep": lax.rem(r + q, n)}, device_id_type=MESH
        )
    load(0).start()
    load(1).start()
    if inside:
        for b in range(1, blocks):
            pl.semaphore_signal(
                barrier, inc=1, device_id={"exp": flip(e, b)}, device_id_type=MESH
            )
        cot_load().start()
        place[...] = slot_rows(routes_ref[...], blocks, cap)
        dispatch(0, 0, 2)
    else:
        pl.semaphore_wait(barrier, n - 1)
    prepare(0, 0)

    def step(t, carry):
        k, s = t // n, lax.rem(t, n)
        k_before, s_before = (t - 1) // n, lax.rem(t + n - 1, n)
        i = k - 1
        par = lax.rem(k, 2)
        p = item_at(s)

        def exchange(h):
            for d in range(2):

                @pl.when(t >= 1)
                def _():
                    wait_received(d, k_before, s_before, h)

                @pl.when(t >= 2)
                def _():
                    wait_sent(d, (t - 2) // n, lax.rem(t + n - 2, n), h)

            @pl.when((s == 0) & (k >= 2))
            def _():
                finish_sum(k - 1, h)

            for d in range(2):
                send(d, k, s, h)

        def grads(j):
            old = k - 2

            @pl.when((s < 2) & (old >= CHUNKS) & (op_type(old) >= 2))
            def _():
                weight_grads(old, lax.rem(k + 1, 2), j)

        exchange(0)

        @pl.when(t == n * ops)
        def _():
            tell_early()

        @pl.when(t == 0)
        def _():
            if inside:
                dispatch(0, 2, blocks)
            prepare(0, 1)

        @pl.when(t == 1)
        def _():
            def clear(b, carry):
                zero_rows = pl.ds(pl.multiple_of(b * 64, 64), 64)
                for w in range(2):
                    gwi[w, zero_rows, :] = jnp.zeros((64, hidden), jnp.float32)
                    gwo[w, zero_rows, :] = jnp.zeros((64, width), jnp.float32)
                return carry

            lax.fori_loop(0, width // 64, clear, 0)
            accs[...] = jnp.zeros_like(accs)
            bacc[...] = jnp.zeros_like(bacc)

        if inside:

            @pl.when(t == 2)
            def _():
                cot_load().wait()
                dispatch(1, 0, blocks)

            @pl.when(t == n * CHUNKS)
            def _():
                for w in range(2):
                    for q in range(1, blocks):
                        outward(w, q).wait_send()

        @pl.when(t == n)
        def _():
            load(0).wait()
            load(1).wait()

        @pl.when(k >= 1)
        def _():
            item_first(i, par, p)

        grads(2 * s)
        exchange(1)

        @pl.when(k >= 1)
        def _():
            item_second(i, par, p)

        grads(2 * s + 1)

        @pl.when((s == 2) & (k >= 2))
        def _():
            for h in range(2):
                finish(k - 2, h)

        @pl.when((s == 3) & (k < ops - 1))
        def _():
            for h in range(2):
                prepare(k + 1, h)

        return carry

    steps = rounds * n
    lax.fori_loop(0, steps, step, 0)

    def last_grads(j, carry):
        weight_grads(ops - 1, (rounds - 1) % 2, j)
        return carry

    lax.fori_loop(0, 4, last_grads, 0)
    for h in range(2):
        for d in range(2):
            wait_received(d, rounds - 1, n - 1, h)
        finish_sum(rounds - 1, h)
        finish(ops - 1, h)
    for h in range(2):
        for d in range(2):
            for back in (2, 1):
                wait_sent(d, (steps - back) // n, (steps - back) % n, h)

    tell_late()

    def place_bins(k, q, bins):
        bin_out[k : k + 1, pl.ds(pl.multiple_of(q * hidden, hidden), hidden)] = bins

    for q in range(1, n):
        tell(0, q).wait_recv()
    sums = mine[0:5, :width]
    place_bins(1, r, mine[5:6, :hidden])
    for q in range(1, n):
        sums += peers[q - 1, 0:5, :width]
        place_bins(1, lax.rem(r - q + n, n), peers[q - 1, 5:6, :hidden])
    cent_out[...] = sums[0:1]
    gain_out[1:2, :] = sums[1:2]
    nbias_out[1:2, :] = sums[2:3]
    bout_out[...] = sums[3:5]
    for q in range(1, n):
        tell(1, q).wait_recv()
    mine_rows = mine_late[...]
    late = mine_rows[: 2 * width // 128]
    place_bins(0, r, unpack(mine_rows, 2 * width // 128, hidden))
    for q in range(1, n):
        theirs = peers_late[q - 1]
        late += theirs[: 2 * width // 128]
        place_bins(0, lax.rem(r - q + n, n), unpack(theirs, 2 * width // 128, hidden))
    gain_out[0:1, :] = unpack(late, 0, width)
    nbias_out[0:1, :] = unpack(late, width // 128, width)
    for q in range(1, n):
        tell(0, q).wait_send()
        tell(1, q).wait_send()
    if inside:
        for w in range(2):
            homeward(w, 0).wait()
            for q in range(1, blocks):
                homeward(w, q).wait_send()
                homeward(w, q).wait_recv()


def run_layer(inside, rows_in, gains, nbias, cent, biases, bout, wi, wo):
    n, blocks = lax.axis_size("rep"), lax.axis_size("exp")
    rows, width = rows_in[0].shape
    hidden = wi.shape[2]
    chunk = rows // CHUNKS
    half = chunk // 2
    wide = max(width, hidden)
    late = (2 * width + hidden) // 128
    low, full = jnp.bfloat16, jnp.float32
    vmem = pl.BlockSpec(memory_space=pltpu.VMEM)
    anywhere = pl.BlockSpec(memory_space=pl.ANY)
    row_specs = [vmem] * 2
    extra = []
    if inside:
        row_specs = [vmem, anywhere, vmem, pl.BlockSpec(memory_space=pltpu.SMEM)]
        extra = (
            [pltpu.VMEM((rows, width), low)] * 4
            + [pltpu.VMEM((rows, rows), low)]
            + [pltpu.VMEM((rows, width), low)]
            + [pltpu.SemaphoreType.DMA((2, blocks))] * 4
            + [pltpu.SemaphoreType.DMA((2,)), pltpu.SemaphoreType.DMA]
        )
    flops = 2 * 16 * n * rows * width * hidden
    return pl.pallas_call(
        functools.partial(kernel, n, blocks, inside),
        out_shape=(
            pltpu.VMEM((rows, width), low) if inside else jax.ShapeDtypeStruct((rows, width), low),
            pltpu.VMEM((rows, width), low) if inside else jax.ShapeDtypeStruct((rows, width), low),
            pltpu.VMEM((2, width, hidden), full),
            pltpu.VMEM((2, hidden, width), full),
            jax.ShapeDtypeStruct((1, width), full),
            jax.ShapeDtypeStruct((2, width), full),
            jax.ShapeDtypeStruct((2, width), full),
            jax.ShapeDtypeStruct((2, n * hidden), full),
            jax.ShapeDtypeStruct((2, width), full),
        ),
        in_specs=row_specs + [vmem] * 5 + [anywhere] * 2,
        out_specs=(vmem, vmem, vmem, vmem, vmem, vmem, vmem, vmem, vmem),
        scratch_shapes=[
            pltpu.VMEM((CHUNKS + POOL, n, chunk, width), low),
            pltpu.VMEM((2, width, hidden), low),
            pltpu.VMEM((2, hidden, width), low),
            pltpu.VMEM((n, chunk, width), full),
            pltpu.VMEM((2, n, chunk, hidden), low),
            pltpu.VMEM((2, n, chunk, hidden), low),
            pltpu.VMEM((chunk, hidden), full),
            pltpu.VMEM((chunk, width), full),
            pltpu.VMEM((rows, width), full),
            pltpu.VMEM((rows, 128), full),
            pltpu.VMEM((2, 2, n, 2, half, width), low),
            pltpu.VMEM((2, 2, 2, half, width), low),
            pltpu.VMEM((7, 8, width), full),
            pltpu.VMEM((2, 8, hidden), full),
            pltpu.VMEM((8, wide), full),
            pltpu.VMEM((n - 1, 8, wide), full),
            pltpu.VMEM((late, 128), full),
            pltpu.VMEM((n - 1, late, 128), full),
            pltpu.SemaphoreType.DMA((2, 2, 2)),
            pltpu.SemaphoreType.DMA((2, 2, n, 2)),
            pltpu.SemaphoreType.DMA((2,)),
            pltpu.SemaphoreType.DMA((2, n - 1)),
            pltpu.SemaphoreType.DMA((2, n - 1)),
        ]
        + extra,
        compiler_params=pltpu.CompilerParams(
            collective_id=0, has_side_effects=True, vmem_limit_bytes=VMEM_BYTES
        ),
        cost_estimate=pl.CostEstimate(
            flops=flops, bytes_accessed=40 * rows * width, transcendentals=8 * rows * hidden * n
        ),
    )(*rows_in, gains, nbias, cent, biases, bout, wi, wo)


def close_kernel(device_count, cap, *refs):
    tok_hbm, cot_hbm, routes_ref, lengths_ref, y, dv, gwi_in, gwo_in = refs[:8]
    small_in, refs = refs[8:13], refs[13:]
    mixed_ref, grad_ref, gwi_out, gwo_out = refs[:4]
    small_out, refs = refs[4:9], refs[9:]
    tok, cot, load_sem, move_sem = refs
    rows = tok.shape[0]
    loads = [
        pltpu.make_async_copy(src, dst, load_sem.at[j])
        for j, (src, dst) in enumerate(((tok_hbm, tok), (cot_hbm, cot)))
    ]
    moves = [
        pltpu.make_async_copy(src.at[k], dst.at[k], move_sem.at[w, k])
        for w, (src, dst) in enumerate(((gwi_in, gwi_out), (gwo_in, gwo_out)))
        for k in range(2)
    ]
    for copy in loads + moves:
        copy.start()
    for src, dst in zip(small_in, small_out):
        dst[...] = src[...]
    place = slot_rows(routes_ref[...], rows // cap, cap)
    device = lax.axis_index("rep") * lax.axis_size("exp") + lax.axis_index("exp")
    live = live_rows(lengths_ref, device, device_count, rows)
    for copy in loads:
        copy.wait()
    mixed_ref[...] = (tok[...].astype(jnp.float32) + live * contract_rows(place, y[...])).astype(
        jnp.bfloat16
    )
    grad_ref[...] = (cot[...].astype(jnp.float32) + contract_rows(place, dv[...])).astype(
        jnp.bfloat16
    )
    for copy in moves:
        copy.wait()


def close(tokens, cotangent, routes, lengths, home_y, home_dv, gwi, gwo, *small):
    n, blocks = lax.axis_size("rep"), lax.axis_size("exp")
    rows, width = tokens.shape
    vmem = pl.BlockSpec(memory_space=pltpu.VMEM)
    anywhere = pl.BlockSpec(memory_space=pl.ANY)
    rows_shape = jax.ShapeDtypeStruct(tokens.shape, tokens.dtype)
    like = lambda a: jax.ShapeDtypeStruct(a.shape, a.dtype)
    home_y, home_dv, gwi, gwo = (
        pltpu.with_memory_space_constraint(a, pltpu.VMEM) for a in (home_y, home_dv, gwi, gwo)
    )
    return pl.pallas_call(
        functools.partial(close_kernel, n * blocks, rows // blocks),
        out_shape=(rows_shape, rows_shape, like(gwi), like(gwo), *map(like, small)),
        in_specs=[anywhere, anywhere, vmem, pl.BlockSpec(memory_space=pltpu.SMEM)]
        + [vmem] * 9,
        out_specs=[vmem, vmem, anywhere, anywhere] + [vmem] * 5,
        scratch_shapes=[pltpu.VMEM((rows, width), tokens.dtype)] * 2
        + [pltpu.SemaphoreType.DMA((2,)), pltpu.SemaphoreType.DMA((2, 2))],
        compiler_params=pltpu.CompilerParams(vmem_limit_bytes=VMEM_BYTES),
    )(tokens, cotangent, routes, lengths, home_y, home_dv, gwi, gwo, *small)


def shards(
    tokens,
    routes,
    lengths,
    centroids,
    norm_gains,
    norm_biases,
    w_in,
    in_biases,
    w_out,
    out_biases,
    cotangent,
):
    n_exp = lax.axis_size("exp")
    tok_rows = tokens.shape[0]
    cap = tok_rows // n_exp
    params = (
        norm_gains[0],
        norm_biases[0],
        centroids,
        in_biases[0],
        out_biases[0],
        w_in[0],
        w_out[0],
    )
    if cap % 16 == 0 and n_exp % (2 * CHUNKS) == 0:
        row_routes = routes.reshape(1, tok_rows)
        results = run_layer(True, (tokens, cotangent, row_routes, lengths), *params)
        results = close(tokens, cotangent, row_routes, lengths, *results)
    else:
        device = lax.axis_index(("rep", "exp"))
        slot = tok_rows * n_exp * lax.axis_size("rep") // lengths.shape[0]
        positions = device * tok_rows + lax.iota(jnp.int32, tok_rows)
        seq_ids = positions // slot
        seq_table = lax.iota(jnp.int32, lengths.shape[0])
        seq_len = jnp.sum(
            jnp.where(seq_ids[:, None] == seq_table[None, :], lengths[None, :], 0), 1
        )
        live = (positions % slot < seq_len).astype(jnp.float32)[:, None]
        route = routes[:, 0]
        hits = (route[:, None] == lax.iota(jnp.int32, n_exp)[None, :]).astype(jnp.int32)
        before = jnp.cumsum(hits, 0) - hits
        target = route * cap + jnp.sum(before * hits, 1)
        place = (lax.iota(jnp.int32, tok_rows)[:, None] == target[None, :]).astype(jnp.bfloat16)
        grad_out = (live * cotangent.astype(jnp.float32)).astype(jnp.bfloat16)

        def send(rows):
            ordered = jnp.dot(place, rows, preferred_element_type=jnp.float32).astype(jnp.bfloat16)
            return lax.all_to_all(ordered, "exp", split_axis=0, concat_axis=0, tiled=True)

        def give_back(rows):
            back = lax.all_to_all(rows, "exp", split_axis=0, concat_axis=0, tiled=True)
            return contract_rows(place, back)

        result, grad_local, *rest = run_layer(False, (send(tokens), send(grad_out)), *params)
        mixed = (tokens.astype(jnp.float32) + live * give_back(result)).astype(jnp.bfloat16)
        tokens_grad = (cotangent.astype(jnp.float32) + give_back(grad_local)).astype(jnp.bfloat16)
        results = (mixed, tokens_grad, *rest)
    mixed, tokens_grad, gwi, gwo, cent_grad, gain_grad, nbias_grad, bin_grad, bout_grad = results
    return (
        mixed,
        tokens_grad,
        cent_grad,
        gain_grad[None],
        nbias_grad[None],
        gwi[None],
        bin_grad[None],
        gwo[None],
        bout_grad[None],
    )


def solution(mesh):
    placed = (
        P(("rep", "exp"), None),
        P(("rep", "exp"), None),
        P(),
        P("exp", None),
        P("exp", None, None),
        P("exp", None, None),
        P("exp", None, None, "rep"),
        P("exp", None, None),
        P("exp", None, "rep", None),
        P("exp", None, None),
        P(("rep", "exp"), None),
    )
    return jax.shard_map(
        shards,
        mesh=mesh,
        in_specs=placed,
        out_specs=(
            P(("rep", "exp"), None),
            P(("rep", "exp"), None),
            P("exp", None),
            P("exp", None, None),
            P("exp", None, None),
            P("exp", None, None, "rep"),
            P("exp", None, None),
            P("exp", None, "rep", None),
            P("exp", None, None),
        ),
        check_vma=False,
    )
```

```python
import functools

import jax
import jax.numpy as jnp
from jax import lax
from jax.experimental import pallas as pl
from jax.experimental.pallas import tpu as pltpu
from jax.sharding import PartitionSpec as P

eps = 1e-05
VMEM_BYTES = 44 * 1024 * 1024


def contract_rows(left, right):
    return lax.dot_general(
        left, right, (((0,), (0,)), ((), ())), preferred_element_type=jnp.float32
    )


def contract_cols(left, right):
    return lax.dot_general(
        left, right, (((1,), (1,)), ((), ())), preferred_element_type=jnp.float32
    )


MESH = pl.DeviceIdType.MESH
POOL = 4
PLANS = {448: (48, 32, 32), 512: (64, 64)}
SPARE = 16
ORDER = (0, 2, 4, 6, 5, 7, 3, 1)
ROOT = 0.7978845608028654
CUBE = 0.044715


def layer_stats(values):
    center = values - jnp.mean(values, -1, keepdims=True)
    spread = jnp.mean(center * center, -1, keepdims=True)
    scale = lax.rsqrt(spread + eps)
    return center * scale, scale


def gelu_and_slope(inner):
    square = inner * inner
    bent = jnp.tanh(inner * (ROOT + (ROOT * CUBE) * square))
    half = 0.5 * (1.0 + bent)
    slope = half + (0.5 * inner) * (1.0 - bent * bent) * (ROOT + (3.0 * ROOT * CUBE) * square)
    return inner * half, slope


def fold(rows):
    return jnp.sum(rows.reshape(rows.shape[0] // 8, 8, rows.shape[1]), 0)


def pair_of(b):
    return (b >> 2) * 2 + (b & 1)


def flip(index, bits):
    out, place = index, 1
    while place <= bits:
        if bits & place:
            out = out + place * (1 - 2 * lax.rem(index // place, 2))
        place *= 2
    return out


def slot_rows(routes, blocks, cap):
    rows = routes.shape[1]
    along = routes.astype(jnp.float32)
    table = lax.broadcasted_iota(jnp.int32, (max(blocks, 8), rows), 0).astype(jnp.float32)
    hits = (table == along).astype(jnp.float32)
    first = lax.broadcasted_iota(jnp.int32, (rows, rows), 0)
    second = lax.broadcasted_iota(jnp.int32, (rows, rows), 1)
    earlier = (first < second).astype(jnp.bfloat16)
    before = jnp.dot(hits.astype(jnp.bfloat16), earlier, preferred_element_type=jnp.float32)
    target = along * cap + jnp.sum(before * hits, 0, keepdims=True)
    return (first.astype(jnp.float32) == target).astype(jnp.bfloat16)


def live_count(lengths_ref, device, devices, rows):
    slot = rows * devices // lengths_ref.shape[0]
    start = device * rows
    return lengths_ref[start // slot] - lax.rem(start, slot)


def live_rows(lengths_ref, device, devices, rows):
    count = live_count(lengths_ref, device, devices, rows)
    return (lax.broadcasted_iota(jnp.int32, (rows, 1), 0) < count).astype(jnp.float32)


def kernel(n, blocks, inside, parts, *refs):
    refs = list(refs)
    take = lambda count: [refs.pop(0) for _ in range(count)]
    if inside:
        tok_ref, cot_hbm, routes_ref, lengths_ref = take(4)
    else:
        x_ref, dy_ref = take(2)
    gain_ref, nbias_ref, cent_ref, bias_ref, bout_ref, wi_hbm, wo_hbm = take(7)
    home_y, home_dv, gwi, gwo, cent_out, gain_out, nbias_out, bin_out, bout_out = take(9)
    top_out = take(1)[0] if inside else None
    gath, wi, wo, part, act, dq, slope, total, state, dlog, recv, stage = take(12)
    accs, bacc, mine, peers, mine_late, peers_late = take(6)
    send_sem, recv_sem, load_sem, peer_send, peer_recv = take(5)
    if inside:
        x_ref, dy_ref, y_ref, dv_ref, place, cot_ref, part_x, part_dy, pack, seen, top = take(11)
        out_x, out_dy = y_ref, dv_ref
        out_send, out_recv, home_send, home_recv, home_own, cot_sem = take(6)
        seen_send, seen_recv = take(2)
    else:
        y_ref, dv_ref = home_y, home_dv
    r = lax.axis_index("rep")
    e = lax.axis_index("exp")
    own_rows, width = x_ref.shape
    hidden = wi_hbm.shape[2]
    rows = home_y.shape[0]
    cap = rows // blocks
    chunk = sum(parts)
    CHUNKS = own_rows // chunk
    starts = [sum(parts[:h]) for h in range(len(parts))]
    every = range(len(parts))
    ops = 4 * CHUNKS
    rounds = ops + 1
    wtile = hidden // 4
    last = n - 1

    def op_type(i):
        return jnp.where(i < CHUNKS, 0, jnp.where(i >= 3 * CHUNKS, 3, 1 + lax.rem(i + CHUNKS, 2)))

    def op_chunk(i):
        return jnp.where(
            i < CHUNKS, i, jnp.where(i >= 3 * CHUNKS, i - 3 * CHUNKS, (i - CHUNKS) // 2)
        )

    def op_slot(i):
        return jnp.where(i < CHUNKS, i, CHUNKS + lax.rem(i, POOL))

    def half_rows(h):
        return pl.ds(starts[h], parts[h])

    def block_of(h):
        return 32 if parts[h] % 32 == 0 else 16

    ahead = (jnp.minimum(r + 1, last), jnp.maximum(r - 1, 0))
    pos = (r, last - r)

    def item_sent(d, s):
        return lax.rem(r - s + n, n) if d == 0 else lax.rem(r + s, n)

    def sends(d, k, s):
        return (pos[d] < last) & jnp.where(s <= pos[d], k < ops, k >= 1)

    def receives(d, k, s):
        return (pos[d] > 0) & jnp.where(s <= pos[d] - 1, k < ops, k >= 1)

    def copy(d, k, s, h, src, dst):
        return pltpu.make_async_remote_copy(
            src_ref=src,
            dst_ref=dst,
            send_sem=send_sem.at[d, lax.rem(s, 2), h],
            recv_sem=recv_sem.at[d, lax.rem(k, 2), s, h],
            device_id={"rep": ahead[d]},
            device_id_type=MESH,
        )

    def landing(d, k, s, h):
        return recv.at[d, lax.rem(k, 2), s, half_rows(h)]

    def staged(d, s, h):
        return stage.at[d, lax.rem(s, 2), half_rows(h)]

    def wait_sent(d, k, s, h):
        @pl.when(sends(d, k, s))
        def _():
            copy(d, k, s, h, staged(d, s, h), landing(d, k, s, h)).wait_send()

    def wait_received(d, k, s, h):
        @pl.when(receives(d, k, s))
        def _():
            copy(d, k, s, h, staged(d, s, h), landing(d, k, s, h)).wait_recv()

    def finish_sum(k, h):
        rs = half_rows(h)
        total[rs, :] = part[r, rs, :]
        for d in range(2):

            @pl.when(pos[d] > 0)
            def _():
                total[rs, :] += landing(d, k, n - 1, h)[...].astype(jnp.float32)

    def send(d, k, s, h):
        gathers = s <= pos[d]
        p = item_sent(d, s)
        rs = half_rows(h)

        @pl.when(sends(d, k, s) & gathers)
        def _():
            here = gath.at[op_slot(k), p, rs]
            copy(d, k, s, h, here, here).start()

        @pl.when(sends(d, k, s) & jnp.logical_not(gathers))
        def _():
            out = staged(d, s, h)

            @pl.when(pos[d] == 0)
            def _():
                out[...] = part[p, rs, :].astype(jnp.bfloat16)

            @pl.when(pos[d] > 0)
            def _():
                came = landing(d, k, s - 1, h)[...].astype(jnp.float32)
                out[...] = (part[p, rs, :] + came).astype(jnp.bfloat16)

            copy(d, k, s, h, out, landing(d, k, s, h)).start()

    def over_blocks(h, body):
        size = block_of(h)

        def step(b, carry):
            body(pl.multiple_of(starts[h] + b * size, 16))
            return carry

        lax.fori_loop(0, parts[h] // size, step, 0)

    side = lax.rem(e // 2, 2)
    full_at = (0, own_rows - cap, cap, own_rows - 2 * cap)
    middle = pl.ds(2 * cap, own_rows - 4 * cap)

    def cap_rows(q):
        return pl.ds(pl.multiple_of(q * cap, cap), cap)

    def out_copy(w, b, kind):
        j = pair_of(b)
        src = (out_x, out_dy)[w]
        dst = ((x_ref, part_x), (dy_ref, part_dy))[w][kind]
        return pltpu.make_async_remote_copy(
            src_ref=src.at[cap_rows(b)],
            dst_ref=dst.at[pl.ds((full_at[j], j * cap)[kind], cap)],
            send_sem=out_send.at[w, b],
            recv_sem=out_recv.at[w, kind, j],
            device_id={"exp": flip(e, b)},
            device_id_type=MESH,
        )

    def results_of(w, j, kind):
        src = ((y_ref, part_x), (dv_ref, part_dy))[w][kind]
        return src.at[pl.ds((full_at[j], j * cap)[kind], cap)]

    def home_copy(w, j, kind):
        return pltpu.make_async_remote_copy(
            src_ref=results_of(w, j, kind),
            dst_ref=(home_y, home_dv)[w].at[cap_rows(e)],
            send_sem=home_send.at[w, kind, j],
            recv_sem=home_recv.at[w, side, j],
            device_id={"exp": flip(e, 4 * (j // 2) + j % 2) + 2 * (kind - side)},
            device_id_type=MESH,
        )

    def home_own_copy(w, kind):
        dst = (home_y, home_dv)[w].at[cap_rows(e)]
        return pltpu.make_async_copy(results_of(w, 0, kind), dst, home_own.at[w])

    def await_home(w, j, expert_side):
        pltpu.make_async_remote_copy(
            src_ref=part_x.at[pl.ds(0, cap)],
            dst_ref=(home_y, home_dv)[w].at[cap_rows(0)],
            send_sem=home_send.at[w, 0, j],
            recv_sem=home_recv.at[w, expert_side, j],
            device_id={"exp": flip(e, 1)},
            device_id_type=MESH,
        ).wait_recv()

    def per_kind(body):
        for kind in range(2):

            @pl.when(side == kind)
            def _():
                body(kind)

    def dispatch(w, first, stop):
        values = (tok_ref, cot_ref)[w][...]
        if w == 1:
            device = r * blocks + e
            live = live_rows(lengths_ref, device, n * blocks, rows)
            values = (live * values.astype(jnp.float32)).astype(jnp.bfloat16)
        for b in ORDER[first:stop]:
            picked = place[cap_rows(flip(e, b)), :]
            ordered = jnp.dot(picked, values, preferred_element_type=jnp.float32)
            ordered = ordered.astype(jnp.bfloat16)
            if b == 0:

                @pl.when(side == 0)
                def _():
                    (x_ref, dy_ref)[w][:cap, :] = ordered

                @pl.when(side == 1)
                def _():
                    (part_x, part_dy)[w][:cap, :] = ordered

            else:
                (out_x, out_dy)[w][cap_rows(b), :] = ordered
                if w == 0 and b == ORDER[1]:
                    pl.semaphore_wait(barrier, n - 1 + blocks - 1)
                per_kind(lambda kind: out_copy(w, b, kind).start())

    def await_block(w, kind, j):
        def wait():
            out_copy(w, 4 * (j // 2) + j % 2 + 2, kind).wait_recv()

        if j:
            wait()
        else:
            pl.when(side != kind)(wait)

    def seen_copy(b):
        return pltpu.make_async_remote_copy(
            src_ref=seen.at[0],
            dst_ref=seen.at[b],
            send_sem=seen_send.at[b],
            recv_sem=seen_recv.at[b],
            device_id={"exp": flip(e, b)},
            device_id_type=MESH,
        )

    def count_live():
        count = live_count(lengths_ref, r * blocks + e, n * blocks, rows)
        live = lax.broadcasted_iota(jnp.int32, (blocks, rows), 1) < count
        table = lax.broadcasted_iota(jnp.int32, (blocks, rows), 0)
        hits = jnp.where((table == routes_ref[...]) & live, 1.0, 0.0)
        seen[0] = jnp.broadcast_to(jnp.sum(hits, 1, keepdims=True), (blocks, 128))
        for b in range(1, blocks):
            seen_copy(b).start()

    def fullest():
        for b in range(1, blocks):
            seen_copy(b).wait_recv()
        total_seen = seen[0]
        for b in range(1, blocks):
            total_seen += seen[b]
        top[...] = jnp.max(total_seen, 0, keepdims=True)

    def make_pack():
        lane = lax.broadcasted_iota(jnp.int32, (1, 4 * cap), 1)
        target = jnp.zeros((1, 4 * cap), jnp.float32)
        before = jnp.zeros((1, 1), jnp.float32)
        for j in range(4):
            from_it = 4 * (j // 2) + j % 2 + 2 * (1 - side)
            count = seen[from_it, pl.ds(e, 1), 0:1]
            within = (lane - j * cap).astype(jnp.float32)
            here = (lane >= j * cap) & (lane < (j + 1) * cap)
            at = jnp.where(within < count, within + before, -1.0)
            target = jnp.where(here, at, target)
            before += count
        row = lax.broadcasted_iota(jnp.int32, (own_rows - 4 * cap, 4 * cap), 0)
        pack[...] = (row.astype(jnp.float32) == target).astype(jnp.bfloat16)

    def pack_middle(w):
        landed, packed = ((part_x, x_ref), (part_dy, dy_ref))[w]
        packed[middle, :] = jnp.dot(
            pack[...], landed[...], preferred_element_type=jnp.float32
        ).astype(jnp.bfloat16)

    def unpack_middle(w):
        landed, packed = ((part_x, y_ref), (part_dy, dv_ref))[w]
        landed[...] = contract_rows(pack[...], packed[middle, :]).astype(jnp.bfloat16)

    def at_half(stop):
        c, offset = divmod(stop - 1, chunk)
        return c, max(h for h in every if starts[h] <= offset)

    def send_home(w, j, kind):
        if j:
            home_copy(w, j, kind).start()
        else:
            pl.when(side == kind)(lambda: home_own_copy(w, kind).start())
            pl.when(side != kind)(lambda: home_copy(w, 0, kind).start())

    def go_home(w, c, h):
        if not inside:
            return
        for chunk_at in range(CHUNKS):
            done = [j for j in range(4) if at_half(full_at[j] + cap) == (chunk_at, h)]
            packed = at_half(own_rows - 2 * cap) == (chunk_at, h)
            if done or packed:

                @pl.when(c == chunk_at)
                def _():
                    for j in done:
                        send_home(w, j, 0)
                    if packed:
                        unpack_middle(w)
                        for j in range(4):
                            send_home(w, j, 1)

    def gate_of(x):
        return jax.nn.sigmoid(jnp.sum(x * cent_ref[...], -1, keepdims=True))

    def prepare(i, h):
        kind, c, slot = op_type(i), op_chunk(i), op_slot(i)

        block = block_of(h)

        def own(offset, value):
            gath[slot, r, pl.ds(offset, block), :] = value.astype(jnp.bfloat16)

        def source(offset):
            return pl.ds(pl.multiple_of(c * chunk + offset, 16), block)

        @pl.when(kind == 0)
        def _():
            over_blocks(
                h,
                lambda o: own(
                    o,
                    layer_stats(x_ref[source(o), :].astype(jnp.float32))[0] * gain_ref[0:1, :]
                    + nbias_ref[0:1, :],
                )
            )

        @pl.when(kind == 1)
        def _():
            over_blocks(
                h,
                lambda o: own(
                    o, layer_stats(state[source(o), :])[0] * gain_ref[1:2, :] + nbias_ref[1:2, :]
                )
            )

        @pl.when(kind == 2)
        def _():
            over_blocks(
                h,
                lambda o: own(
                    o,
                    gate_of(x_ref[source(o), :].astype(jnp.float32))
                    * dy_ref[source(o), :].astype(jnp.float32),
                )
            )

        @pl.when(kind == 3)
        def _():
            over_blocks(h, lambda o: own(o, state[source(o), :]))

    def norm_back(values, grad, k):
        unit, scale = layer_stats(values)
        accs[1 + k] += fold(grad * unit)
        accs[3 + k] += fold(grad)
        through = grad * gain_ref[k : k + 1, :]
        return scale * (
            through
            - jnp.mean(through, -1, keepdims=True)
            - unit * jnp.mean(through * unit, -1, keepdims=True)
        )

    def finish(i, h):
        kind, c = op_type(i), op_chunk(i)
        block = block_of(h)

        def source(offset):
            return pl.ds(pl.multiple_of(c * chunk + offset, 16), block)

        @pl.when(kind == 0)
        def _():
            def body(o):
                state[source(o), :] = (
                    x_ref[source(o), :].astype(jnp.float32)
                    + total[pl.ds(o, block), :]
                    + bout_ref[0:1, :]
                )

            over_blocks(h, body)

        @pl.when(kind == 1)
        def _():
            def body(o):
                x = x_ref[source(o), :].astype(jnp.float32)
                dy = dy_ref[source(o), :].astype(jnp.float32)
                upper = state[source(o), :] + total[pl.ds(o, block), :] + bout_ref[1:2, :]
                gate = gate_of(x)
                y_ref[source(o), :] = (gate * upper).astype(jnp.bfloat16)
                logit = jnp.sum(dy * upper, -1, keepdims=True) * gate * (1.0 - gate)
                dlog[source(o), :] = jnp.broadcast_to(logit, (block, dlog.shape[1]))
                accs[0] += fold(logit * x)

            over_blocks(h, body)
            go_home(0, c, h)

        @pl.when(kind == 2)
        def _():
            def body(o):
                x = x_ref[source(o), :].astype(jnp.float32)
                top = gate_of(x) * dy_ref[source(o), :].astype(jnp.float32)
                middle = top + norm_back(state[source(o), :], total[pl.ds(o, block), :], 1)
                state[source(o), :] = middle
                accs[5] += fold(middle)
                accs[6] += fold(top)

            over_blocks(h, body)

        @pl.when(kind == 3)
        def _():
            def body(o):
                x = x_ref[source(o), :].astype(jnp.float32)
                dv_ref[source(o), :] = (
                    state[source(o), :]
                    + norm_back(x, total[pl.ds(o, block), :], 0)
                    + dlog[source(o), 0:1] * cent_ref[...]
                ).astype(jnp.bfloat16)

            over_blocks(h, body)
            go_home(1, c, h)

    def item_first(i, par, p):
        kind = op_type(i)
        k = jnp.where((kind == 1) | (kind == 2), 1, 0)
        slot = jnp.where(
            kind == 2, op_slot(i - 1), jnp.where(kind == 3, op_chunk(i), op_slot(i))
        )

        inner = (
            jnp.dot(gath[slot, p], wi[k], preferred_element_type=jnp.float32)
            + bias_ref[pl.ds(k, 1), pl.ds(pl.multiple_of(r * hidden, hidden), hidden)]
        )
        low, pull = gelu_and_slope(inner)
        act[par, p] = low.astype(jnp.bfloat16)
        slope[...] = pull

    def item_pull(i, par, p):
        kind = op_type(i)
        k = jnp.where((kind == 1) | (kind == 2), 1, 0)

        @pl.when(kind >= 2)
        def _():
            grad = contract_cols(gath[op_slot(i), p], wo[k]) * slope[...]
            bacc[k] += fold(grad)
            dq[par, p] = grad.astype(jnp.bfloat16)

    def item_second(i, par, p):
        kind = op_type(i)
        k = jnp.where((kind == 1) | (kind == 2), 1, 0)

        @pl.when(kind < 2)
        def _():
            part[p] = jnp.dot(act[par, p], wo[k], preferred_element_type=jnp.float32)

        @pl.when(kind >= 2)
        def _():
            part[p] = contract_cols(dq[par, p], wi[k])

    def weight_grads(i, par, j):
        kind = op_type(i)
        k = jnp.where(kind == 2, 1, 0)
        slot = jnp.where(kind == 2, op_slot(i - 1), op_chunk(i))
        cs = pl.ds(pl.multiple_of(j * wtile, wtile), wtile)
        depth = n * chunk
        normed = gath[slot, :, :, cs].reshape(depth, wtile)
        gwi[k, cs, :] += contract_rows(normed, dq[par].reshape(depth, hidden))
        active = act[par, :, :, cs].reshape(depth, wtile)
        gwo[k, cs, :] += contract_rows(active, gath[op_slot(i)].reshape(depth, width))

    def item_at(s):
        near = jnp.minimum(r, last - r)
        base = jnp.where(near == 0, last - s, jnp.where(s < 2, last - s, s - 2))
        return jnp.where(r < 2, base, last - base)

    def cot_load():
        return pltpu.make_async_copy(cot_hbm, cot_ref, cot_sem)

    EARLY, LATE = (0, 2, 4, 5, 6), (1, 3)

    def tell(late, q):
        src, dst = ((mine, peers), (mine_late, peers_late))[late]
        return pltpu.make_async_remote_copy(
            src_ref=src,
            dst_ref=dst.at[q - 1],
            send_sem=peer_send.at[late, q - 1],
            recv_sem=peer_recv.at[late, q - 1],
            device_id={"rep": lax.rem(r + q, n)},
            device_id_type=MESH,
        )

    def tell_early():
        for a, row in enumerate(EARLY):
            mine[a : a + 1, :width] = jnp.sum(accs[row], 0, keepdims=True)
        mine[5:6, :hidden] = jnp.sum(bacc[1], 0, keepdims=True)
        mine[6:8, :] = jnp.zeros((2, mine.shape[1]), jnp.float32)
        if inside:
            mine[6:7, :128] = top[...]
        for q in range(1, n):
            tell(0, q).start()

    def tell_late():
        at = 0
        for values in (accs[LATE[0]], accs[LATE[1]], bacc[0]):
            flat = jnp.sum(values, 0, keepdims=True)
            for j in range(flat.shape[1] // 128):
                mine_late[at : at + 1, :] = flat[:, j * 128 : (j + 1) * 128]
                at += 1
        for q in range(1, n):
            tell(1, q).start()

    def unpack(packed, at, size):
        return jnp.concatenate([packed[at + j : at + j + 1] for j in range(size // 128)], 1)

    def load(w):
        src, dst = ((wi_hbm, wi), (wo_hbm, wo))[w]
        return pltpu.make_async_copy(src, dst, load_sem.at[w])

    barrier = pltpu.get_barrier_semaphore()
    for q in range(1, n):
        pl.semaphore_signal(
            barrier, inc=1, device_id={"rep": lax.rem(r + q, n)}, device_id_type=MESH
        )
    load(0).start()
    load(1).start()
    if inside:
        for b in range(1, blocks):
            pl.semaphore_signal(
                barrier, inc=1, device_id={"exp": flip(e, b)}, device_id_type=MESH
            )
        cot_load().start()
        place[...] = slot_rows(routes_ref[...], blocks, cap)
        dispatch(0, 0, 2)
        await_block(0, 0, 0)
    else:
        pl.semaphore_wait(barrier, n - 1)
    prepare(0, 0)

    def step(t, carry):
        k, s = t // n, lax.rem(t, n)
        k_before, s_before = (t - 1) // n, lax.rem(t + n - 1, n)
        i = k - 1
        par = lax.rem(k, 2)
        p = item_at(s)

        def exchange(h):
            for d in range(2):

                @pl.when(t >= 1)
                def _():
                    wait_received(d, k_before, s_before, h)

                @pl.when(t >= 2)
                def _():
                    wait_sent(d, (t - 2) // n, lax.rem(t + n - 2, n), h)

            @pl.when((s == 0) & (k >= 2))
            def _():
                finish_sum(k - 1, h)

            for d in range(2):
                send(d, k, s, h)

        def grads(j):
            old = k - 2

            @pl.when((s < 2) & (old >= CHUNKS) & (op_type(old) >= 2))
            def _():
                weight_grads(old, lax.rem(k + 1, 2), j)

        exchange(0)

        @pl.when(t == n * ops)
        def _():
            tell_early()

        @pl.when(t == 0)
        def _():
            if inside:
                dispatch(0, 2, blocks)
                await_block(0, 0, 2)
            for h in every[1:]:
                prepare(0, h)

        @pl.when(t == 1)
        def _():
            def clear(b, carry):
                zero_rows = pl.ds(pl.multiple_of(b * 64, 64), 64)
                for w in range(2):
                    gwi[w, zero_rows, :] = jnp.zeros((64, hidden), jnp.float32)
                    gwo[w, zero_rows, :] = jnp.zeros((64, width), jnp.float32)
                return carry

            lax.fori_loop(0, width // 64, clear, 0)
            accs[...] = jnp.zeros_like(accs)
            bacc[...] = jnp.zeros_like(bacc)

        if inside:

            @pl.when(t == 2)
            def _():
                cot_load().wait()
                dispatch(1, 0, blocks)

            @pl.when(t == 1)
            def _():
                count_live()

            @pl.when(t == 3)
            def _():
                fullest()
                make_pack()
                for kind, j in ((0, 1), (0, 3), (1, 0), (1, 1), (1, 2), (1, 3)):
                    await_block(0, kind, j)
                pack_middle(0)

            @pl.when(t == n * CHUNKS)
            def _():
                for w in range(2):
                    for b in range(1, blocks):
                        out_copy(w, b, 0).wait_send()
                for b in range(1, blocks):
                    seen_copy(b).wait_send()
                for kind in range(2):
                    for j in range(4):
                        await_block(1, kind, j)
                pack_middle(1)

        @pl.when(t == n)
        def _():
            load(0).wait()
            load(1).wait()

        pieces = [item_first, item_pull, item_second]
        for h in every:
            if h:
                exchange(h)
            mine_now = pieces[h : h + 1] if h < len(parts) - 1 else pieces[h:]
            if len(parts) == 2:
                mine_now = (pieces[:2], pieces[2:])[h]

            @pl.when(k >= 1)
            def _():
                for piece in mine_now:
                    piece(i, par, p)

            if h == 0:
                grads(2 * s)
            elif h == len(parts) - 1:
                grads(2 * s + 1)

        @pl.when((s == 2) & (k >= 2))
        def _():
            for h in every:
                finish(k - 2, h)

        @pl.when((s == 3) & (k < ops - 1))
        def _():
            for h in every:
                prepare(k + 1, h)

        return carry

    steps = rounds * n
    lax.fori_loop(0, steps, step, 0)

    def last_grads(j, carry):
        weight_grads(ops - 1, (rounds - 1) % 2, j)
        return carry

    lax.fori_loop(0, 4, last_grads, 0)
    for h in every:
        for d in range(2):
            wait_received(d, rounds - 1, n - 1, h)
        finish_sum(rounds - 1, h)
        finish(ops - 1, h)
    for h in every:
        for d in range(2):
            for back in (2, 1):
                wait_sent(d, (steps - back) // n, (steps - back) % n, h)

    tell_late()

    def place_bins(k, q, bins):
        bin_out[k : k + 1, pl.ds(pl.multiple_of(q * hidden, hidden), hidden)] = bins

    for q in range(1, n):
        tell(0, q).wait_recv()
    sums = mine[0:5, :width]
    place_bins(1, r, mine[5:6, :hidden])
    for q in range(1, n):
        sums += peers[q - 1, 0:5, :width]
        place_bins(1, lax.rem(r - q + n, n), peers[q - 1, 5:6, :hidden])
    cent_out[...] = sums[0:1]
    gain_out[1:2, :] = sums[1:2]
    nbias_out[1:2, :] = sums[2:3]
    bout_out[...] = sums[3:5]
    if inside:
        most = mine[6:7, :128]
        for q in range(1, n):
            most = jnp.maximum(most, peers[q - 1, 6:7, :128])
        top_out[...] = jnp.broadcast_to(most, top_out.shape)
    for q in range(1, n):
        tell(1, q).wait_recv()
    mine_rows = mine_late[...]
    late = mine_rows[: 2 * width // 128]
    place_bins(0, r, unpack(mine_rows, 2 * width // 128, hidden))
    for q in range(1, n):
        theirs = peers_late[q - 1]
        late += theirs[: 2 * width // 128]
        place_bins(0, lax.rem(r - q + n, n), unpack(theirs, 2 * width // 128, hidden))
    gain_out[0:1, :] = unpack(late, 0, width)
    nbias_out[0:1, :] = unpack(late, width // 128, width)
    for q in range(1, n):
        tell(0, q).wait_send()
        tell(1, q).wait_send()
    if inside:
        for w in range(2):
            for kind in range(2):
                for j in range(4):
                    if j:
                        home_copy(w, j, kind).wait_send()
                    else:
                        pl.when(side == kind)(lambda: home_own_copy(w, kind).wait())
                        pl.when(side != kind)(lambda: home_copy(w, 0, kind).wait_send())
            for j in range(4):
                for expert_side in range(2):
                    if j:
                        await_home(w, j, expert_side)
                    else:
                        pl.when(side != expert_side)(
                            functools.partial(await_home, w, j, expert_side)
                        )


def run_layer(own_rows, name, inside, rows_in, gains, nbias, cent, biases, bout, wi, wo):
    n, blocks = lax.axis_size("rep"), lax.axis_size("exp")
    rows, width = rows_in[0].shape
    hidden = wi.shape[2]
    parts = PLANS[own_rows] if inside else (rows // 8, rows // 8)
    chunk = sum(parts)
    CHUNKS = own_rows // chunk
    wide = max(width, hidden)
    late = (2 * width + hidden) // 128
    low, full = jnp.bfloat16, jnp.float32
    vmem = pl.BlockSpec(memory_space=pltpu.VMEM)
    anywhere = pl.BlockSpec(memory_space=pl.ANY)
    row_specs = [vmem] * 2
    extra = []
    if inside:
        row_specs = [vmem, anywhere, vmem, pl.BlockSpec(memory_space=pltpu.SMEM)]
        extra = (
            [pltpu.VMEM((own_rows, width), low)] * 2
            + [pltpu.VMEM((rows, width), low)] * 2
            + [pltpu.VMEM((rows, rows), low)]
            + [pltpu.VMEM((rows, width), low)]
            + [pltpu.VMEM((rows // 2, width), low)] * 2
            + [pltpu.VMEM((own_rows - rows // 2, rows // 2), low)]
            + [pltpu.VMEM((blocks, blocks, 128), full), pltpu.VMEM((1, 128), full)]
            + [pltpu.SemaphoreType.DMA((2, blocks)), pltpu.SemaphoreType.DMA((2, 2, blocks // 2))]
            + [pltpu.SemaphoreType.DMA((2, 2, blocks // 2))] * 2
            + [pltpu.SemaphoreType.DMA((2,)), pltpu.SemaphoreType.DMA]
            + [pltpu.SemaphoreType.DMA((blocks,))] * 2
        )
    flops = 2 * 16 * n * own_rows * width * hidden
    return pl.pallas_call(
        functools.partial(kernel, n, blocks, inside, parts),
        out_shape=(
            pltpu.VMEM((rows, width), low) if inside else jax.ShapeDtypeStruct((rows, width), low),
            pltpu.VMEM((rows, width), low) if inside else jax.ShapeDtypeStruct((rows, width), low),
            pltpu.VMEM((2, width, hidden), full),
            pltpu.VMEM((2, hidden, width), full),
            jax.ShapeDtypeStruct((1, width), full),
            jax.ShapeDtypeStruct((2, width), full),
            jax.ShapeDtypeStruct((2, width), full),
            jax.ShapeDtypeStruct((2, n * hidden), full),
            jax.ShapeDtypeStruct((2, width), full),
        )
        + ((jax.ShapeDtypeStruct((8, 128), full),) if inside else ()),
        in_specs=row_specs + [vmem] * 5 + [anywhere] * 2,
        out_specs=(vmem,) * (10 if inside else 9),
        scratch_shapes=[
            pltpu.VMEM((CHUNKS + POOL, n, chunk, width), low),
            pltpu.VMEM((2, width, hidden), low),
            pltpu.VMEM((2, hidden, width), low),
            pltpu.VMEM((n, chunk, width), full),
            pltpu.VMEM((2, n, chunk, hidden), low),
            pltpu.VMEM((2, n, chunk, hidden), low),
            pltpu.VMEM((chunk, hidden), full),
            pltpu.VMEM((chunk, width), full),
            pltpu.VMEM((own_rows, width), full),
            pltpu.VMEM((own_rows, 128), full),
            pltpu.VMEM((2, 2, n, chunk, width), low),
            pltpu.VMEM((2, 2, chunk, width), low),
            pltpu.VMEM((7, 8, width), full),
            pltpu.VMEM((2, 8, hidden), full),
            pltpu.VMEM((8, wide), full),
            pltpu.VMEM((n - 1, 8, wide), full),
            pltpu.VMEM((late, 128), full),
            pltpu.VMEM((n - 1, late, 128), full),
            pltpu.SemaphoreType.DMA((2, 2, len(parts))),
            pltpu.SemaphoreType.DMA((2, 2, n, len(parts))),
            pltpu.SemaphoreType.DMA((2,)),
            pltpu.SemaphoreType.DMA((2, n - 1)),
            pltpu.SemaphoreType.DMA((2, n - 1)),
        ]
        + extra,
        compiler_params=pltpu.CompilerParams(
            collective_id=name, has_side_effects=True, vmem_limit_bytes=VMEM_BYTES
        ),
        cost_estimate=pl.CostEstimate(
            flops=flops, bytes_accessed=40 * rows * width, transcendentals=8 * rows * hidden * n
        ),
    )(*rows_in, gains, nbias, cent, biases, bout, wi, wo)


def close_kernel(device_count, cap, *refs):
    tok_hbm, cot_hbm, routes_ref, lengths_ref, y, dv, gwi_in, gwo_in = refs[:8]
    small_in, refs = refs[8:13], refs[13:]
    mixed_ref, grad_ref, gwi_out, gwo_out = refs[:4]
    small_out, refs = refs[4:9], refs[9:]
    tok, cot, load_sem, move_sem = refs
    rows = tok.shape[0]
    loads = [
        pltpu.make_async_copy(src, dst, load_sem.at[j])
        for j, (src, dst) in enumerate(((tok_hbm, tok), (cot_hbm, cot)))
    ]
    moves = [
        pltpu.make_async_copy(src.at[k], dst.at[k], move_sem.at[w, k])
        for w, (src, dst) in enumerate(((gwi_in, gwi_out), (gwo_in, gwo_out)))
        for k in range(2)
    ]
    for copy in loads + moves:
        copy.start()
    for src, dst in zip(small_in, small_out):
        dst[...] = src[...]
    place = slot_rows(routes_ref[...], rows // cap, cap)
    device = lax.axis_index("rep") * lax.axis_size("exp") + lax.axis_index("exp")
    live = live_rows(lengths_ref, device, device_count, rows)
    for copy in loads:
        copy.wait()
    mixed_ref[...] = (tok[...].astype(jnp.float32) + live * contract_rows(place, y[...])).astype(
        jnp.bfloat16
    )
    grad_ref[...] = (cot[...].astype(jnp.float32) + contract_rows(place, dv[...])).astype(
        jnp.bfloat16
    )
    for copy in moves:
        copy.wait()


def close(tokens, cotangent, routes, lengths, home_y, home_dv, gwi, gwo, *small):
    n, blocks = lax.axis_size("rep"), lax.axis_size("exp")
    rows, width = tokens.shape
    vmem = pl.BlockSpec(memory_space=pltpu.VMEM)
    anywhere = pl.BlockSpec(memory_space=pl.ANY)
    rows_shape = jax.ShapeDtypeStruct(tokens.shape, tokens.dtype)
    like = lambda a: jax.ShapeDtypeStruct(a.shape, a.dtype)
    home_y, home_dv, gwi, gwo = (
        pltpu.with_memory_space_constraint(a, pltpu.VMEM) for a in (home_y, home_dv, gwi, gwo)
    )
    return pl.pallas_call(
        functools.partial(close_kernel, n * blocks, rows // blocks),
        out_shape=(rows_shape, rows_shape, like(gwi), like(gwo), *map(like, small)),
        in_specs=[anywhere, anywhere, vmem, pl.BlockSpec(memory_space=pltpu.SMEM)]
        + [vmem] * 9,
        out_specs=[vmem, vmem, anywhere, anywhere] + [vmem] * 5,
        scratch_shapes=[pltpu.VMEM((rows, width), tokens.dtype)] * 2
        + [pltpu.SemaphoreType.DMA((2,)), pltpu.SemaphoreType.DMA((2, 2))],
        compiler_params=pltpu.CompilerParams(vmem_limit_bytes=VMEM_BYTES),
    )(tokens, cotangent, routes, lengths, home_y, home_dv, gwi, gwo, *small)


def no_results(shapes):
    def kernel(*refs):
        refs[-1][...] = jnp.zeros_like(refs[-1])

    anywhere = pl.BlockSpec(memory_space=pl.ANY)
    *results, _ = pl.pallas_call(
        kernel,
        out_shape=(*shapes, jax.ShapeDtypeStruct((8, 128), jnp.float32)),
        out_specs=[anywhere] * len(shapes) + [pl.BlockSpec(memory_space=pltpu.VMEM)],
    )()
    return tuple(results)


def shards(
    tokens,
    routes,
    lengths,
    centroids,
    norm_gains,
    norm_biases,
    w_in,
    in_biases,
    w_out,
    out_biases,
    cotangent,
):
    n_exp = lax.axis_size("exp")
    tok_rows = tokens.shape[0]
    cap = tok_rows // n_exp
    params = (
        norm_gains[0],
        norm_biases[0],
        centroids,
        in_biases[0],
        out_biases[0],
        w_in[0],
        w_out[0],
    )
    devices = n_exp * lax.axis_size("rep")
    if n_exp == 8 and tok_rows == max(PLANS) and devices == 4 * lengths.shape[0]:
        less, whole = sorted(PLANS)
        given = (tokens, cotangent, routes.reshape(1, tok_rows), lengths)

        def layer(own_rows, name, given, *params):
            *results, most = run_layer(own_rows, name, True, given, *params)
            return tuple(close(*given, *results)), most[0, 0] <= own_rows

        seqs, planes = lengths.shape[0], lax.axis_size("rep")
        of_plane = lax.iota(jnp.int32, seqs) // (seqs // planes) == lax.iota(jnp.int32, planes)[:, None]
        plane_live = jnp.sum(jnp.where(of_plane, lengths, 0), 1)
        shapes = jax.eval_shape(functools.partial(layer, less, 0), given, *params)[0]
        results, done = lax.cond(
            jnp.max(plane_live) <= (less - SPARE) * n_exp,
            functools.partial(layer, less, 0),
            lambda *_: (no_results(shapes), jnp.array(False)),
            given,
            *params,
        )
        results = lax.cond(
            done,
            lambda results, *_: results,
            lambda results, *rest: layer(whole, 1, *rest)[0],
            results,
            given,
            *params,
        )
    else:
        device = lax.axis_index(("rep", "exp"))
        slot = tok_rows * n_exp * lax.axis_size("rep") // lengths.shape[0]
        positions = device * tok_rows + lax.iota(jnp.int32, tok_rows)
        seq_ids = positions // slot
        seq_table = lax.iota(jnp.int32, lengths.shape[0])
        seq_len = jnp.sum(
            jnp.where(seq_ids[:, None] == seq_table[None, :], lengths[None, :], 0), 1
        )
        live = (positions % slot < seq_len).astype(jnp.float32)[:, None]
        route = routes[:, 0]
        hits = (route[:, None] == lax.iota(jnp.int32, n_exp)[None, :]).astype(jnp.int32)
        before = jnp.cumsum(hits, 0) - hits
        target = route * cap + jnp.sum(before * hits, 1)
        place = (lax.iota(jnp.int32, tok_rows)[:, None] == target[None, :]).astype(jnp.bfloat16)
        grad_out = (live * cotangent.astype(jnp.float32)).astype(jnp.bfloat16)

        def send(rows):
            ordered = jnp.dot(place, rows, preferred_element_type=jnp.float32).astype(jnp.bfloat16)
            return lax.all_to_all(ordered, "exp", split_axis=0, concat_axis=0, tiled=True)

        def give_back(rows):
            back = lax.all_to_all(rows, "exp", split_axis=0, concat_axis=0, tiled=True)
            return contract_rows(place, back)

        given = (send(tokens), send(grad_out))
        result, grad_local, *rest = run_layer(tok_rows, 0, False, given, *params)
        mixed = (tokens.astype(jnp.float32) + live * give_back(result)).astype(jnp.bfloat16)
        tokens_grad = (cotangent.astype(jnp.float32) + give_back(grad_local)).astype(jnp.bfloat16)
        results = (mixed, tokens_grad, *rest)
    mixed, tokens_grad, gwi, gwo, cent_grad, gain_grad, nbias_grad, bin_grad, bout_grad = results
    return (
        mixed,
        tokens_grad,
        cent_grad,
        gain_grad[None],
        nbias_grad[None],
        gwi[None],
        bin_grad[None],
        gwo[None],
        bout_grad[None],
    )


def solution(mesh):
    placed = (
        P(("rep", "exp"), None),
        P(("rep", "exp"), None),
        P(),
        P("exp", None),
        P("exp", None, None),
        P("exp", None, None),
        P("exp", None, None, "rep"),
        P("exp", None, None),
        P("exp", None, "rep", None),
        P("exp", None, None),
        P(("rep", "exp"), None),
    )
    return jax.shard_map(
        shards,
        mesh=mesh,
        in_specs=placed,
        out_specs=(
            P(("rep", "exp"), None),
            P(("rep", "exp"), None),
            P("exp", None),
            P("exp", None, None),
            P("exp", None, None),
            P("exp", None, None, "rep"),
            P("exp", None, None),
            P("exp", None, "rep", None),
            P("exp", None, None),
        ),
        check_vma=False,
    )
```

```python
import functools

import jax
import jax.numpy as jnp
from jax import lax
from jax.experimental import pallas as pl
from jax.experimental.pallas import tpu as pltpu
from jax.sharding import PartitionSpec as P

eps = 1e-05
VMEM_BYTES = 44 * 1024 * 1024


def contract_rows(left, right):
    return lax.dot_general(
        left, right, (((0,), (0,)), ((), ())), preferred_element_type=jnp.float32
    )


def contract_cols(left, right):
    return lax.dot_general(
        left, right, (((1,), (1,)), ((), ())), preferred_element_type=jnp.float32
    )


MESH = pl.DeviceIdType.MESH
POOL = 4
PLANS = {448: (32, 32, 32, 16), 512: (64, 64)}
SPARE = 16
ORDER = (0, 2, 4, 6, 5, 7, 3, 1)
ROOT = 0.7978845608028654
CUBE = 0.044715


def layer_stats(values):
    center = values - jnp.mean(values, -1, keepdims=True)
    spread = jnp.mean(center * center, -1, keepdims=True)
    scale = lax.rsqrt(spread + eps)
    return center * scale, scale


def gelu_and_slope(inner):
    square = inner * inner
    bent = jnp.tanh(inner * (ROOT + (ROOT * CUBE) * square))
    half = 0.5 * (1.0 + bent)
    slope = half + (0.5 * inner) * (1.0 - bent * bent) * (ROOT + (3.0 * ROOT * CUBE) * square)
    return inner * half, slope


def fold(rows):
    return jnp.sum(rows.reshape(rows.shape[0] // 8, 8, rows.shape[1]), 0)


def pair_of(b):
    return (b >> 2) * 2 + (b & 1)


def flip(index, bits):
    out, place = index, 1
    while place <= bits:
        if bits & place:
            out = out + place * (1 - 2 * lax.rem(index // place, 2))
        place *= 2
    return out


def slot_rows(routes, blocks, cap):
    rows = routes.shape[1]
    along = routes.astype(jnp.float32)
    table = lax.broadcasted_iota(jnp.int32, (max(blocks, 8), rows), 0).astype(jnp.float32)
    hits = (table == along).astype(jnp.float32)
    first = lax.broadcasted_iota(jnp.int32, (rows, rows), 0)
    second = lax.broadcasted_iota(jnp.int32, (rows, rows), 1)
    earlier = (first < second).astype(jnp.bfloat16)
    before = jnp.dot(hits.astype(jnp.bfloat16), earlier, preferred_element_type=jnp.float32)
    target = along * cap + jnp.sum(before * hits, 0, keepdims=True)
    return (first.astype(jnp.float32) == target).astype(jnp.bfloat16)


def live_count(lengths_ref, device, devices, rows):
    slot = rows * devices // lengths_ref.shape[0]
    start = device * rows
    return lengths_ref[start // slot] - lax.rem(start, slot)


def live_rows(lengths_ref, device, devices, rows):
    count = live_count(lengths_ref, device, devices, rows)
    return (lax.broadcasted_iota(jnp.int32, (rows, 1), 0) < count).astype(jnp.float32)


def kernel(n, blocks, inside, parts, *refs):
    refs = list(refs)
    take = lambda count: [refs.pop(0) for _ in range(count)]
    if inside:
        tok_ref, cot_hbm, routes_ref, lengths_ref = take(4)
    else:
        x_ref, dy_ref = take(2)
    gain_ref, nbias_ref, cent_ref, bias_ref, bout_ref, wi_hbm, wo_hbm = take(7)
    home_y, home_dv, gwi, gwo, cent_out, gain_out, nbias_out, bin_out, bout_out = take(9)
    top_out = take(1)[0] if inside else None
    gath, wi, wo, part, act, dq, slope, total, state, dlog, recv, stage = take(12)
    accs, bacc, mine, peers, mine_late, peers_late = take(6)
    send_sem, recv_sem, load_sem, peer_send, peer_recv = take(5)
    if inside:
        x_ref, dy_ref, y_ref, dv_ref, place, cot_ref, part_x, part_dy, pack, seen, top = take(11)
        out_x, out_dy = y_ref, dv_ref
        out_send, out_recv, home_send, home_recv, home_own, cot_sem = take(6)
        seen_send, seen_recv = take(2)
    else:
        y_ref, dv_ref = home_y, home_dv
    r = lax.axis_index("rep")
    e = lax.axis_index("exp")
    own_rows, width = x_ref.shape
    hidden = wi_hbm.shape[2]
    rows = home_y.shape[0]
    cap = rows // blocks
    chunk = sum(parts)
    CHUNKS = own_rows // chunk
    starts = [sum(parts[:h]) for h in range(len(parts))]
    every = range(len(parts))
    ops = 4 * CHUNKS
    rounds = ops + 1
    wtile = hidden // 4
    last = n - 1

    def op_type(i):
        return jnp.where(i < CHUNKS, 0, jnp.where(i >= 3 * CHUNKS, 3, 1 + lax.rem(i + CHUNKS, 2)))

    def op_chunk(i):
        return jnp.where(
            i < CHUNKS, i, jnp.where(i >= 3 * CHUNKS, i - 3 * CHUNKS, (i - CHUNKS) // 2)
        )

    def op_slot(i):
        return jnp.where(i < CHUNKS, i, CHUNKS + lax.rem(i, POOL))

    def half_rows(h):
        return pl.ds(starts[h], parts[h])

    def extent(h):
        return (0, chunk) if h is None else (starts[h], parts[h])

    def block_of(h):
        return 32 if extent(h)[1] % 32 == 0 else 16

    ahead = (jnp.minimum(r + 1, last), jnp.maximum(r - 1, 0))
    pos = (r, last - r)

    def item_sent(d, s):
        return lax.rem(r - s + n, n) if d == 0 else lax.rem(r + s, n)

    def sends(d, k, s):
        return (pos[d] < last) & jnp.where(s <= pos[d], k < ops, k >= 1)

    def receives(d, k, s):
        return (pos[d] > 0) & jnp.where(s <= pos[d] - 1, k < ops, k >= 1)

    def copy(d, k, s, h, src, dst):
        return pltpu.make_async_remote_copy(
            src_ref=src,
            dst_ref=dst,
            send_sem=send_sem.at[d, lax.rem(s, 2), h],
            recv_sem=recv_sem.at[d, lax.rem(k, 2), s, h],
            device_id={"rep": ahead[d]},
            device_id_type=MESH,
        )

    def landing(d, k, s, h):
        return recv.at[d, lax.rem(k, 2), s, half_rows(h)]

    def staged(d, s, h):
        return stage.at[d, lax.rem(s, 2), half_rows(h)]

    def wait_sent(d, k, s, h):
        @pl.when(sends(d, k, s))
        def _():
            copy(d, k, s, h, staged(d, s, h), landing(d, k, s, h)).wait_send()

    def wait_received(d, k, s, h):
        @pl.when(receives(d, k, s))
        def _():
            copy(d, k, s, h, staged(d, s, h), landing(d, k, s, h)).wait_recv()

    def finish_sum(k, h):
        rs = half_rows(h)
        total[rs, :] = part[r, rs, :]
        for d in range(2):

            @pl.when(pos[d] > 0)
            def _():
                total[rs, :] += landing(d, k, n - 1, h)[...].astype(jnp.float32)

    def send(d, k, s, h):
        gathers = s <= pos[d]
        p = item_sent(d, s)
        rs = half_rows(h)

        @pl.when(sends(d, k, s) & gathers)
        def _():
            here = gath.at[op_slot(k), p, rs]
            copy(d, k, s, h, here, here).start()

        @pl.when(sends(d, k, s) & jnp.logical_not(gathers))
        def _():
            out = staged(d, s, h)

            @pl.when(pos[d] == 0)
            def _():
                out[...] = part[p, rs, :].astype(jnp.bfloat16)

            @pl.when(pos[d] > 0)
            def _():
                came = landing(d, k, s - 1, h)[...].astype(jnp.float32)
                out[...] = (part[p, rs, :] + came).astype(jnp.bfloat16)

            copy(d, k, s, h, out, landing(d, k, s, h)).start()

    def over_blocks(h, body):
        size = block_of(h)

        def step(b, carry):
            body(pl.multiple_of(extent(h)[0] + b * size, 16))
            return carry

        lax.fori_loop(0, extent(h)[1] // size, step, 0)

    side = lax.rem(e // 2, 2)
    full_at = (0, own_rows - cap, cap, own_rows - 2 * cap)
    middle = pl.ds(2 * cap, own_rows - 4 * cap)

    def cap_rows(q):
        return pl.ds(pl.multiple_of(q * cap, cap), cap)

    def out_copy(w, b, kind):
        j = pair_of(b)
        src = (out_x, out_dy)[w]
        dst = ((x_ref, part_x), (dy_ref, part_dy))[w][kind]
        return pltpu.make_async_remote_copy(
            src_ref=src.at[cap_rows(b)],
            dst_ref=dst.at[pl.ds((full_at[j], j * cap)[kind], cap)],
            send_sem=out_send.at[w, b],
            recv_sem=out_recv.at[w, kind, j],
            device_id={"exp": flip(e, b)},
            device_id_type=MESH,
        )

    def results_of(w, j, kind):
        src = ((y_ref, part_x), (dv_ref, part_dy))[w][kind]
        return src.at[pl.ds((full_at[j], j * cap)[kind], cap)]

    def home_copy(w, j, kind):
        return pltpu.make_async_remote_copy(
            src_ref=results_of(w, j, kind),
            dst_ref=(home_y, home_dv)[w].at[cap_rows(e)],
            send_sem=home_send.at[w, kind, j],
            recv_sem=home_recv.at[w, side, j],
            device_id={"exp": flip(e, 4 * (j // 2) + j % 2) + 2 * (kind - side)},
            device_id_type=MESH,
        )

    def home_own_copy(w, kind):
        dst = (home_y, home_dv)[w].at[cap_rows(e)]
        return pltpu.make_async_copy(results_of(w, 0, kind), dst, home_own.at[w])

    def await_home(w, j, expert_side):
        pltpu.make_async_remote_copy(
            src_ref=part_x.at[pl.ds(0, cap)],
            dst_ref=(home_y, home_dv)[w].at[cap_rows(0)],
            send_sem=home_send.at[w, 0, j],
            recv_sem=home_recv.at[w, expert_side, j],
            device_id={"exp": flip(e, 1)},
            device_id_type=MESH,
        ).wait_recv()

    def per_kind(body):
        for kind in range(2):

            @pl.when(side == kind)
            def _():
                body(kind)

    def dispatch(w, first, stop):
        values = (tok_ref, cot_ref)[w][...]
        if w == 1:
            device = r * blocks + e
            live = live_rows(lengths_ref, device, n * blocks, rows)
            values = (live * values.astype(jnp.float32)).astype(jnp.bfloat16)
        for b in ORDER[first:stop]:
            picked = place[cap_rows(flip(e, b)), :]
            ordered = jnp.dot(picked, values, preferred_element_type=jnp.float32)
            ordered = ordered.astype(jnp.bfloat16)
            if b == 0:

                @pl.when(side == 0)
                def _():
                    (x_ref, dy_ref)[w][:cap, :] = ordered

                @pl.when(side == 1)
                def _():
                    (part_x, part_dy)[w][:cap, :] = ordered

            else:
                (out_x, out_dy)[w][cap_rows(b), :] = ordered
                if w == 0 and b == ORDER[1]:
                    pl.semaphore_wait(barrier, n - 1 + blocks - 1)
                per_kind(lambda kind: out_copy(w, b, kind).start())

    def await_block(w, kind, j):
        def wait():
            out_copy(w, 4 * (j // 2) + j % 2 + 2, kind).wait_recv()

        if j:
            wait()
        else:
            pl.when(side != kind)(wait)

    def seen_copy(b):
        return pltpu.make_async_remote_copy(
            src_ref=seen.at[0],
            dst_ref=seen.at[b],
            send_sem=seen_send.at[b],
            recv_sem=seen_recv.at[b],
            device_id={"exp": flip(e, b)},
            device_id_type=MESH,
        )

    def count_live():
        count = live_count(lengths_ref, r * blocks + e, n * blocks, rows)
        live = lax.broadcasted_iota(jnp.int32, (blocks, rows), 1) < count
        table = lax.broadcasted_iota(jnp.int32, (blocks, rows), 0)
        hits = jnp.where((table == routes_ref[...]) & live, 1.0, 0.0)
        seen[0] = jnp.broadcast_to(jnp.sum(hits, 1, keepdims=True), (blocks, 128))
        for b in range(1, blocks):
            seen_copy(b).start()

    def fullest():
        for b in range(1, blocks):
            seen_copy(b).wait_recv()
        total_seen = seen[0]
        for b in range(1, blocks):
            total_seen += seen[b]
        top[...] = jnp.max(total_seen, 0, keepdims=True)

    def make_pack():
        lane = lax.broadcasted_iota(jnp.int32, (1, 4 * cap), 1)
        target = jnp.zeros((1, 4 * cap), jnp.float32)
        before = jnp.zeros((1, 1), jnp.float32)
        for j in range(4):
            from_it = 4 * (j // 2) + j % 2 + 2 * (1 - side)
            count = seen[from_it, pl.ds(e, 1), 0:1]
            within = (lane - j * cap).astype(jnp.float32)
            here = (lane >= j * cap) & (lane < (j + 1) * cap)
            at = jnp.where(within < count, within + before, -1.0)
            target = jnp.where(here, at, target)
            before += count
        row = lax.broadcasted_iota(jnp.int32, (own_rows - 4 * cap, 4 * cap), 0)
        pack[...] = (row.astype(jnp.float32) == target).astype(jnp.bfloat16)

    def pack_middle(w):
        landed, packed = ((part_x, x_ref), (part_dy, dy_ref))[w]
        packed[middle, :] = jnp.dot(
            pack[...], landed[...], preferred_element_type=jnp.float32
        ).astype(jnp.bfloat16)

    def unpack_middle(w):
        landed, packed = ((part_x, y_ref), (part_dy, dv_ref))[w]
        landed[...] = contract_rows(pack[...], packed[middle, :]).astype(jnp.bfloat16)

    def at_half(stop):
        c, offset = divmod(stop - 1, chunk)
        return c, max(h for h in every if starts[h] <= offset)

    def send_home(w, j, kind):
        if j:
            home_copy(w, j, kind).start()
        else:
            pl.when(side == kind)(lambda: home_own_copy(w, kind).start())
            pl.when(side != kind)(lambda: home_copy(w, 0, kind).start())

    def go_home(w, c, h):
        if not inside:
            return
        for chunk_at in range(CHUNKS):
            done = [j for j in range(4) if at_half(full_at[j] + cap) == (chunk_at, h)]
            packed = at_half(own_rows - 2 * cap) == (chunk_at, h)
            if done or packed:

                @pl.when(c == chunk_at)
                def _():
                    for j in done:
                        send_home(w, j, 0)
                    if packed:
                        unpack_middle(w)
                        for j in range(4):
                            send_home(w, j, 1)

    def gate_of(x):
        return jax.nn.sigmoid(jnp.sum(x * cent_ref[...], -1, keepdims=True))

    def prepare(i, h):
        kind, c, slot = op_type(i), op_chunk(i), op_slot(i)

        block = block_of(h)

        def own(offset, value):
            gath[slot, r, pl.ds(offset, block), :] = value.astype(jnp.bfloat16)

        def source(offset):
            return pl.ds(pl.multiple_of(c * chunk + offset, 16), block)

        @pl.when(kind == 0)
        def _():
            over_blocks(
                h,
                lambda o: own(
                    o,
                    layer_stats(x_ref[source(o), :].astype(jnp.float32))[0] * gain_ref[0:1, :]
                    + nbias_ref[0:1, :],
                )
            )

        @pl.when(kind == 1)
        def _():
            over_blocks(
                h,
                lambda o: own(
                    o, layer_stats(state[source(o), :])[0] * gain_ref[1:2, :] + nbias_ref[1:2, :]
                )
            )

        @pl.when(kind == 2)
        def _():
            over_blocks(
                h,
                lambda o: own(
                    o,
                    gate_of(x_ref[source(o), :].astype(jnp.float32))
                    * dy_ref[source(o), :].astype(jnp.float32),
                )
            )

        @pl.when(kind == 3)
        def _():
            over_blocks(h, lambda o: own(o, state[source(o), :]))

    def norm_back(values, grad, k):
        unit, scale = layer_stats(values)
        accs[1 + k] += fold(grad * unit)
        accs[3 + k] += fold(grad)
        through = grad * gain_ref[k : k + 1, :]
        return scale * (
            through
            - jnp.mean(through, -1, keepdims=True)
            - unit * jnp.mean(through * unit, -1, keepdims=True)
        )

    def finish(i, h):
        kind, c = op_type(i), op_chunk(i)
        block = block_of(h)

        def source(offset):
            return pl.ds(pl.multiple_of(c * chunk + offset, 16), block)

        @pl.when(kind == 0)
        def _():
            def body(o):
                state[source(o), :] = (
                    x_ref[source(o), :].astype(jnp.float32)
                    + total[pl.ds(o, block), :]
                    + bout_ref[0:1, :]
                )

            over_blocks(h, body)

        @pl.when(kind == 1)
        def _():
            def body(o):
                x = x_ref[source(o), :].astype(jnp.float32)
                dy = dy_ref[source(o), :].astype(jnp.float32)
                upper = state[source(o), :] + total[pl.ds(o, block), :] + bout_ref[1:2, :]
                gate = gate_of(x)
                y_ref[source(o), :] = (gate * upper).astype(jnp.bfloat16)
                logit = jnp.sum(dy * upper, -1, keepdims=True) * gate * (1.0 - gate)
                dlog[source(o), :] = jnp.broadcast_to(logit, (block, dlog.shape[1]))
                accs[0] += fold(logit * x)

            over_blocks(h, body)
            for part_at in every if h is None else [h]:
                go_home(0, c, part_at)

        @pl.when(kind == 2)
        def _():
            def body(o):
                x = x_ref[source(o), :].astype(jnp.float32)
                top = gate_of(x) * dy_ref[source(o), :].astype(jnp.float32)
                middle = top + norm_back(state[source(o), :], total[pl.ds(o, block), :], 1)
                state[source(o), :] = middle
                accs[5] += fold(middle)
                accs[6] += fold(top)

            over_blocks(h, body)

        @pl.when(kind == 3)
        def _():
            def body(o):
                x = x_ref[source(o), :].astype(jnp.float32)
                dv_ref[source(o), :] = (
                    state[source(o), :]
                    + norm_back(x, total[pl.ds(o, block), :], 0)
                    + dlog[source(o), 0:1] * cent_ref[...]
                ).astype(jnp.bfloat16)

            over_blocks(h, body)
            for part_at in every if h is None else [h]:
                go_home(1, c, part_at)

    def item_first(i, par, p):
        kind = op_type(i)
        k = jnp.where((kind == 1) | (kind == 2), 1, 0)
        slot = jnp.where(
            kind == 2, op_slot(i - 1), jnp.where(kind == 3, op_chunk(i), op_slot(i))
        )

        inner = (
            jnp.dot(gath[slot, p], wi[k], preferred_element_type=jnp.float32)
            + bias_ref[pl.ds(k, 1), pl.ds(pl.multiple_of(r * hidden, hidden), hidden)]
        )
        low, pull = gelu_and_slope(inner)
        act[par, p] = low.astype(jnp.bfloat16)
        slope[...] = pull

    def item_pull(i, par, p):
        kind = op_type(i)
        k = jnp.where((kind == 1) | (kind == 2), 1, 0)

        @pl.when(kind >= 2)
        def _():
            grad = contract_cols(gath[op_slot(i), p], wo[k]) * slope[...]
            bacc[k] += fold(grad)
            dq[par, p] = grad.astype(jnp.bfloat16)

    def item_second(i, par, p):
        kind = op_type(i)
        k = jnp.where((kind == 1) | (kind == 2), 1, 0)

        @pl.when(kind < 2)
        def _():
            part[p] = jnp.dot(act[par, p], wo[k], preferred_element_type=jnp.float32)

        @pl.when(kind >= 2)
        def _():
            part[p] = contract_cols(dq[par, p], wi[k])

    def weight_grads(i, par, j):
        kind = op_type(i)
        k = jnp.where(kind == 2, 1, 0)
        slot = jnp.where(kind == 2, op_slot(i - 1), op_chunk(i))
        cs = pl.ds(pl.multiple_of(j * wtile, wtile), wtile)
        depth = n * chunk
        normed = gath[slot, :, :, cs].reshape(depth, wtile)
        gwi[k, cs, :] += contract_rows(normed, dq[par].reshape(depth, hidden))
        active = act[par, :, :, cs].reshape(depth, wtile)
        gwo[k, cs, :] += contract_rows(active, gath[op_slot(i)].reshape(depth, width))

    def item_at(s):
        near = jnp.minimum(r, last - r)
        base = jnp.where(near == 0, last - s, jnp.where(s < 2, last - s, s - 2))
        return jnp.where(r < 2, base, last - base)

    def cot_load():
        return pltpu.make_async_copy(cot_hbm, cot_ref, cot_sem)

    EARLY, LATE = (0, 2, 4, 5, 6), (1, 3)

    def tell(late, q):
        src, dst = ((mine, peers), (mine_late, peers_late))[late]
        return pltpu.make_async_remote_copy(
            src_ref=src,
            dst_ref=dst.at[q - 1],
            send_sem=peer_send.at[late, q - 1],
            recv_sem=peer_recv.at[late, q - 1],
            device_id={"rep": lax.rem(r + q, n)},
            device_id_type=MESH,
        )

    def tell_early():
        for a, row in enumerate(EARLY):
            mine[a : a + 1, :width] = jnp.sum(accs[row], 0, keepdims=True)
        mine[5:6, :hidden] = jnp.sum(bacc[1], 0, keepdims=True)
        mine[6:8, :] = jnp.zeros((2, mine.shape[1]), jnp.float32)
        if inside:
            mine[6:7, :128] = top[...]
        for q in range(1, n):
            tell(0, q).start()

    def tell_late():
        at = 0
        for values in (accs[LATE[0]], accs[LATE[1]], bacc[0]):
            flat = jnp.sum(values, 0, keepdims=True)
            for j in range(flat.shape[1] // 128):
                mine_late[at : at + 1, :] = flat[:, j * 128 : (j + 1) * 128]
                at += 1
        for q in range(1, n):
            tell(1, q).start()

    def unpack(packed, at, size):
        return jnp.concatenate([packed[at + j : at + j + 1] for j in range(size // 128)], 1)

    def load(w):
        src, dst = ((wi_hbm, wi), (wo_hbm, wo))[w]
        return pltpu.make_async_copy(src, dst, load_sem.at[w])

    barrier = pltpu.get_barrier_semaphore()
    for q in range(1, n):
        pl.semaphore_signal(
            barrier, inc=1, device_id={"rep": lax.rem(r + q, n)}, device_id_type=MESH
        )
    load(0).start()
    load(1).start()
    if inside:
        for b in range(1, blocks):
            pl.semaphore_signal(
                barrier, inc=1, device_id={"exp": flip(e, b)}, device_id_type=MESH
            )
        cot_load().start()
        place[...] = slot_rows(routes_ref[...], blocks, cap)
        dispatch(0, 0, 2)
        await_block(0, 0, 0)
    else:
        pl.semaphore_wait(barrier, n - 1)
    prepare(0, 0)

    def step(t, carry):
        k, s = t // n, lax.rem(t, n)
        k_before, s_before = (t - 1) // n, lax.rem(t + n - 1, n)
        i = k - 1
        par = lax.rem(k, 2)
        p = item_at(s)

        def exchange(h):
            for d in range(2):

                @pl.when(t >= 1)
                def _():
                    wait_received(d, k_before, s_before, h)

                @pl.when(t >= 2)
                def _():
                    wait_sent(d, (t - 2) // n, lax.rem(t + n - 2, n), h)

            @pl.when((s == 0) & (k >= 2))
            def _():
                finish_sum(k - 1, h)

            for d in range(2):
                send(d, k, s, h)

        def grads(j):
            old = k - 2

            @pl.when((s < 2) & (old >= CHUNKS) & (op_type(old) >= 2))
            def _():
                weight_grads(old, lax.rem(k + 1, 2), j)

        exchange(0)

        @pl.when(t == n * ops)
        def _():
            tell_early()

        @pl.when(t == 0)
        def _():
            if inside:
                dispatch(0, 2, blocks)
                await_block(0, 0, 2)
            for h in every[1:]:
                prepare(0, h)

        @pl.when(t == 1)
        def _():
            def clear(b, carry):
                zero_rows = pl.ds(pl.multiple_of(b * 64, 64), 64)
                for w in range(2):
                    gwi[w, zero_rows, :] = jnp.zeros((64, hidden), jnp.float32)
                    gwo[w, zero_rows, :] = jnp.zeros((64, width), jnp.float32)
                return carry

            lax.fori_loop(0, width // 64, clear, 0)
            accs[...] = jnp.zeros_like(accs)
            bacc[...] = jnp.zeros_like(bacc)

        if inside:

            @pl.when(t == 2)
            def _():
                cot_load().wait()
                dispatch(1, 0, blocks)

            @pl.when(t == 1)
            def _():
                count_live()

            @pl.when(t == 3)
            def _():
                fullest()
                make_pack()
                for kind, j in ((0, 1), (0, 3), (1, 0), (1, 1), (1, 2), (1, 3)):
                    await_block(0, kind, j)
                pack_middle(0)

            @pl.when(t == n * CHUNKS)
            def _():
                for w in range(2):
                    for b in range(1, blocks):
                        out_copy(w, b, 0).wait_send()
                for b in range(1, blocks):
                    seen_copy(b).wait_send()
                for kind in range(2):
                    for j in range(4):
                        await_block(1, kind, j)
                pack_middle(1)

        @pl.when(t == n)
        def _():
            load(0).wait()
            load(1).wait()

        pieces = [item_first, item_pull, item_second]
        for h in every:
            if h:
                exchange(h)
            mine_now = pieces[h : h + 1] if h < len(parts) - 1 else pieces[h:]
            if len(parts) == 2:
                mine_now = (pieces[:2], pieces[2:])[h]

            @pl.when(k >= 1)
            def _():
                for piece in mine_now:
                    piece(i, par, p)

            if h == 0:
                grads(2 * s)
            elif h == len(parts) - 1:
                grads(2 * s + 1)

        @pl.when((s == 2) & (k >= 2))
        def _():
            finish(k - 2, None)

        @pl.when((s == 3) & (k < ops - 1))
        def _():
            prepare(k + 1, None)

        return carry

    steps = rounds * n
    lax.fori_loop(0, steps, step, 0)

    def last_grads(j, carry):
        weight_grads(ops - 1, (rounds - 1) % 2, j)
        return carry

    lax.fori_loop(0, 4, last_grads, 0)
    for h in every:
        for d in range(2):
            wait_received(d, rounds - 1, n - 1, h)
        finish_sum(rounds - 1, h)
        finish(ops - 1, h)
    for h in every:
        for d in range(2):
            for back in (2, 1):
                wait_sent(d, (steps - back) // n, (steps - back) % n, h)

    tell_late()

    def place_bins(k, q, bins):
        bin_out[k : k + 1, pl.ds(pl.multiple_of(q * hidden, hidden), hidden)] = bins

    for q in range(1, n):
        tell(0, q).wait_recv()
    sums = mine[0:5, :width]
    place_bins(1, r, mine[5:6, :hidden])
    for q in range(1, n):
        sums += peers[q - 1, 0:5, :width]
        place_bins(1, lax.rem(r - q + n, n), peers[q - 1, 5:6, :hidden])
    cent_out[...] = sums[0:1]
    gain_out[1:2, :] = sums[1:2]
    nbias_out[1:2, :] = sums[2:3]
    bout_out[...] = sums[3:5]
    if inside:
        most = mine[6:7, :128]
        for q in range(1, n):
            most = jnp.maximum(most, peers[q - 1, 6:7, :128])
        top_out[...] = jnp.broadcast_to(most, top_out.shape)
    for q in range(1, n):
        tell(1, q).wait_recv()
    mine_rows = mine_late[...]
    late = mine_rows[: 2 * width // 128]
    place_bins(0, r, unpack(mine_rows, 2 * width // 128, hidden))
    for q in range(1, n):
        theirs = peers_late[q - 1]
        late += theirs[: 2 * width // 128]
        place_bins(0, lax.rem(r - q + n, n), unpack(theirs, 2 * width // 128, hidden))
    gain_out[0:1, :] = unpack(late, 0, width)
    nbias_out[0:1, :] = unpack(late, width // 128, width)
    for q in range(1, n):
        tell(0, q).wait_send()
        tell(1, q).wait_send()
    if inside:
        for w in range(2):
            for kind in range(2):
                for j in range(4):
                    if j:
                        home_copy(w, j, kind).wait_send()
                    else:
                        pl.when(side == kind)(lambda: home_own_copy(w, kind).wait())
                        pl.when(side != kind)(lambda: home_copy(w, 0, kind).wait_send())
            for j in range(4):
                for expert_side in range(2):
                    if j:
                        await_home(w, j, expert_side)
                    else:
                        pl.when(side != expert_side)(
                            functools.partial(await_home, w, j, expert_side)
                        )


def run_layer(own_rows, name, inside, rows_in, gains, nbias, cent, biases, bout, wi, wo):
    n, blocks = lax.axis_size("rep"), lax.axis_size("exp")
    rows, width = rows_in[0].shape
    hidden = wi.shape[2]
    parts = PLANS[own_rows] if inside else (rows // 8, rows // 8)
    chunk = sum(parts)
    CHUNKS = own_rows // chunk
    wide = max(width, hidden)
    late = (2 * width + hidden) // 128
    low, full = jnp.bfloat16, jnp.float32
    vmem = pl.BlockSpec(memory_space=pltpu.VMEM)
    anywhere = pl.BlockSpec(memory_space=pl.ANY)
    row_specs = [vmem] * 2
    extra = []
    if inside:
        row_specs = [vmem, anywhere, vmem, pl.BlockSpec(memory_space=pltpu.SMEM)]
        extra = (
            [pltpu.VMEM((own_rows, width), low)] * 2
            + [pltpu.VMEM((rows, width), low)] * 2
            + [pltpu.VMEM((rows, rows), low)]
            + [pltpu.VMEM((rows, width), low)]
            + [pltpu.VMEM((rows // 2, width), low)] * 2
            + [pltpu.VMEM((own_rows - rows // 2, rows // 2), low)]
            + [pltpu.VMEM((blocks, blocks, 128), full), pltpu.VMEM((1, 128), full)]
            + [pltpu.SemaphoreType.DMA((2, blocks)), pltpu.SemaphoreType.DMA((2, 2, blocks // 2))]
            + [pltpu.SemaphoreType.DMA((2, 2, blocks // 2))] * 2
            + [pltpu.SemaphoreType.DMA((2,)), pltpu.SemaphoreType.DMA]
            + [pltpu.SemaphoreType.DMA((blocks,))] * 2
        )
    flops = 2 * 16 * n * own_rows * width * hidden
    return pl.pallas_call(
        functools.partial(kernel, n, blocks, inside, parts),
        out_shape=(
            pltpu.VMEM((rows, width), low) if inside else jax.ShapeDtypeStruct((rows, width), low),
            pltpu.VMEM((rows, width), low) if inside else jax.ShapeDtypeStruct((rows, width), low),
            pltpu.VMEM((2, width, hidden), full),
            pltpu.VMEM((2, hidden, width), full),
            jax.ShapeDtypeStruct((1, width), full),
            jax.ShapeDtypeStruct((2, width), full),
            jax.ShapeDtypeStruct((2, width), full),
            jax.ShapeDtypeStruct((2, n * hidden), full),
            jax.ShapeDtypeStruct((2, width), full),
        )
        + ((jax.ShapeDtypeStruct((8, 128), full),) if inside else ()),
        in_specs=row_specs + [vmem] * 5 + [anywhere] * 2,
        out_specs=(vmem,) * (10 if inside else 9),
        scratch_shapes=[
            pltpu.VMEM((CHUNKS + POOL, n, chunk, width), low),
            pltpu.VMEM((2, width, hidden), low),
            pltpu.VMEM((2, hidden, width), low),
            pltpu.VMEM((n, chunk, width), full),
            pltpu.VMEM((2, n, chunk, hidden), low),
            pltpu.VMEM((2, n, chunk, hidden), low),
            pltpu.VMEM((chunk, hidden), full),
            pltpu.VMEM((chunk, width), full),
            pltpu.VMEM((own_rows, width), full),
            pltpu.VMEM((own_rows, 128), full),
            pltpu.VMEM((2, 2, n, chunk, width), low),
            pltpu.VMEM((2, 2, chunk, width), low),
            pltpu.VMEM((7, 8, width), full),
            pltpu.VMEM((2, 8, hidden), full),
            pltpu.VMEM((8, wide), full),
            pltpu.VMEM((n - 1, 8, wide), full),
            pltpu.VMEM((late, 128), full),
            pltpu.VMEM((n - 1, late, 128), full),
            pltpu.SemaphoreType.DMA((2, 2, len(parts))),
            pltpu.SemaphoreType.DMA((2, 2, n, len(parts))),
            pltpu.SemaphoreType.DMA((2,)),
            pltpu.SemaphoreType.DMA((2, n - 1)),
            pltpu.SemaphoreType.DMA((2, n - 1)),
        ]
        + extra,
        compiler_params=pltpu.CompilerParams(
            collective_id=name, has_side_effects=True, vmem_limit_bytes=VMEM_BYTES
        ),
        cost_estimate=pl.CostEstimate(
            flops=flops, bytes_accessed=40 * rows * width, transcendentals=8 * rows * hidden * n
        ),
    )(*rows_in, gains, nbias, cent, biases, bout, wi, wo)


def close_kernel(device_count, cap, *refs):
    tok_hbm, cot_hbm, routes_ref, lengths_ref, y, dv, gwi_in, gwo_in = refs[:8]
    small_in, refs = refs[8:13], refs[13:]
    mixed_ref, grad_ref, gwi_out, gwo_out = refs[:4]
    small_out, refs = refs[4:9], refs[9:]
    tok, cot, load_sem, move_sem = refs
    rows = tok.shape[0]
    loads = [
        pltpu.make_async_copy(src, dst, load_sem.at[j])
        for j, (src, dst) in enumerate(((tok_hbm, tok), (cot_hbm, cot)))
    ]
    moves = [
        pltpu.make_async_copy(src.at[k], dst.at[k], move_sem.at[w, k])
        for w, (src, dst) in enumerate(((gwi_in, gwi_out), (gwo_in, gwo_out)))
        for k in range(2)
    ]
    for copy in loads + moves:
        copy.start()
    for src, dst in zip(small_in, small_out):
        dst[...] = src[...]
    place = slot_rows(routes_ref[...], rows // cap, cap)
    device = lax.axis_index("rep") * lax.axis_size("exp") + lax.axis_index("exp")
    live = live_rows(lengths_ref, device, device_count, rows)
    for copy in loads:
        copy.wait()
    mixed_ref[...] = (tok[...].astype(jnp.float32) + live * contract_rows(place, y[...])).astype(
        jnp.bfloat16
    )
    grad_ref[...] = (cot[...].astype(jnp.float32) + contract_rows(place, dv[...])).astype(
        jnp.bfloat16
    )
    for copy in moves:
        copy.wait()


def close(tokens, cotangent, routes, lengths, home_y, home_dv, gwi, gwo, *small):
    n, blocks = lax.axis_size("rep"), lax.axis_size("exp")
    rows, width = tokens.shape
    vmem = pl.BlockSpec(memory_space=pltpu.VMEM)
    anywhere = pl.BlockSpec(memory_space=pl.ANY)
    rows_shape = jax.ShapeDtypeStruct(tokens.shape, tokens.dtype)
    like = lambda a: jax.ShapeDtypeStruct(a.shape, a.dtype)
    home_y, home_dv, gwi, gwo = (
        pltpu.with_memory_space_constraint(a, pltpu.VMEM) for a in (home_y, home_dv, gwi, gwo)
    )
    return pl.pallas_call(
        functools.partial(close_kernel, n * blocks, rows // blocks),
        out_shape=(rows_shape, rows_shape, like(gwi), like(gwo), *map(like, small)),
        in_specs=[anywhere, anywhere, vmem, pl.BlockSpec(memory_space=pltpu.SMEM)]
        + [vmem] * 9,
        out_specs=[vmem, vmem, anywhere, anywhere] + [vmem] * 5,
        scratch_shapes=[pltpu.VMEM((rows, width), tokens.dtype)] * 2
        + [pltpu.SemaphoreType.DMA((2,)), pltpu.SemaphoreType.DMA((2, 2))],
        compiler_params=pltpu.CompilerParams(vmem_limit_bytes=VMEM_BYTES),
    )(tokens, cotangent, routes, lengths, home_y, home_dv, gwi, gwo, *small)


def no_results(shapes):
    def kernel(*refs):
        refs[-1][...] = jnp.zeros_like(refs[-1])

    anywhere = pl.BlockSpec(memory_space=pl.ANY)
    *results, _ = pl.pallas_call(
        kernel,
        out_shape=(*shapes, jax.ShapeDtypeStruct((8, 128), jnp.float32)),
        out_specs=[anywhere] * len(shapes) + [pl.BlockSpec(memory_space=pltpu.VMEM)],
    )()
    return tuple(results)


def shards(
    tokens,
    routes,
    lengths,
    centroids,
    norm_gains,
    norm_biases,
    w_in,
    in_biases,
    w_out,
    out_biases,
    cotangent,
):
    n_exp = lax.axis_size("exp")
    tok_rows = tokens.shape[0]
    cap = tok_rows // n_exp
    params = (
        norm_gains[0],
        norm_biases[0],
        centroids,
        in_biases[0],
        out_biases[0],
        w_in[0],
        w_out[0],
    )
    devices = n_exp * lax.axis_size("rep")
    if n_exp == 8 and tok_rows == max(PLANS) and devices == 4 * lengths.shape[0]:
        less, whole = sorted(PLANS)
        given = (tokens, cotangent, routes.reshape(1, tok_rows), lengths)

        def layer(own_rows, name, given, *params):
            *results, most = run_layer(own_rows, name, True, given, *params)
            return tuple(close(*given, *results)), most[0, 0] <= own_rows

        seqs, planes = lengths.shape[0], lax.axis_size("rep")
        of_plane = lax.iota(jnp.int32, seqs) // (seqs // planes) == lax.iota(jnp.int32, planes)[:, None]
        plane_live = jnp.sum(jnp.where(of_plane, lengths, 0), 1)
        shapes = jax.eval_shape(functools.partial(layer, less, 0), given, *params)[0]
        results, done = lax.cond(
            jnp.max(plane_live) <= (less - SPARE) * n_exp,
            functools.partial(layer, less, 0),
            lambda *_: (no_results(shapes), jnp.array(False)),
            given,
            *params,
        )
        results = lax.cond(
            done,
            lambda results, *_: results,
            lambda results, *rest: layer(whole, 1, *rest)[0],
            results,
            given,
            *params,
        )
    else:
        device = lax.axis_index(("rep", "exp"))
        slot = tok_rows * n_exp * lax.axis_size("rep") // lengths.shape[0]
        positions = device * tok_rows + lax.iota(jnp.int32, tok_rows)
        seq_ids = positions // slot
        seq_table = lax.iota(jnp.int32, lengths.shape[0])
        seq_len = jnp.sum(
            jnp.where(seq_ids[:, None] == seq_table[None, :], lengths[None, :], 0), 1
        )
        live = (positions % slot < seq_len).astype(jnp.float32)[:, None]
        route = routes[:, 0]
        hits = (route[:, None] == lax.iota(jnp.int32, n_exp)[None, :]).astype(jnp.int32)
        before = jnp.cumsum(hits, 0) - hits
        target = route * cap + jnp.sum(before * hits, 1)
        place = (lax.iota(jnp.int32, tok_rows)[:, None] == target[None, :]).astype(jnp.bfloat16)
        grad_out = (live * cotangent.astype(jnp.float32)).astype(jnp.bfloat16)

        def send(rows):
            ordered = jnp.dot(place, rows, preferred_element_type=jnp.float32).astype(jnp.bfloat16)
            return lax.all_to_all(ordered, "exp", split_axis=0, concat_axis=0, tiled=True)

        def give_back(rows):
            back = lax.all_to_all(rows, "exp", split_axis=0, concat_axis=0, tiled=True)
            return contract_rows(place, back)

        given = (send(tokens), send(grad_out))
        result, grad_local, *rest = run_layer(tok_rows, 0, False, given, *params)
        mixed = (tokens.astype(jnp.float32) + live * give_back(result)).astype(jnp.bfloat16)
        tokens_grad = (cotangent.astype(jnp.float32) + give_back(grad_local)).astype(jnp.bfloat16)
        results = (mixed, tokens_grad, *rest)
    mixed, tokens_grad, gwi, gwo, cent_grad, gain_grad, nbias_grad, bin_grad, bout_grad = results
    return (
        mixed,
        tokens_grad,
        cent_grad,
        gain_grad[None],
        nbias_grad[None],
        gwi[None],
        bin_grad[None],
        gwo[None],
        bout_grad[None],
    )


def solution(mesh):
    placed = (
        P(("rep", "exp"), None),
        P(("rep", "exp"), None),
        P(),
        P("exp", None),
        P("exp", None, None),
        P("exp", None, None),
        P("exp", None, None, "rep"),
        P("exp", None, None),
        P("exp", None, "rep", None),
        P("exp", None, None),
        P(("rep", "exp"), None),
    )
    return jax.shard_map(
        shards,
        mesh=mesh,
        in_specs=placed,
        out_specs=(
            P(("rep", "exp"), None),
            P(("rep", "exp"), None),
            P("exp", None),
            P("exp", None, None),
            P("exp", None, None),
            P("exp", None, None, "rep"),
            P("exp", None, None),
            P("exp", None, "rep", None),
            P("exp", None, None),
        ),
        check_vma=False,
    )
```

```python
import functools

import jax
import jax.numpy as jnp
from jax import lax
from jax.experimental import pallas as pl
from jax.experimental.pallas import tpu as pltpu
from jax.sharding import PartitionSpec as P

eps = 1e-05
VMEM_BYTES = 44 * 1024 * 1024


def contract_rows(left, right):
    return lax.dot_general(
        left, right, (((0,), (0,)), ((), ())), preferred_element_type=jnp.float32
    )


def contract_cols(left, right):
    return lax.dot_general(
        left, right, (((1,), (1,)), ((), ())), preferred_element_type=jnp.float32
    )


MESH = pl.DeviceIdType.MESH
POOL = 4
PLANS = {448: (32, 32, 32, 16), 512: (64, 64)}
SPARE = 16
ORDER = (0, 2, 4, 6, 5, 7, 3, 1)
ROOT = 0.7978845608028654
CUBE = 0.044715


def layer_stats(values):
    center = values - jnp.mean(values, -1, keepdims=True)
    spread = jnp.mean(center * center, -1, keepdims=True)
    scale = lax.rsqrt(spread + eps)
    return center * scale, scale


def gelu_and_slope(inner):
    square = inner * inner
    bent = jnp.tanh(inner * (ROOT + (ROOT * CUBE) * square))
    half = 0.5 * (1.0 + bent)
    slope = half + (0.5 * inner) * (1.0 - bent * bent) * (ROOT + (3.0 * ROOT * CUBE) * square)
    return inner * half, slope


def fold(rows):
    return jnp.sum(rows.reshape(rows.shape[0] // 8, 8, rows.shape[1]), 0)


def pair_of(b):
    return (b >> 2) * 2 + (b & 1)


def flip(index, bits):
    out, place = index, 1
    while place <= bits:
        if bits & place:
            out = out + place * (1 - 2 * lax.rem(index // place, 2))
        place *= 2
    return out


def slot_rows(routes, blocks, cap):
    rows = routes.shape[1]
    along = routes.astype(jnp.float32)
    table = lax.broadcasted_iota(jnp.int32, (max(blocks, 8), rows), 0).astype(jnp.float32)
    hits = (table == along).astype(jnp.float32)
    first = lax.broadcasted_iota(jnp.int32, (rows, rows), 0)
    second = lax.broadcasted_iota(jnp.int32, (rows, rows), 1)
    earlier = (first < second).astype(jnp.bfloat16)
    before = jnp.dot(hits.astype(jnp.bfloat16), earlier, preferred_element_type=jnp.float32)
    target = along * cap + jnp.sum(before * hits, 0, keepdims=True)
    return (first.astype(jnp.float32) == target).astype(jnp.bfloat16)


def live_count(lengths_ref, device, devices, rows):
    slot = rows * devices // lengths_ref.shape[0]
    start = device * rows
    return lengths_ref[start // slot] - lax.rem(start, slot)


def live_rows(lengths_ref, device, devices, rows):
    count = live_count(lengths_ref, device, devices, rows)
    return (lax.broadcasted_iota(jnp.int32, (rows, 1), 0) < count).astype(jnp.float32)


def kernel(n, blocks, inside, parts, *refs):
    refs = list(refs)
    take = lambda count: [refs.pop(0) for _ in range(count)]
    if inside:
        tok_ref, cot_hbm, routes_ref, lengths_ref = take(4)
    else:
        x_ref, dy_ref = take(2)
    gain_ref, nbias_ref, cent_ref, bias_ref, bout_ref, wi_hbm, wo_hbm = take(7)
    home_y, home_dv, gwi, gwo, cent_out, gain_out, nbias_out, bin_out, bout_out = take(9)
    top_out = take(1)[0] if inside else None
    gath, wi, wo, part, act, dq, slope, total, state, dlog, recv, stage = take(12)
    accs, bacc, mine, peers, mine_late, peers_late = take(6)
    send_sem, recv_sem, load_sem, peer_send, peer_recv = take(5)
    if inside:
        x_ref, dy_ref, y_ref, dv_ref, place, cot_ref, part_x, part_dy, pack, seen, top = take(11)
        out_x, out_dy = y_ref, dv_ref
        out_send, out_recv, home_send, home_recv, home_own, cot_sem = take(6)
        seen_send, seen_recv = take(2)
    else:
        y_ref, dv_ref = home_y, home_dv
    r = lax.axis_index("rep")
    e = lax.axis_index("exp")
    own_rows, width = x_ref.shape
    hidden = wi_hbm.shape[2]
    rows = home_y.shape[0]
    cap = rows // blocks
    chunk = sum(parts)
    CHUNKS = own_rows // chunk
    starts = [sum(parts[:h]) for h in range(len(parts))]
    every = range(len(parts))
    ops = 4 * CHUNKS
    rounds = ops + 1
    wtile = hidden // 4
    last = n - 1

    def op_type(i):
        return jnp.where(i < CHUNKS, 0, jnp.where(i >= 3 * CHUNKS, 3, 1 + lax.rem(i + CHUNKS, 2)))

    def op_chunk(i):
        return jnp.where(
            i < CHUNKS, i, jnp.where(i >= 3 * CHUNKS, i - 3 * CHUNKS, (i - CHUNKS) // 2)
        )

    def op_slot(i):
        return jnp.where(i < CHUNKS, i, CHUNKS + lax.rem(i, POOL))

    def half_rows(h):
        return pl.ds(starts[h], parts[h])

    def extent(h):
        return (0, chunk) if h is None else (starts[h], parts[h])

    def block_of(h):
        return 32 if extent(h)[1] % 32 == 0 else 16

    ahead = (jnp.minimum(r + 1, last), jnp.maximum(r - 1, 0))
    pos = (r, last - r)

    def item_sent(d, s):
        return lax.rem(r - s + n, n) if d == 0 else lax.rem(r + s, n)

    def sends(d, k, s):
        return (pos[d] < last) & jnp.where(s <= pos[d], k < ops, k >= 1)

    def receives(d, k, s):
        return (pos[d] > 0) & jnp.where(s <= pos[d] - 1, k < ops, k >= 1)

    def copy(d, k, s, h, src, dst):
        return pltpu.make_async_remote_copy(
            src_ref=src,
            dst_ref=dst,
            send_sem=send_sem.at[d, lax.rem(s, 2), h],
            recv_sem=recv_sem.at[d, lax.rem(k, 2), s, h],
            device_id={"rep": ahead[d]},
            device_id_type=MESH,
        )

    def landing(d, k, s, h):
        return recv.at[d, lax.rem(k, 2), s, half_rows(h)]

    def staged(d, s, h):
        return stage.at[d, lax.rem(s, 2), half_rows(h)]

    def wait_sent(d, k, s, h):
        @pl.when(sends(d, k, s))
        def _():
            copy(d, k, s, h, staged(d, s, h), landing(d, k, s, h)).wait_send()

    def wait_received(d, k, s, h):
        @pl.when(receives(d, k, s))
        def _():
            copy(d, k, s, h, staged(d, s, h), landing(d, k, s, h)).wait_recv()

    def finish_sum(k, h):
        rs = half_rows(h)
        total[rs, :] = part[r, rs, :]
        for d in range(2):

            @pl.when(pos[d] > 0)
            def _():
                total[rs, :] += landing(d, k, n - 1, h)[...].astype(jnp.float32)

    def send(d, k, s, h):
        gathers = s <= pos[d]
        p = item_sent(d, s)
        rs = half_rows(h)

        @pl.when(sends(d, k, s) & gathers)
        def _():
            here = gath.at[op_slot(k), p, rs]
            copy(d, k, s, h, here, here).start()

        @pl.when(sends(d, k, s) & jnp.logical_not(gathers))
        def _():
            out = staged(d, s, h)

            @pl.when(pos[d] == 0)
            def _():
                out[...] = part[p, rs, :].astype(jnp.bfloat16)

            @pl.when(pos[d] > 0)
            def _():
                came = landing(d, k, s - 1, h)[...].astype(jnp.float32)
                out[...] = (part[p, rs, :] + came).astype(jnp.bfloat16)

            copy(d, k, s, h, out, landing(d, k, s, h)).start()

    def over_blocks(h, body):
        size = block_of(h)

        def step(b, carry):
            body(pl.multiple_of(extent(h)[0] + b * size, 16))
            return carry

        lax.fori_loop(0, extent(h)[1] // size, step, 0)

    side = lax.rem(e // 2, 2)
    full_at = (0, own_rows - cap, cap, own_rows - 2 * cap)
    middle = pl.ds(2 * cap, own_rows - 4 * cap)

    def cap_rows(q):
        return pl.ds(pl.multiple_of(q * cap, cap), cap)

    def out_copy(w, b, kind):
        j = pair_of(b)
        src = (out_x, out_dy)[w]
        dst = ((x_ref, part_x), (dy_ref, part_dy))[w][kind]
        return pltpu.make_async_remote_copy(
            src_ref=src.at[cap_rows(b)],
            dst_ref=dst.at[pl.ds((full_at[j], j * cap)[kind], cap)],
            send_sem=out_send.at[w, b],
            recv_sem=out_recv.at[w, kind, j],
            device_id={"exp": flip(e, b)},
            device_id_type=MESH,
        )

    def results_of(w, j, kind):
        src = ((y_ref, part_x), (dv_ref, part_dy))[w][kind]
        return src.at[pl.ds((full_at[j], j * cap)[kind], cap)]

    def home_copy(w, j, kind):
        return pltpu.make_async_remote_copy(
            src_ref=results_of(w, j, kind),
            dst_ref=(home_y, home_dv)[w].at[cap_rows(e)],
            send_sem=home_send.at[w, kind, j],
            recv_sem=home_recv.at[w, side, j],
            device_id={"exp": flip(e, 4 * (j // 2) + j % 2) + 2 * (kind - side)},
            device_id_type=MESH,
        )

    def home_own_copy(w, kind):
        dst = (home_y, home_dv)[w].at[cap_rows(e)]
        return pltpu.make_async_copy(results_of(w, 0, kind), dst, home_own.at[w])

    def await_home(w, j, expert_side):
        pltpu.make_async_remote_copy(
            src_ref=part_x.at[pl.ds(0, cap)],
            dst_ref=(home_y, home_dv)[w].at[cap_rows(0)],
            send_sem=home_send.at[w, 0, j],
            recv_sem=home_recv.at[w, expert_side, j],
            device_id={"exp": flip(e, 1)},
            device_id_type=MESH,
        ).wait_recv()

    def per_kind(body):
        for kind in range(2):

            @pl.when(side == kind)
            def _():
                body(kind)

    def dispatch(w, first, stop):
        values = (tok_ref, cot_ref)[w][...]
        if w == 1:
            device = r * blocks + e
            live = live_rows(lengths_ref, device, n * blocks, rows)
            values = (live * values.astype(jnp.float32)).astype(jnp.bfloat16)
        for b in ORDER[first:stop]:
            picked = place[cap_rows(flip(e, b)), :]
            ordered = jnp.dot(picked, values, preferred_element_type=jnp.float32)
            ordered = ordered.astype(jnp.bfloat16)
            if b == 0:

                @pl.when(side == 0)
                def _():
                    (x_ref, dy_ref)[w][:cap, :] = ordered

                @pl.when(side == 1)
                def _():
                    (part_x, part_dy)[w][:cap, :] = ordered

            else:
                (out_x, out_dy)[w][cap_rows(b), :] = ordered
                if w == 0 and b == ORDER[1]:
                    pl.semaphore_wait(barrier, n - 1 + blocks - 1)
                per_kind(lambda kind: out_copy(w, b, kind).start())

    def await_block(w, kind, j):
        def wait():
            out_copy(w, 4 * (j // 2) + j % 2 + 2, kind).wait_recv()

        if j:
            wait()
        else:
            pl.when(side != kind)(wait)

    def seen_copy(b):
        return pltpu.make_async_remote_copy(
            src_ref=seen.at[0],
            dst_ref=seen.at[b],
            send_sem=seen_send.at[b],
            recv_sem=seen_recv.at[b],
            device_id={"exp": flip(e, b)},
            device_id_type=MESH,
        )

    def count_live():
        count = live_count(lengths_ref, r * blocks + e, n * blocks, rows)
        live = lax.broadcasted_iota(jnp.int32, (blocks, rows), 1) < count
        table = lax.broadcasted_iota(jnp.int32, (blocks, rows), 0)
        hits = jnp.where((table == routes_ref[...]) & live, 1.0, 0.0)
        seen[0] = jnp.broadcast_to(jnp.sum(hits, 1, keepdims=True), (blocks, 128))
        for b in range(1, blocks):
            seen_copy(b).start()

    def fullest():
        for b in range(1, blocks):
            seen_copy(b).wait_recv()
        total_seen = seen[0]
        for b in range(1, blocks):
            total_seen += seen[b]
        top[...] = jnp.max(total_seen, 0, keepdims=True)

    def make_pack():
        lane = lax.broadcasted_iota(jnp.int32, (1, 4 * cap), 1)
        target = jnp.zeros((1, 4 * cap), jnp.float32)
        before = jnp.zeros((1, 1), jnp.float32)
        for j in range(4):
            from_it = 4 * (j // 2) + j % 2 + 2 * (1 - side)
            count = seen[from_it, pl.ds(e, 1), 0:1]
            within = (lane - j * cap).astype(jnp.float32)
            here = (lane >= j * cap) & (lane < (j + 1) * cap)
            at = jnp.where(within < count, within + before, -1.0)
            target = jnp.where(here, at, target)
            before += count
        row = lax.broadcasted_iota(jnp.int32, (own_rows - 4 * cap, 4 * cap), 0)
        pack[...] = (row.astype(jnp.float32) == target).astype(jnp.bfloat16)

    def pack_middle(w):
        landed, packed = ((part_x, x_ref), (part_dy, dy_ref))[w]
        packed[middle, :] = jnp.dot(
            pack[...], landed[...], preferred_element_type=jnp.float32
        ).astype(jnp.bfloat16)

    def unpack_middle(w):
        landed, packed = ((part_x, y_ref), (part_dy, dv_ref))[w]
        landed[...] = contract_rows(pack[...], packed[middle, :]).astype(jnp.bfloat16)

    def at_half(stop):
        c, offset = divmod(stop - 1, chunk)
        return c, max(h for h in every if starts[h] <= offset)

    def send_home(w, j, kind):
        if j:
            home_copy(w, j, kind).start()
        else:
            pl.when(side == kind)(lambda: home_own_copy(w, kind).start())
            pl.when(side != kind)(lambda: home_copy(w, 0, kind).start())

    def go_home(w, c, h):
        if not inside:
            return
        for chunk_at in range(CHUNKS):
            done = [j for j in range(4) if at_half(full_at[j] + cap) == (chunk_at, h)]
            packed = at_half(own_rows - 2 * cap) == (chunk_at, h)
            if done or packed:

                @pl.when(c == chunk_at)
                def _():
                    for j in done:
                        send_home(w, j, 0)
                    if packed:
                        unpack_middle(w)
                        for j in range(4):
                            send_home(w, j, 1)

    def gate_of(x):
        return jax.nn.sigmoid(jnp.sum(x * cent_ref[...], -1, keepdims=True))

    def prepare(i, h):
        kind, c, slot = op_type(i), op_chunk(i), op_slot(i)

        block = block_of(h)

        def own(offset, value):
            gath[slot, r, pl.ds(offset, block), :] = value.astype(jnp.bfloat16)

        def source(offset):
            return pl.ds(pl.multiple_of(c * chunk + offset, 16), block)

        @pl.when(kind == 0)
        def _():
            over_blocks(
                h,
                lambda o: own(
                    o,
                    layer_stats(x_ref[source(o), :].astype(jnp.float32))[0] * gain_ref[0:1, :]
                    + nbias_ref[0:1, :],
                )
            )

        @pl.when(kind == 1)
        def _():
            over_blocks(
                h,
                lambda o: own(
                    o, layer_stats(state[source(o), :])[0] * gain_ref[1:2, :] + nbias_ref[1:2, :]
                )
            )

        @pl.when(kind == 2)
        def _():
            over_blocks(
                h,
                lambda o: own(
                    o,
                    gate_of(x_ref[source(o), :].astype(jnp.float32))
                    * dy_ref[source(o), :].astype(jnp.float32),
                )
            )

        @pl.when(kind == 3)
        def _():
            over_blocks(h, lambda o: own(o, state[source(o), :]))

    def norm_back(values, grad, k):
        unit, scale = layer_stats(values)
        accs[1 + k] += fold(grad * unit)
        accs[3 + k] += fold(grad)
        through = grad * gain_ref[k : k + 1, :]
        return scale * (
            through
            - jnp.mean(through, -1, keepdims=True)
            - unit * jnp.mean(through * unit, -1, keepdims=True)
        )

    def finish(i, h):
        kind, c = op_type(i), op_chunk(i)
        block = block_of(h)

        def source(offset):
            return pl.ds(pl.multiple_of(c * chunk + offset, 16), block)

        @pl.when(kind == 0)
        def _():
            def body(o):
                state[source(o), :] = (
                    x_ref[source(o), :].astype(jnp.float32)
                    + total[pl.ds(o, block), :]
                    + bout_ref[0:1, :]
                )

            over_blocks(h, body)

        @pl.when(kind == 1)
        def _():
            def body(o):
                x = x_ref[source(o), :].astype(jnp.float32)
                dy = dy_ref[source(o), :].astype(jnp.float32)
                upper = state[source(o), :] + total[pl.ds(o, block), :] + bout_ref[1:2, :]
                gate = gate_of(x)
                y_ref[source(o), :] = (gate * upper).astype(jnp.bfloat16)
                logit = jnp.sum(dy * upper, -1, keepdims=True) * gate * (1.0 - gate)
                dlog[source(o), :] = jnp.broadcast_to(logit, (block, dlog.shape[1]))
                accs[0] += fold(logit * x)

            over_blocks(h, body)
            for part_at in every if h is None else [h]:
                go_home(0, c, part_at)

        @pl.when(kind == 2)
        def _():
            def body(o):
                x = x_ref[source(o), :].astype(jnp.float32)
                top = gate_of(x) * dy_ref[source(o), :].astype(jnp.float32)
                middle = top + norm_back(state[source(o), :], total[pl.ds(o, block), :], 1)
                state[source(o), :] = middle
                accs[5] += fold(middle)
                accs[6] += fold(top)

            over_blocks(h, body)

        @pl.when(kind == 3)
        def _():
            def body(o):
                x = x_ref[source(o), :].astype(jnp.float32)
                dv_ref[source(o), :] = (
                    state[source(o), :]
                    + norm_back(x, total[pl.ds(o, block), :], 0)
                    + dlog[source(o), 0:1] * cent_ref[...]
                ).astype(jnp.bfloat16)

            over_blocks(h, body)
            for part_at in every if h is None else [h]:
                go_home(1, c, part_at)

    def item_first(i, par, p):
        kind = op_type(i)
        k = jnp.where((kind == 1) | (kind == 2), 1, 0)
        slot = jnp.where(
            kind == 2, op_slot(i - 1), jnp.where(kind == 3, op_chunk(i), op_slot(i))
        )

        inner = (
            jnp.dot(gath[slot, p], wi[k], preferred_element_type=jnp.float32)
            + bias_ref[pl.ds(k, 1), pl.ds(pl.multiple_of(r * hidden, hidden), hidden)]
        )
        low, pull = gelu_and_slope(inner)
        act[par, p] = low.astype(jnp.bfloat16)
        slope[...] = pull

    def item_pull(i, par, p):
        kind = op_type(i)
        k = jnp.where((kind == 1) | (kind == 2), 1, 0)

        @pl.when(kind >= 2)
        def _():
            grad = contract_cols(gath[op_slot(i), p], wo[k]) * slope[...]
            bacc[k] += fold(grad)
            dq[par, p] = grad.astype(jnp.bfloat16)

    def item_second(i, par, p):
        kind = op_type(i)
        k = jnp.where((kind == 1) | (kind == 2), 1, 0)

        @pl.when(kind < 2)
        def _():
            part[p] = jnp.dot(act[par, p], wo[k], preferred_element_type=jnp.float32)

        @pl.when(kind >= 2)
        def _():
            part[p] = contract_cols(dq[par, p], wi[k])

    def weight_grads(i, par, j):
        kind = op_type(i)
        k = jnp.where(kind == 2, 1, 0)
        slot = jnp.where(kind == 2, op_slot(i - 1), op_chunk(i))
        cs = pl.ds(pl.multiple_of(j * wtile, wtile), wtile)
        depth = n * chunk
        normed = gath[slot, :, :, cs].reshape(depth, wtile)
        gwi[k, cs, :] += contract_rows(normed, dq[par].reshape(depth, hidden))
        active = act[par, :, :, cs].reshape(depth, wtile)
        gwo[k, cs, :] += contract_rows(active, gath[op_slot(i)].reshape(depth, width))

    def item_at(s):
        near = jnp.minimum(r, last - r)
        base = jnp.where(near == 0, last - s, jnp.where(s < 2, last - s, s - 2))
        return jnp.where(r < 2, base, last - base)

    def cot_load():
        return pltpu.make_async_copy(cot_hbm, cot_ref, cot_sem)

    EARLY, LATE = (0, 2, 4, 5, 6), (1, 3)

    def tell(late, q):
        src, dst = ((mine, peers), (mine_late, peers_late))[late]
        return pltpu.make_async_remote_copy(
            src_ref=src,
            dst_ref=dst.at[q - 1],
            send_sem=peer_send.at[late, q - 1],
            recv_sem=peer_recv.at[late, q - 1],
            device_id={"rep": lax.rem(r + q, n)},
            device_id_type=MESH,
        )

    def tell_early():
        for a, row in enumerate(EARLY):
            mine[a : a + 1, :width] = jnp.sum(accs[row], 0, keepdims=True)
        mine[5:6, :hidden] = jnp.sum(bacc[1], 0, keepdims=True)
        mine[6:8, :] = jnp.zeros((2, mine.shape[1]), jnp.float32)
        if inside:
            mine[6:7, :128] = top[...]
        for q in range(1, n):
            tell(0, q).start()

    def tell_late():
        at = 0
        for values in (accs[LATE[0]], accs[LATE[1]], bacc[0]):
            flat = jnp.sum(values, 0, keepdims=True)
            for j in range(flat.shape[1] // 128):
                mine_late[at : at + 1, :] = flat[:, j * 128 : (j + 1) * 128]
                at += 1
        for q in range(1, n):
            tell(1, q).start()

    def unpack(packed, at, size):
        return jnp.concatenate([packed[at + j : at + j + 1] for j in range(size // 128)], 1)

    def load(w):
        src, dst = ((wi_hbm, wi), (wo_hbm, wo))[w]
        return pltpu.make_async_copy(src, dst, load_sem.at[w])

    barrier = pltpu.get_barrier_semaphore()
    for q in range(1, n):
        pl.semaphore_signal(
            barrier, inc=1, device_id={"rep": lax.rem(r + q, n)}, device_id_type=MESH
        )
    load(0).start()
    load(1).start()
    if inside:
        for b in range(1, blocks):
            pl.semaphore_signal(
                barrier, inc=1, device_id={"exp": flip(e, b)}, device_id_type=MESH
            )
        cot_load().start()
        place[...] = slot_rows(routes_ref[...], blocks, cap)
        dispatch(0, 0, 2)
        await_block(0, 0, 0)
    else:
        pl.semaphore_wait(barrier, n - 1)
    prepare(0, 0)

    def step(t, carry):
        k, s = t // n, lax.rem(t, n)
        k_before, s_before = (t - 1) // n, lax.rem(t + n - 1, n)
        i = k - 1
        par = lax.rem(k, 2)
        p = item_at(s)

        def exchange(h):
            for d in range(2):

                @pl.when(t >= 1)
                def _():
                    wait_received(d, k_before, s_before, h)

                @pl.when(t >= 2)
                def _():
                    wait_sent(d, (t - 2) // n, lax.rem(t + n - 2, n), h)

            @pl.when((s == 0) & (k >= 2))
            def _():
                finish_sum(k - 1, h)

            for d in range(2):
                send(d, k, s, h)

        def grads(j):
            old = k - 2

            @pl.when((s < 2) & (old >= CHUNKS) & (op_type(old) >= 2))
            def _():
                weight_grads(old, lax.rem(k + 1, 2), j)

        exchange(0)

        @pl.when(t == n * ops)
        def _():
            tell_early()

        @pl.when(t == 0)
        def _():
            if inside:
                dispatch(0, 2, blocks)
                await_block(0, 0, 2)
            for h in every[1:]:
                prepare(0, h)

        @pl.when(t == 1)
        def _():
            def clear(b, carry):
                zero_rows = pl.ds(pl.multiple_of(b * 64, 64), 64)
                for w in range(2):
                    gwi[w, zero_rows, :] = jnp.zeros((64, hidden), jnp.float32)
                    gwo[w, zero_rows, :] = jnp.zeros((64, width), jnp.float32)
                return carry

            lax.fori_loop(0, width // 64, clear, 0)
            accs[...] = jnp.zeros_like(accs)
            bacc[...] = jnp.zeros_like(bacc)

        if inside:

            @pl.when(t == 2)
            def _():
                cot_load().wait()
                dispatch(1, 0, blocks)

            @pl.when(t == 1)
            def _():
                count_live()

            @pl.when(t == 3)
            def _():
                fullest()
                make_pack()
                for kind, j in ((0, 1), (0, 3), (1, 0), (1, 1), (1, 2), (1, 3)):
                    await_block(0, kind, j)
                pack_middle(0)

            @pl.when(t == n * CHUNKS)
            def _():
                for w in range(2):
                    for b in range(1, blocks):
                        out_copy(w, b, 0).wait_send()
                for b in range(1, blocks):
                    seen_copy(b).wait_send()
                for kind in range(2):
                    for j in range(4):
                        await_block(1, kind, j)
                pack_middle(1)

        @pl.when(t == n)
        def _():
            load(0).wait()
            load(1).wait()

        pieces = [item_first, item_pull, item_second]
        for h in every:
            if h:
                exchange(h)
            mine_now = pieces[h : h + 1] if h < len(parts) - 1 else pieces[h:]
            if len(parts) == 2:
                mine_now = (pieces[:2], pieces[2:])[h]

            @pl.when(k >= 1)
            def _():
                for piece in mine_now:
                    piece(i, par, p)

            if h == 0:
                grads(2 * s)
            elif h == len(parts) - 1:
                grads(2 * s + 1)

        @pl.when((s == 2) & (k >= 2))
        def _():
            finish(k - 2, None)

        @pl.when((s == 3) & (k < ops - 1))
        def _():
            prepare(k + 1, None)

        return carry

    steps = rounds * n
    lax.fori_loop(0, steps, step, 0)

    def last_grads(j, carry):
        weight_grads(ops - 1, (rounds - 1) % 2, j)
        return carry

    lax.fori_loop(0, 4, last_grads, 0)
    for h in every:
        for d in range(2):
            wait_received(d, rounds - 1, n - 1, h)
        finish_sum(rounds - 1, h)
        finish(ops - 1, h)
    for h in every:
        for d in range(2):
            for back in (2, 1):
                wait_sent(d, (steps - back) // n, (steps - back) % n, h)

    tell_late()

    def place_bins(k, q, bins):
        bin_out[k : k + 1, pl.ds(pl.multiple_of(q * hidden, hidden), hidden)] = bins

    for q in range(1, n):
        tell(0, q).wait_recv()
    sums = mine[0:5, :width]
    place_bins(1, r, mine[5:6, :hidden])
    for q in range(1, n):
        sums += peers[q - 1, 0:5, :width]
        place_bins(1, lax.rem(r - q + n, n), peers[q - 1, 5:6, :hidden])
    cent_out[...] = sums[0:1]
    gain_out[1:2, :] = sums[1:2]
    nbias_out[1:2, :] = sums[2:3]
    bout_out[...] = sums[3:5]
    if inside:
        most = mine[6:7, :128]
        for q in range(1, n):
            most = jnp.maximum(most, peers[q - 1, 6:7, :128])
        top_out[...] = most[:, 0:1]
    for q in range(1, n):
        tell(1, q).wait_recv()
    mine_rows = mine_late[...]
    late = mine_rows[: 2 * width // 128]
    place_bins(0, r, unpack(mine_rows, 2 * width // 128, hidden))
    for q in range(1, n):
        theirs = peers_late[q - 1]
        late += theirs[: 2 * width // 128]
        place_bins(0, lax.rem(r - q + n, n), unpack(theirs, 2 * width // 128, hidden))
    gain_out[0:1, :] = unpack(late, 0, width)
    nbias_out[0:1, :] = unpack(late, width // 128, width)
    for q in range(1, n):
        tell(0, q).wait_send()
        tell(1, q).wait_send()
    if inside:
        for w in range(2):
            for kind in range(2):
                for j in range(4):
                    if j:
                        home_copy(w, j, kind).wait_send()
                    else:
                        pl.when(side == kind)(lambda: home_own_copy(w, kind).wait())
                        pl.when(side != kind)(lambda: home_copy(w, 0, kind).wait_send())
            for j in range(4):
                for expert_side in range(2):
                    if j:
                        await_home(w, j, expert_side)
                    else:
                        pl.when(side != expert_side)(
                            functools.partial(await_home, w, j, expert_side)
                        )


def run_layer(own_rows, name, inside, rows_in, gains, nbias, cent, biases, bout, wi, wo):
    n, blocks = lax.axis_size("rep"), lax.axis_size("exp")
    rows, width = rows_in[0].shape
    hidden = wi.shape[2]
    parts = PLANS[own_rows] if inside else (rows // 8, rows // 8)
    chunk = sum(parts)
    CHUNKS = own_rows // chunk
    wide = max(width, hidden)
    late = (2 * width + hidden) // 128
    low, full = jnp.bfloat16, jnp.float32
    vmem = pl.BlockSpec(memory_space=pltpu.VMEM)
    anywhere = pl.BlockSpec(memory_space=pl.ANY)
    row_specs = [vmem] * 2
    extra = []
    if inside:
        row_specs = [vmem, anywhere, vmem, pl.BlockSpec(memory_space=pltpu.SMEM)]
        extra = (
            [pltpu.VMEM((own_rows, width), low)] * 2
            + [pltpu.VMEM((rows, width), low)] * 2
            + [pltpu.VMEM((rows, rows), low)]
            + [pltpu.VMEM((rows, width), low)]
            + [pltpu.VMEM((rows // 2, width), low)] * 2
            + [pltpu.VMEM((own_rows - rows // 2, rows // 2), low)]
            + [pltpu.VMEM((blocks, blocks, 128), full), pltpu.VMEM((1, 128), full)]
            + [pltpu.SemaphoreType.DMA((2, blocks)), pltpu.SemaphoreType.DMA((2, 2, blocks // 2))]
            + [pltpu.SemaphoreType.DMA((2, 2, blocks // 2))] * 2
            + [pltpu.SemaphoreType.DMA((2,)), pltpu.SemaphoreType.DMA]
            + [pltpu.SemaphoreType.DMA((blocks,))] * 2
        )
    flops = 2 * 16 * n * own_rows * width * hidden
    return pl.pallas_call(
        functools.partial(kernel, n, blocks, inside, parts),
        out_shape=(
            pltpu.VMEM((rows, width), low) if inside else jax.ShapeDtypeStruct((rows, width), low),
            pltpu.VMEM((rows, width), low) if inside else jax.ShapeDtypeStruct((rows, width), low),
            pltpu.VMEM((2, width, hidden), full),
            pltpu.VMEM((2, hidden, width), full),
            jax.ShapeDtypeStruct((1, width), full),
            jax.ShapeDtypeStruct((2, width), full),
            jax.ShapeDtypeStruct((2, width), full),
            jax.ShapeDtypeStruct((2, n * hidden), full),
            jax.ShapeDtypeStruct((2, width), full),
        )
        + ((jax.ShapeDtypeStruct((1, 1), full),) if inside else ()),
        in_specs=row_specs + [vmem] * 5 + [anywhere] * 2,
        out_specs=(vmem,) * (10 if inside else 9),
        scratch_shapes=[
            pltpu.VMEM((CHUNKS + POOL, n, chunk, width), low),
            pltpu.VMEM((2, width, hidden), low),
            pltpu.VMEM((2, hidden, width), low),
            pltpu.VMEM((n, chunk, width), full),
            pltpu.VMEM((2, n, chunk, hidden), low),
            pltpu.VMEM((2, n, chunk, hidden), low),
            pltpu.VMEM((chunk, hidden), full),
            pltpu.VMEM((chunk, width), full),
            pltpu.VMEM((own_rows, width), full),
            pltpu.VMEM((own_rows, 128), full),
            pltpu.VMEM((2, 2, n, chunk, width), low),
            pltpu.VMEM((2, 2, chunk, width), low),
            pltpu.VMEM((7, 8, width), full),
            pltpu.VMEM((2, 8, hidden), full),
            pltpu.VMEM((8, wide), full),
            pltpu.VMEM((n - 1, 8, wide), full),
            pltpu.VMEM((late, 128), full),
            pltpu.VMEM((n - 1, late, 128), full),
            pltpu.SemaphoreType.DMA((2, 2, len(parts))),
            pltpu.SemaphoreType.DMA((2, 2, n, len(parts))),
            pltpu.SemaphoreType.DMA((2,)),
            pltpu.SemaphoreType.DMA((2, n - 1)),
            pltpu.SemaphoreType.DMA((2, n - 1)),
        ]
        + extra,
        compiler_params=pltpu.CompilerParams(
            collective_id=name, has_side_effects=True, vmem_limit_bytes=VMEM_BYTES
        ),
        cost_estimate=pl.CostEstimate(
            flops=flops, bytes_accessed=40 * rows * width, transcendentals=8 * rows * hidden * n
        ),
    )(*rows_in, gains, nbias, cent, biases, bout, wi, wo)


def close_kernel(device_count, cap, *refs):
    tok_hbm, cot_hbm, routes_ref, lengths_ref, y, dv, gwi_in, gwo_in = refs[:8]
    small_in, refs = refs[8:13], refs[13:]
    mixed_ref, grad_ref, gwi_out, gwo_out = refs[:4]
    small_out, refs = refs[4:9], refs[9:]
    tok, cot, load_sem, move_sem = refs
    rows = tok.shape[0]
    loads = [
        pltpu.make_async_copy(src, dst, load_sem.at[j])
        for j, (src, dst) in enumerate(((tok_hbm, tok), (cot_hbm, cot)))
    ]
    moves = [
        pltpu.make_async_copy(src.at[k], dst.at[k], move_sem.at[w, k])
        for w, (src, dst) in enumerate(((gwi_in, gwi_out), (gwo_in, gwo_out)))
        for k in range(2)
    ]
    for copy in loads + moves:
        copy.start()
    for src, dst in zip(small_in, small_out):
        dst[...] = src[...]
    place = slot_rows(routes_ref[...], rows // cap, cap)
    device = lax.axis_index("rep") * lax.axis_size("exp") + lax.axis_index("exp")
    live = live_rows(lengths_ref, device, device_count, rows)
    for copy in loads:
        copy.wait()
    mixed_ref[...] = (tok[...].astype(jnp.float32) + live * contract_rows(place, y[...])).astype(
        jnp.bfloat16
    )
    grad_ref[...] = (cot[...].astype(jnp.float32) + contract_rows(place, dv[...])).astype(
        jnp.bfloat16
    )
    for copy in moves:
        copy.wait()


def close(tokens, cotangent, routes, lengths, home_y, home_dv, gwi, gwo, *small):
    n, blocks = lax.axis_size("rep"), lax.axis_size("exp")
    rows, width = tokens.shape
    vmem = pl.BlockSpec(memory_space=pltpu.VMEM)
    anywhere = pl.BlockSpec(memory_space=pl.ANY)
    rows_shape = jax.ShapeDtypeStruct(tokens.shape, tokens.dtype)
    like = lambda a: jax.ShapeDtypeStruct(a.shape, a.dtype)
    home_y, home_dv, gwi, gwo = (
        pltpu.with_memory_space_constraint(a, pltpu.VMEM) for a in (home_y, home_dv, gwi, gwo)
    )
    return pl.pallas_call(
        functools.partial(close_kernel, n * blocks, rows // blocks),
        out_shape=(rows_shape, rows_shape, like(gwi), like(gwo), *map(like, small)),
        in_specs=[anywhere, anywhere, vmem, pl.BlockSpec(memory_space=pltpu.SMEM)]
        + [vmem] * 9,
        out_specs=[vmem, vmem, anywhere, anywhere] + [vmem] * 5,
        scratch_shapes=[pltpu.VMEM((rows, width), tokens.dtype)] * 2
        + [pltpu.SemaphoreType.DMA((2,)), pltpu.SemaphoreType.DMA((2, 2))],
        compiler_params=pltpu.CompilerParams(vmem_limit_bytes=VMEM_BYTES),
    )(tokens, cotangent, routes, lengths, home_y, home_dv, gwi, gwo, *small)


def no_results(shapes):
    def kernel(*refs):
        refs[-1][...] = jnp.zeros_like(refs[-1])

    anywhere = pl.BlockSpec(memory_space=pl.ANY)
    *results, _ = pl.pallas_call(
        kernel,
        out_shape=(*shapes, jax.ShapeDtypeStruct((8, 128), jnp.float32)),
        out_specs=[anywhere] * len(shapes) + [pl.BlockSpec(memory_space=pltpu.VMEM)],
    )()
    return tuple(results)


def shards(
    tokens,
    routes,
    lengths,
    centroids,
    norm_gains,
    norm_biases,
    w_in,
    in_biases,
    w_out,
    out_biases,
    cotangent,
):
    n_exp = lax.axis_size("exp")
    tok_rows = tokens.shape[0]
    cap = tok_rows // n_exp
    params = (
        norm_gains[0],
        norm_biases[0],
        centroids,
        in_biases[0],
        out_biases[0],
        w_in[0],
        w_out[0],
    )
    devices = n_exp * lax.axis_size("rep")
    if n_exp == 8 and tok_rows == max(PLANS) and devices == 4 * lengths.shape[0]:
        less, whole = sorted(PLANS)
        given = (tokens, cotangent, routes.reshape(1, tok_rows), lengths)

        def layer(own_rows, name, given, *params):
            *results, most = run_layer(own_rows, name, True, given, *params)
            return tuple(close(*given, *results)), most.reshape(()) <= own_rows

        seqs, planes = lengths.shape[0], lax.axis_size("rep")
        of_plane = lax.iota(jnp.int32, seqs) // (seqs // planes) == lax.iota(jnp.int32, planes)[:, None]
        plane_live = jnp.sum(jnp.where(of_plane, lengths, 0), 1)
        shapes = jax.eval_shape(functools.partial(layer, less, 0), given, *params)[0]
        results, done = lax.cond(
            jnp.max(plane_live) <= (less - SPARE) * n_exp,
            functools.partial(layer, less, 0),
            lambda *_: (no_results(shapes), jnp.array(False)),
            given,
            *params,
        )
        results = lax.cond(
            done,
            lambda results, *_: results,
            lambda results, *rest: layer(whole, 1, *rest)[0],
            results,
            given,
            *params,
        )
    else:
        device = lax.axis_index(("rep", "exp"))
        slot = tok_rows * n_exp * lax.axis_size("rep") // lengths.shape[0]
        positions = device * tok_rows + lax.iota(jnp.int32, tok_rows)
        seq_ids = positions // slot
        seq_table = lax.iota(jnp.int32, lengths.shape[0])
        seq_len = jnp.sum(
            jnp.where(seq_ids[:, None] == seq_table[None, :], lengths[None, :], 0), 1
        )
        live = (positions % slot < seq_len).astype(jnp.float32)[:, None]
        route = routes[:, 0]
        hits = (route[:, None] == lax.iota(jnp.int32, n_exp)[None, :]).astype(jnp.int32)
        before = jnp.cumsum(hits, 0) - hits
        target = route * cap + jnp.sum(before * hits, 1)
        place = (lax.iota(jnp.int32, tok_rows)[:, None] == target[None, :]).astype(jnp.bfloat16)
        grad_out = (live * cotangent.astype(jnp.float32)).astype(jnp.bfloat16)

        def send(rows):
            ordered = jnp.dot(place, rows, preferred_element_type=jnp.float32).astype(jnp.bfloat16)
            return lax.all_to_all(ordered, "exp", split_axis=0, concat_axis=0, tiled=True)

        def give_back(rows):
            back = lax.all_to_all(rows, "exp", split_axis=0, concat_axis=0, tiled=True)
            return contract_rows(place, back)

        given = (send(tokens), send(grad_out))
        result, grad_local, *rest = run_layer(tok_rows, 0, False, given, *params)
        mixed = (tokens.astype(jnp.float32) + live * give_back(result)).astype(jnp.bfloat16)
        tokens_grad = (cotangent.astype(jnp.float32) + give_back(grad_local)).astype(jnp.bfloat16)
        results = (mixed, tokens_grad, *rest)
    mixed, tokens_grad, gwi, gwo, cent_grad, gain_grad, nbias_grad, bin_grad, bout_grad = results
    return (
        mixed,
        tokens_grad,
        cent_grad,
        gain_grad[None],
        nbias_grad[None],
        gwi[None],
        bin_grad[None],
        gwo[None],
        bout_grad[None],
    )


def solution(mesh):
    placed = (
        P(("rep", "exp"), None),
        P(("rep", "exp"), None),
        P(),
        P("exp", None),
        P("exp", None, None),
        P("exp", None, None),
        P("exp", None, None, "rep"),
        P("exp", None, None),
        P("exp", None, "rep", None),
        P("exp", None, None),
        P(("rep", "exp"), None),
    )
    return jax.shard_map(
        shards,
        mesh=mesh,
        in_specs=placed,
        out_specs=(
            P(("rep", "exp"), None),
            P(("rep", "exp"), None),
            P("exp", None),
            P("exp", None, None),
            P("exp", None, None),
            P("exp", None, None, "rep"),
            P("exp", None, None),
            P("exp", None, "rep", None),
            P("exp", None, None),
        ),
        check_vma=False,
    )
```
